128 devices in a mesh: section: 16 (over z, y_lo, core), tensor: 8 (over y_hi, x).
Axes of the slice: x: 4, y: 4 (y_hi: 2, y_lo: 2; y = y_hi * 2 + y_lo), z: 4, core: 2. Of those that a mesh axis runs over, the one named last changes fastest.
Arguments:
- token_ids: int32 [4096], P('section'), may hold values from 0 to 152063, as said below
- column_order: int32 [8192], replicated, may hold values from 0 to 8191, each once
- residual: bfloat16 [4096, 8192], P('section', 'tensor'), may hold values from -40 to 40
- attn_out: bfloat16 [4096, 8192], P('section', 'tensor'), may hold values from -6 to 6
- out_proj: bfloat16 [8192, 8192], P(None, 'tensor'), may hold values from -0.0625 to 0.0625
- norm_gain: float32 [8192], P('tensor'), may hold values from 0.5 to 1.5
Outputs:
- factored: float32 [8192, 8192], P('section', 'tensor')
The draws below stay inside these ranges and needn't reach their ends.
Inputs may be any that keep to these rules, and one draw needn't show every extreme that they name: `token_ids`: id 0 marks padding. In each block of 256 tokens of one section index the padding fills trailing positions, and each block holds at least one non-padding token.
All inputs are finite; a program needn't handle non-finite values.
Results may differ from the reference program's by a relative error of at most 0.0067.
Values may be sent and summed in bfloat16 or wider, within the bound.
No kernel may reach another device: no remote copies, remote signals or barrier semaphores. Data moves between devices by JAX's collectives and lax.ppermute only.
A program may use at most 128 MiB of HBM per device.

```python
import jax
import jax.numpy as jnp
from jax import lax

D = 8192
TOK_S = 256
TILE = 128
PANEL = 1024
TOKENS = 4096
PROW = 16
PCOL = 8


def draw_token_ids(key, part):
    key = jax.random.fold_in(key, 11)
    key_jitter, key_ids = jax.random.split(key)
    section_of = jnp.arange(TOKENS, dtype=jnp.int32) // TOK_S
    position = jnp.arange(TOKENS, dtype=jnp.int32) % TOK_S
    spread = PROW - 1
    planned = TOK_S * (spread + 2 * jnp.arange(PROW, dtype=jnp.int32)) // (3 * spread)
    jitter = jax.random.randint(key_jitter, (PROW,), 0, TOK_S // 8 + 1)
    length = jnp.maximum(planned - jitter, 1)
    drawn = jax.random.randint(key_ids, (TOKENS,), 1, 152064)
    return jnp.where(position < length[section_of], drawn, 0).astype(jnp.int32)


def draw_residual(key, part):
    key = jax.random.fold_in(key, 23)
    key_cols, key_rows, key_base = jax.random.split(key, 3)
    col_scale = jnp.exp(jax.random.uniform(key_cols, (1, D), jnp.float32, jnp.log(0.3), jnp.log(3.0)))
    row_scale = jnp.exp(jax.random.uniform(key_rows, (TOKENS, 1), jnp.float32, jnp.log(0.5), jnp.log(2.0)))
    values = jax.random.normal(key_base, (TOKENS, D), jnp.float32) * col_scale * row_scale
    return jnp.clip(values, -40.0, 40.0).astype(jnp.bfloat16)


def level_of(rng, extent, pieces, smallest, high):
    def one(dim, shards_of):
        steps = jax.random.uniform(jax.random.fold_in(jax.random.fold_in(rng, 6), dim), (shards_of,), jnp.float32, smallest / len(pieces), high / len(pieces))
        return jnp.repeat(jnp.exp(steps), extent[dim] // shards_of).reshape((-1,) + (1,) * (len(extent) - dim - 1))

    factor_of = one(*pieces[0])
    for cut in pieces[1:]:
        factor_of = factor_of * one(*cut)
    return factor_of


def scatter_about(stream_key, shape, scale, limit, pieces=(), kind=jnp.bfloat16):
    entries = scale * jax.random.normal(stream_key, shape, jnp.float32)
    if pieces:
        entries = entries * level_of(stream_key, shape, pieces, -0.22, 0.18)
    return jnp.clip(entries, -limit, limit).astype(kind)


def setup_inputs(seed: int = 0) -> dict:
    keys = jax.random.split(jax.random.key(seed), 7)
    return {
        "token_ids": draw_token_ids(jax.random.fold_in(keys[6], 71), 0),
        "column_order": jax.random.permutation(keys[1], D).astype(jnp.int32),
        "residual": draw_residual(jax.random.fold_in(keys[6], 71), 0),
        "attn_out": scatter_about(keys[3], (TOKENS, D), 1.0, 6.0, ((0, 16), (1, 8))),
        "out_proj": scatter_about(keys[4], (D, D), D ** -0.5, 0.0625, ((1, 8),)),
        "norm_gain": jnp.clip(1.0 + 0.1 * jax.random.normal(keys[5], (D,), jnp.float32), 0.5, 1.5),
    }


epsilon = 1e-06

def reference(token_ids, column_order, residual, attn_out, out_proj, norm_gain):
    projected = jnp.dot(attn_out.astype(jnp.float32), out_proj.astype(jnp.float32), precision=lax.Precision.HIGHEST)
    rounded = (residual.astype(jnp.float32) + projected).astype(jnp.bfloat16)
    hidden = lax.optimization_barrier(rounded).astype(jnp.float32)
    squares = lax.optimization_barrier(jnp.sum(hidden * hidden, axis=1))
    kept_rows = (token_ids != 0).astype(jnp.float32)
    token_count = jnp.sum(kept_rows)
    row_scale = lax.rsqrt(squares / D + epsilon) * kept_rows
    normed = (hidden * row_scale[:, None] * norm_gain[None, :]).astype(jnp.bfloat16)
    ordered = jnp.take(normed, column_order, axis=1).astype(jnp.float32)
    hessian = jnp.dot(ordered.T, ordered, precision=lax.Precision.HIGHEST) / token_count
    chol_low = jnp.linalg.cholesky(hessian[:PANEL, :PANEL])
    lower = lax.linalg.triangular_solve(chol_low, hessian[:, :PANEL], left_side=False, lower=True, transpose_a=True)
    trailing = hessian[:, PANEL:] - jnp.dot(lower, lower[PANEL:].T, precision=lax.Precision.HIGHEST)
    row_pos = jnp.arange(D, dtype=jnp.int32)[:, None]
    col_pos = jnp.arange(PANEL, dtype=jnp.int32)[None, :]
    left_part = jnp.where(row_pos >= col_pos, lower, jnp.float32(0.0))
    plain = jnp.concatenate([left_part, trailing], axis=1)
    row_map = jnp.arange(D, dtype=jnp.int32).reshape(D // (TILE * PROW), PROW, TILE).transpose(1, 0, 2).reshape(D)
    col_map = jnp.arange(D, dtype=jnp.int32).reshape(D // (TILE * PCOL), PCOL, TILE).transpose(1, 0, 2).reshape(D)
    return jnp.take(jnp.take(plain, row_map, axis=0), col_map, axis=1)
```

```python
import functools

import jax
import jax.numpy as jnp
from jax import lax
from jax.experimental import pallas as pl
from jax.experimental.pallas import tpu as pltpu
from jax.sharding import PartitionSpec as P

TILE = 128
PANEL = 1024
WIDTH = 8192
TOK = 256
EXT = 16
epsilon = 1e-06
F32 = jnp.float32
BF16 = jnp.bfloat16
KEYS = [(0, 0), (0, 1), (1, 0), (1, 1), (3, 0), (3, 1), (2, 0), (2, 1)]
CHUNK = {(d, f): d * 2 + f for d in range(4) for f in range(2)}
MIB = 1024 * 1024


def params(limit=48):
    return pltpu.CompilerParams(vmem_limit_bytes=limit * MIB)


def shift_t(value, dx, dy):
    pairs = [(t, ((t // 4) ^ dy) * 4 + (t % 4 + dx) % 4) for t in range(8)]
    return lax.ppermute(value, "tensor", pairs)


def shift_s(value, dz, dy, dc=0):
    pairs = [(s, ((s // 4 + dz) % 4) * 4 + ((s % 4) ^ (2 * dy + dc))) for s in range(16)]
    return lax.ppermute(value, "section", pairs)


def gather8(x, shift, half):
    b = shift(x, 0, 1)
    ra, la = shift(x, 1, 0), shift(x, 3, 0)
    rb, lb = shift(b, 1, 0), shift(b, 3, 0)
    fa = [shift(ra[:half], 1, 0), shift(la[half:], 3, 0)]
    fb = [shift(rb[:half], 1, 0), shift(lb[half:], 3, 0)]
    return [[x], [b], [ra], [rb], [la], [lb], fa, fb]


def flatten(shards):
    arrays, meta = [], []
    for pieces in shards:
        off, entry = 0, []
        for piece in pieces:
            entry.append((len(arrays), off, piece.shape[0]))
            arrays.append(piece)
            off += piece.shape[0]
        meta.append(entry)
    return arrays, meta


def nt(a, b):
    return lax.dot_general(a, b, (((1,), (1,)), ((), ())), preferred_element_type=F32)


def nn(a, b):
    return lax.dot_general(a, b, (((1,), (0,)), ((), ())), preferred_element_type=F32)


def split(a):
    hi = a.astype(BF16)
    return hi, (a - hi.astype(F32)).astype(BF16)


def dot3(op, a, b):
    return op(a[0], b[0]) + (op(a[0], b[1]) + op(a[1], b[0]))


def project(shards, out_proj, origins, acc=None, residual=None):
    arrays, meta = flatten(shards)
    n = len(shards)
    final = residual is not None
    cols = out_proj.shape[1]

    def body(*refs):
        _, w_ref, *rest = refs
        pieces, rest = rest[: len(arrays)], rest[len(arrays) :]
        if acc is not None:
            acc_ref, *rest = rest
        if final:
            res_ref, *rest = rest
        out_ref, acc_s = rest
        i = pl.program_id(0)

        @pl.when(i == 0)
        def _():
            acc_s[...] = acc_ref[...] if acc is not None else jnp.zeros_like(acc_s)

        for r in range(n):

            @pl.when(i == r)
            def _(r=r):
                for j, off, size in meta[r]:
                    size = min(size, TOK - off)
                    acc_s[off : off + size, :] += nn(pieces[j][:size, :], w_ref[...])

        @pl.when(i == n - 1)
        def _():
            if final:
                h = (res_ref[...].astype(F32) + acc_s[...]).astype(BF16).astype(F32)
                out_ref[...] = h.T.astype(BF16)
            else:
                out_ref[...] = acc_s[...]

    whole = lambda shape: pl.BlockSpec(shape, lambda i, o: (0,) * len(shape))
    operands = [out_proj, *arrays]
    specs = [pl.BlockSpec((1024, cols), lambda i, o: (o[i], 0))] + [whole(a.shape) for a in arrays]
    if acc is not None:
        operands.append(acc)
        specs.append(whole(acc.shape))
    if final:
        operands.append(residual)
        specs.append(whole(residual.shape))
    shape = (cols, TOK) if final else (TOK, cols)
    return pl.pallas_call(
        body,
        out_shape=jax.ShapeDtypeStruct(shape, BF16 if final else F32),
        grid_spec=pltpu.PrefetchScalarGridSpec(
            num_scalar_prefetch=1,
            grid=(n,),
            in_specs=specs,
            out_specs=whole(shape),
            scratch_shapes=[pltpu.VMEM((TOK, cols), F32)],
        ),
        compiler_params=params(),
        cost_estimate=pl.CostEstimate(flops=2 * TOK * 1024 * cols * n, bytes_accessed=n * 2 * MIB, transcendentals=0),
        name="project",
    )(origins, *operands)


def select(shards, gains, origins, index, kept):
    arrays, meta = flatten(shards)
    n_cols, n_rows = 1024, 512

    def body(*refs):
        origin, index_ref, kept_ref, *rest = refs
        pieces, rest = rest[: len(arrays)], rest[len(arrays) :]
        gain_refs, rest = rest[:8], rest[8:]
        cols_ref, rows0_ref, rows1_ref, pan_ref, nrm = rest
        step = 128

        def squares(ref, size, total):
            def add(c, total):
                v = ref[pl.ds(pl.multiple_of(c * step, step), step), :].astype(F32)
                return total + jnp.sum((v * v).reshape(step // 8, 8, TOK), axis=0)

            return lax.fori_loop(0, size // step, add, total)

        total = jnp.zeros((8, TOK), F32)
        for r in range(8):
            for j, off, size in meta[r]:
                total = squares(pieces[j], size, total)
        scale = lax.rsqrt(jnp.sum(total, axis=0, keepdims=True) / WIDTH + epsilon) * kept_ref[...]
        for r in range(8):
            g = jnp.sum(gain_refs[r][...].astype(F32), axis=0, keepdims=True)
            gain = jnp.broadcast_to(g, (8, 1024)).T[:, :1]
            for j, off, size in meta[r]:
                for c in range(size // step):
                    h = pieces[j][c * step : (c + 1) * step, :].astype(F32)
                    at = off + c * step
                    nrm[r * 1024 + at : r * 1024 + at + step, :] = (h * scale * gain[at : at + step, :]).astype(BF16)

        def pick(start, size):
            idx = index_ref[pl.ds(start, size), :]
            lane = lax.broadcasted_iota(jnp.int32, (size, 1024), 1)
            acc = jnp.zeros((size, TOK), F32)
            for r in range(8):
                hot = jnp.where(idx - origin[r] * 1024 == lane, 1.0, 0.0).astype(BF16)
                acc += nn(hot, nrm[r * 1024 : (r + 1) * 1024, :])
            return acc.astype(BF16)

        pan_ref[:TILE, :] = pick(0, TILE)
        first = lax.broadcasted_iota(jnp.int32, (EXT, TOK), 0) == 0
        pan_ref[TILE:, :] = jnp.where(first, kept_ref[...], 0.0).astype(BF16)

        def fill(ref, base):
            def one(c, _):
                at = pl.multiple_of(c * 256, 256)
                ref[pl.ds(at, 256), :] = pick(pl.multiple_of(base + c * 256, 128), 256)
                return 0

            lax.fori_loop(0, ref.shape[0] // 256, one, 0)

        fill(rows1_ref, TILE)
        fill(rows0_ref, TILE + n_rows)
        fill(cols_ref, TILE + 2 * n_rows)

    vm = pl.BlockSpec(memory_space=pltpu.VMEM)
    gain_arrays = [g for g, _ in gains]
    gain_specs = [pl.BlockSpec((EXT, 1024), functools.partial(lambda b, i: (b, 0), b)) for _, b in gains]
    outs = [(n_cols, TOK), (n_rows, TOK), (n_rows, TOK), (TILE + EXT, TOK)]
    return pl.pallas_call(
        body,
        grid=(1,),
        out_shape=[jax.ShapeDtypeStruct(s, BF16) for s in outs],
        in_specs=[pl.BlockSpec(memory_space=pltpu.SMEM), vm, vm] + [vm] * len(arrays) + gain_specs,
        out_specs=[vm] * 4,
        scratch_shapes=[pltpu.VMEM((WIDTH, TOK), BF16)],
        compiler_params=params(),
        cost_estimate=pl.CostEstimate(flops=2 * 2176 * WIDTH * TOK, bytes_accessed=8 * MIB, transcendentals=0),
        name="select",
    )(origins, index, kept, *arrays, *gain_arrays)


def place(pieces, meta, slot, scratch):
    for r in range(8):
        row = pl.multiple_of(slot[r] * TILE, TILE)
        for j, off, size in meta[r]:
            for c in range(size):
                scratch[pl.ds(row, TILE), (off + c) * TOK : (off + c + 1) * TOK] = pieces[j][c]


def panel_gram(shards, slots):
    arrays, meta = flatten(shards)

    def body(slot, *refs):
        pieces, (pan_ref, gram_ref) = refs[: len(arrays)], refs[len(arrays) :]
        place(pieces, meta, slot, pan_ref)

        def one(c, _):
            rows = pl.ds(pl.multiple_of(c * 256, 256), 256)
            gram_ref[rows, :] = nt(pan_ref[rows, :], pan_ref[...])
            return 0

        lax.fori_loop(0, 4, one, 0)

    vm = pl.BlockSpec(memory_space=pltpu.VMEM)
    return pl.pallas_call(
        body,
        out_shape=[jax.ShapeDtypeStruct((PANEL, 2048), BF16), jax.ShapeDtypeStruct((PANEL, PANEL), F32)],
        in_specs=[pl.BlockSpec(memory_space=pltpu.SMEM)] + [vm] * len(arrays),
        out_specs=[vm] * 2,
        compiler_params=params(),
        cost_estimate=pl.CostEstimate(flops=2 * 1024 * 1024 * 2048, bytes_accessed=12 * MIB, transcendentals=0),
        name="panel_gram",
    )(slots, *arrays)


def block_gram(row_shards, col_shards, pan, slots):
    row_arrays, row_meta = flatten(row_shards)
    col_arrays, col_meta = flatten(col_shards)

    def body(slot, pan_ref, *refs):
        rp, refs = refs[: len(row_arrays)], refs[len(row_arrays) :]
        cp, refs = refs[: len(col_arrays)], refs[len(col_arrays) :]
        hk_ref, hs_ref, pk_ref, ps_ref, pc_ref, rows, cols = refs
        place(rp, row_meta, slot, rows)
        for key, entry in zip(KEYS, col_meta):
            lane = CHUNK[key] * TOK
            for j, off, size in entry:
                cols[off : off + size, lane : lane + TOK] = cp[j][...]

        def one(c, _):
            at = pl.ds(pl.multiple_of(c * 256, 256), 256)
            keep = rows[at, :]
            send = rows[pl.ds(pl.multiple_of(512 + c * 256, 256), 256), :]
            pk_ref[at, :] = nt(keep, pan_ref[...])
            ps_ref[at, :] = nt(send, pan_ref[...])
            hk_ref[at, :] = nt(keep, cols[...])
            hs_ref[at, :] = nt(send, cols[...])
            return 0

        lax.fori_loop(0, 2, one, 0)

        def two(c, _):
            at = pl.ds(pl.multiple_of(c * 256, 256), 256)
            pc_ref[at, :] = nt(cols[at, :], pan_ref[...])
            return 0

        lax.fori_loop(0, 4, two, 0)

    vm = pl.BlockSpec(memory_space=pltpu.VMEM)
    outs = [(512, 1024)] * 4 + [(1024, PANEL)]
    return pl.pallas_call(
        body,
        out_shape=[jax.ShapeDtypeStruct(s, F32) for s in outs],
        in_specs=[pl.BlockSpec(memory_space=pltpu.SMEM), vm] + [vm] * (len(row_arrays) + len(col_arrays)),
        out_specs=[vm] * 5,
        scratch_shapes=[pltpu.VMEM((1024, 2048), BF16)] * 2,
        compiler_params=params(),
        cost_estimate=pl.CostEstimate(flops=6 * 1024 * 1024 * 2048, bytes_accessed=24 * MIB, transcendentals=0),
        name="block_gram",
    )(slots, pan, *row_arrays, *col_arrays)


def factor_tile(a, groups=TILE // 8):
    lane = lax.broadcasted_iota(jnp.int32, (8, TILE), 1)
    sub = lax.broadcasted_iota(jnp.int32, (8, TILE), 0)
    A = [a[8 * g : 8 * g + 8, :] for g in range(groups)]
    E = [jnp.where(lane == sub + 8 * g, 1.0, 0.0).astype(F32) for g in range(groups)]
    for j in range(TILE):
        g0, s0 = divmod(j, 8)
        inv = 1.0 / A[g0][s0 : s0 + 1, j : j + 1]
        row = A[g0][s0 : s0 + 1, :] * inv
        erow = E[g0][s0 : s0 + 1, :] * inv
        for g in range(g0, groups):
            col = A[g][:, j : j + 1]
            if g == g0:
                if s0 == 7:
                    continue
                col = jnp.where(sub[:, :1] > s0, col, 0.0)
            A[g] = A[g] - col * row
            E[g] = E[g] - col * erow
    U, V = [], []
    for g in range(groups):
        diag = jnp.sum(jnp.where(lane == sub + 8 * g, A[g], 0.0), axis=1, keepdims=True)
        rs = lax.rsqrt(diag)
        U.append(jnp.where(lane >= sub + 8 * g, A[g] * rs, 0.0))
        V.append(E[g] * rs)
    return jnp.concatenate(U, axis=0), jnp.concatenate(V, axis=0)


def cholesky(gram, other, count):
    tiles = PANEL // TILE

    def body(count_ref, g_ref, o_ref, u_ref, v_ref, ph, plo, lh, ll):
        inv = 1.0 / count_ref[0]

        def load(c, _):
            rows = pl.ds(pl.multiple_of(c * 64, 64), 64)
            u_ref[rows, :] = (g_ref[rows, :] + o_ref[rows, :]) * inv
            return 0

        lax.fori_loop(0, PANEL // 64, load, 0)

        def step(k, _):
            at = pl.ds(pl.multiple_of(k * TILE, TILE), TILE)
            U, V = factor_tile(u_ref[at, at])
            v_ref[at, :] = V
            vs = split(V)
            panel = dot3(nn, vs, split(u_ref[at, :]))
            ph[...], plo[...] = split(panel)
            left = dot3(nt, split(u_ref[:, at]), vs)
            lh[...], ll[...] = split(left)
            u_ref[at, :] = panel
            u_ref[at, at] = U

            def update(j, _):
                rows = pl.ds(pl.multiple_of(j * TILE, TILE), TILE)
                u_ref[rows, :] -= dot3(nn, (lh[rows, :], ll[rows, :]), (ph[...], plo[...]))
                return 0

            lax.fori_loop(k + 1, tiles, update, 0)
            return 0

        lax.fori_loop(0, tiles, step, 0)

    vm = pl.BlockSpec(memory_space=pltpu.VMEM)
    return pl.pallas_call(
        body,
        out_shape=[jax.ShapeDtypeStruct((PANEL, PANEL), F32), jax.ShapeDtypeStruct((PANEL, TILE), F32)],
        in_specs=[pl.BlockSpec(memory_space=pltpu.SMEM), vm, vm],
        out_specs=[vm, vm],
        scratch_shapes=[pltpu.VMEM((TILE, PANEL), BF16)] * 2 + [pltpu.VMEM((PANEL, TILE), BF16)] * 2,
        compiler_params=params(),
        cost_estimate=pl.CostEstimate(flops=80_000_000_000, bytes_accessed=12 * MIB, transcendentals=0),
        name="cholesky",
    )(count, gram, other)


def finish(scalars, count, hk, hr, pk, pr, pc, pcr, u, v):
    tiles = PANEL // TILE

    def body(sc, count_ref, hk_ref, hr_ref, pk_ref, pr_ref, pc_ref, pcr_ref, u_ref, v_ref, out_ref, uh, ul, vh, vl, xh, xl, xr):
        inv = 1.0 / count_ref[0]

        def cut(c, _):
            rows = pl.ds(pl.multiple_of(c * 64, 64), 64)
            uh[rows, :], ul[rows, :] = split(u_ref[rows, :])
            vh[rows, :], vl[rows, :] = split(v_ref[rows, :])
            return 0

        lax.fori_loop(0, PANEL // 64, cut, 0)

        def solve(b):
            parts = []
            for k in range(tiles):
                rows = slice(k * TILE, (k + 1) * TILE)
                x = dot3(nt, split(b[:, :TILE]), (vh[rows, :], vl[rows, :]))
                parts.append(x)
                if k + 1 < tiles:
                    b = b[:, TILE:] - dot3(nn, split(x), (uh[rows, (k + 1) * TILE :], ul[rows, (k + 1) * TILE :]))
            return jnp.concatenate(parts, axis=1)

        def from_rows(c, _):
            rows = pl.ds(pl.multiple_of(c * 256, 256), 256)
            x = solve((pk_ref[rows, :] + pr_ref[rows, :]) * inv)
            xr[rows, :] = x
            xh[rows, :], xl[rows, :] = split(x)
            return 0

        lax.fori_loop(0, 2, from_rows, 0)

        def from_cols(c, _):
            rows = pl.ds(pl.multiple_of(c * 256, 256), 256)
            x = solve((pc_ref[rows, :] + pcr_ref[rows, :]) * inv)
            to = pl.ds(pl.multiple_of(512 + c * 256, 256), 256)
            xh[to, :], xl[to, :] = split(x)
            return 0

        lax.fori_loop(0, 4, from_cols, 0)

        def trail(c, _):
            rows = pl.ds(pl.multiple_of(c * 128, 128), 128)
            cols = slice(512 + TILE, 512 + 1024)
            up = dot3(nt, (xh[rows, :], xl[rows, :]), (xh[cols, :], xl[cols, :]))
            out_ref[rows, TILE:] = (hk_ref[rows, TILE:] + hr_ref[rows, TILE:]) * inv - up
            left = xr[rows, pl.ds(pl.multiple_of(sc[1] * TILE, TILE), TILE)]
            row = (c * 16 + sc[0]) * TILE + lax.broadcasted_iota(jnp.int32, (TILE, TILE), 0)
            col = sc[1] * TILE + lax.broadcasted_iota(jnp.int32, (TILE, TILE), 1)
            out_ref[rows, :TILE] = jnp.where(row >= col, left, 0.0)
            return 0

        lax.fori_loop(0, 4, trail, 0)

    vm = pl.BlockSpec(memory_space=pltpu.VMEM)
    sm = pl.BlockSpec(memory_space=pltpu.SMEM)
    return pl.pallas_call(
        body,
        out_shape=jax.ShapeDtypeStruct((512, 1024), F32),
        in_specs=[sm, sm] + [vm] * 8,
        out_specs=vm,
        scratch_shapes=[pltpu.VMEM((PANEL, PANEL), BF16)] * 2
        + [pltpu.VMEM((PANEL, TILE), BF16)] * 2
        + [pltpu.VMEM((1536, PANEL), BF16)] * 2
        + [pltpu.VMEM((512, PANEL), F32)],
        compiler_params=params(56),
        cost_estimate=pl.CostEstimate(flops=16_000_000_000, bytes_accessed=28 * MIB, transcendentals=0),
        name="finish",
    )(scalars, count, hk, hr, pk, pr, pc, pcr, u, v)


def shards_of(token_ids, column_order, residual, attn_out, out_proj, norm_gain):
    s = lax.axis_index("section").astype(jnp.int32)
    t = lax.axis_index("tensor").astype(jnp.int32)
    y, x = t // 4, t % 4
    z, yl, core = s // 4, (s // 2) % 2, s % 2

    def origin(dx, dy):
        return (y ^ dy) * 4 + (x - dx) % 4

    origins = jnp.stack([origin(*k) for k in KEYS])
    slots = jnp.stack([((o // 4) ^ core) * 4 + o % 4 for o in [origin(*k) for k in KEYS]])

    g_hi = lax.reduce_precision(norm_gain, 8, 7)
    g_mid = lax.reduce_precision(norm_gain - g_hi, 8, 7)
    g_lo = norm_gain - g_hi - g_mid
    parts = jnp.stack([g_hi, g_mid, g_lo]).astype(BF16)
    ext = jnp.concatenate([parts, jnp.zeros((EXT - 3, 1024), BF16)], axis=0)
    own = jnp.concatenate([attn_out, ext], axis=0)
    a = gather8(own, shift_t, 144)

    acc = project(a[:2], out_proj, origins[:2])
    acc = project(a[2:6], out_proj, origins[2:6], acc)
    hidden = project(a[6:], out_proj, origins[6:], acc, residual)

    gains = []
    for pieces in a:
        last = pieces[-1]
        gains.append((last, last.shape[0] // EXT - 1))

    tiles = [t]
    for dy in (1, 0):
        for dz in range(4):
            group = ((z + dz) % 4) * 2 + (yl ^ dy)
            tiles.append(16 * x + 2 * group + y)
    tiles += [j * 8 + t for j in range(8)]
    index = jnp.take(column_order.reshape(64, TILE), jnp.stack(tiles), axis=0).reshape(-1, 1)
    kept = (token_ids != 0).astype(F32).reshape(1, TOK)

    h = gather8(hidden, shift_t, 512)
    cols, rows0, rows1, pan = select(h, gains, origins, index, kept)

    pan2 = jnp.stack([pan, shift_s(pan, 0, 1)])
    pan8 = jnp.concatenate([pan2] + [shift_s(pan2, dz, 0) for dz in (1, 2, 3)], axis=0)
    kept_here = jnp.sum(pan8[:, TILE : TILE + 1, :].astype(F32))
    count = (kept_here + shift_s(kept_here.reshape(1, 1), 0, 0, 1)[0, 0]).reshape(1)
    pan_shards = gather8(pan8[:, :TILE, :], shift_t, 4)

    theirs = shift_s(rows1, 0, 1).reshape(4, TILE, TOK)
    mine = rows0.reshape(4, TILE, TOK)
    both = jnp.stack([mine, theirs], axis=1)
    rows8 = jnp.concatenate([both[0]] + [shift_s(both[dz], dz, 0) for dz in (1, 2, 3)], axis=0)
    row_shards = gather8(rows8, shift_t, 4)
    col_shards = gather8(cols, shift_s, 512)

    pan_all, gram = panel_gram(pan_shards, origins)
    gram_other = shift_s(gram, 0, 0, 1)
    hk, hs, pk, ps, pc = block_gram(row_shards, col_shards, pan_all, slots)
    u, v = cholesky(gram, gram_other, count)
    hr, pr, pcr = [shift_s(w, 0, 0, 1) for w in (hs, ps, pc)]
    return finish(jnp.stack([s, t]), count, hk, hr, pk, pr, pc, pcr, u, v)


def solution(mesh):
    placed = (
        P("section"),
        P(),
        P("section", "tensor"),
        P("section", "tensor"),
        P(None, "tensor"),
        P("tensor"),
    )
    return jax.shard_map(
        shards_of, mesh=mesh, in_specs=placed, out_specs=P("section", "tensor"), check_vma=False
    )
```

```python
import functools

import jax
import jax.numpy as jnp
from jax import lax
from jax.experimental import pallas as pl
from jax.experimental.pallas import tpu as pltpu
from jax.sharding import PartitionSpec as P

TILE = 128
PANEL = 1024
WIDTH = 8192
TOK = 256
EXT = 16
epsilon = 1e-06
F32 = jnp.float32
BF16 = jnp.bfloat16
KEYS = [(0, 0), (0, 1), (1, 0), (1, 1), (3, 0), (3, 1), (2, 0), (2, 1)]
CHUNK = {(d, f): d * 2 + f for d in range(4) for f in range(2)}
MIB = 1024 * 1024


def params(limit=48):
    return pltpu.CompilerParams(vmem_limit_bytes=limit * MIB)


def shift_t(value, dx, dy):
    pairs = [(t, ((t // 4) ^ dy) * 4 + (t % 4 + dx) % 4) for t in range(8)]
    return lax.ppermute(value, "tensor", pairs)


def shift_s(value, dz, dy, dc=0):
    pairs = [(s, ((s // 4 + dz) % 4) * 4 + ((s % 4) ^ (2 * dy + dc))) for s in range(16)]
    return lax.ppermute(value, "section", pairs)


def tie(*values):
    return lax.optimization_barrier(values)


def first(x, shift):
    return shift(x, 0, 1), shift(x, 1, 0), shift(x, 3, 0)


def second(b, ra, la, shift, half):
    return shift(b, 1, 0), shift(b, 3, 0), shift(ra[:half], 1, 0), shift(la[half:], 3, 0)


def third(rb, lb, shift, half):
    return shift(rb[:half], 1, 0), shift(lb[half:], 3, 0)


def listed(x, one, two, three):
    return [[x], [one[0]], [one[1]], [two[0]], [one[2]], [two[1]], [two[2], two[3]], list(three)]


def flatten(shards):
    arrays, meta = [], []
    for pieces in shards:
        off, entry = 0, []
        for piece in pieces:
            entry.append((len(arrays), off, piece.shape[0]))
            arrays.append(piece)
            off += piece.shape[0]
        meta.append(entry)
    return arrays, meta


def nt(a, b):
    return lax.dot_general(a, b, (((1,), (1,)), ((), ())), preferred_element_type=F32)


def nn(a, b):
    return lax.dot_general(a, b, (((1,), (0,)), ((), ())), preferred_element_type=F32)


def split(a):
    hi = a.astype(BF16)
    return hi, (a - hi.astype(F32)).astype(BF16)


def dot3(op, a, b):
    left = jnp.concatenate([a[0], a[0], a[1]], axis=1)
    right = jnp.concatenate([b[0], b[1], b[0]], axis=0 if op is nn else 1)
    return op(left, right)


def project(shards, out_proj, origins, acc=None, residual=None):
    arrays, meta = flatten(shards)
    n = len(shards)
    final = residual is not None
    cols = out_proj.shape[1]

    def body(*refs):
        _, w_ref, *rest = refs
        pieces, rest = rest[: len(arrays)], rest[len(arrays) :]
        if acc is not None:
            acc_ref, *rest = rest
        if final:
            res_ref, *rest = rest
        out_ref, acc_s = rest
        i = pl.program_id(0)

        @pl.when(i == 0)
        def _():
            acc_s[...] = acc_ref[...] if acc is not None else jnp.zeros_like(acc_s)

        for r in range(n):

            @pl.when(i == r)
            def _(r=r):
                for j, off, size in meta[r]:
                    size = min(size, TOK - off)
                    acc_s[off : off + size, :] += nn(pieces[j][:size, :], w_ref[...])

        @pl.when(i == n - 1)
        def _():
            if final:
                h = (res_ref[...].astype(F32) + acc_s[...]).astype(BF16).astype(F32)
                out_ref[...] = h.T.astype(BF16)
            else:
                out_ref[...] = acc_s[...]

    whole = lambda shape: pl.BlockSpec(shape, lambda i, o: (0,) * len(shape))
    operands = [out_proj, *arrays]
    specs = [pl.BlockSpec((1024, cols), lambda i, o: (o[i], 0))] + [whole(a.shape) for a in arrays]
    if acc is not None:
        operands.append(acc)
        specs.append(whole(acc.shape))
    if final:
        operands.append(residual)
        specs.append(whole(residual.shape))
    shape = (cols, TOK) if final else (TOK, cols)
    return pl.pallas_call(
        body,
        out_shape=jax.ShapeDtypeStruct(shape, BF16 if final else F32),
        grid_spec=pltpu.PrefetchScalarGridSpec(
            num_scalar_prefetch=1,
            grid=(n,),
            in_specs=specs,
            out_specs=whole(shape),
            scratch_shapes=[pltpu.VMEM((TOK, cols), F32)],
        ),
        compiler_params=params(),
        cost_estimate=pl.CostEstimate(flops=2 * TOK * 1024 * cols * n, bytes_accessed=n * 2 * MIB, transcendentals=0),
        name="project",
    )(origins, *operands)


PICKS = 2176
SPLITS = ((0, TILE), (TILE, 512), (TILE + 512, 512), (TILE + 1024, 1024))


def hot_rows(index_ref, start, size, base):
    lane = lax.broadcasted_iota(jnp.int32, (size, 1024), 1)
    return jnp.where(index_ref[pl.ds(start, size), :] - base == lane, 1.0, 0.0).astype(BF16)


def pick_gains(gains, origins, index_rows):
    def body(origin, index_ref, *refs):
        gain_refs, out_ref = refs[:8], refs[8]
        got = [jnp.zeros((8, TILE), F32) for _ in range(3)]
        for r in range(8):
            whole = jnp.sum(gain_refs[r][...].astype(F32), axis=0, keepdims=True)
            for q in range(8):
                row = jnp.broadcast_to(whole[:, q * TILE : (q + 1) * TILE], (8, TILE))
                for i in range(3):
                    idx = index_ref[8 * i : 8 * i + 8, :]
                    here = jnp.take_along_axis(row, idx % TILE, axis=1)
                    got[i] = jnp.where(idx // TILE == origin[r] * 8 + q, here, got[i])
        for c in range(PICKS // TILE):
            if c % 8 == 0:
                column = got[c // 8].T
            out_ref[c * TILE : (c + 1) * TILE, :] = column[:, c % 8 : c % 8 + 1]

    vm = pl.BlockSpec(memory_space=pltpu.VMEM)
    specs = [pl.BlockSpec((EXT, 1024), functools.partial(lambda b, i: (b, 0), b)) for _, b in gains]
    return pl.pallas_call(
        body,
        grid=(1,),
        out_shape=jax.ShapeDtypeStruct((PICKS, 1), F32),
        in_specs=[pl.BlockSpec(memory_space=pltpu.SMEM), vm] + specs,
        out_specs=vm,
        compiler_params=params(),
        cost_estimate=pl.CostEstimate(flops=2_000_000_000, bytes_accessed=1 * MIB, transcendentals=0),
        name="pick_gains",
    )(origins, index_rows, *[g for g, _ in gains])


def pick(shards, origins, index, carry=None, gain=None, kept=None):
    arrays, meta = flatten(shards)
    n = len(shards)
    final = gain is not None

    def body(*refs):
        origin, index_ref, *rest = refs
        pieces, rest = rest[: len(arrays)], rest[len(arrays) :]
        if carry is not None:
            (acc_ref, sq_ref), rest = rest[:2], rest[2:]
        if final:
            (gain_ref, kept_ref), rest = rest[:2], rest[2:]
        outs, table = rest[:-1], rest[-1]
        step = 128
        total = sq_ref[...] if carry is not None else jnp.zeros((8, TOK), F32)
        for r in range(n):
            for j, off, size in meta[r]:

                def add(c, total, j=j, at=r * 1024 + off):
                    from_rows = pl.ds(pl.multiple_of(c * step, step), step)
                    v = pieces[j][from_rows, :]
                    table[pl.ds(pl.multiple_of(at + c * step, step), step), :] = v
                    v = v.astype(F32)
                    return total + jnp.sum((v * v).reshape(step // 8, 8, TOK), axis=0)

                total = lax.fori_loop(0, size // step, add, total)
        if final:
            scale = lax.rsqrt(jnp.sum(total, axis=0, keepdims=True) / WIDTH + epsilon) * kept_ref[...]
        else:
            outs[1][...] = total

        def value(start, size):
            got = jnp.zeros((size, TOK), F32)
            if carry is not None:
                got = acc_ref[pl.ds(start, size), :].astype(F32)
            for r in range(n):
                got += nn(hot_rows(index_ref, start, size, origin[r] * 1024), table[r * 1024 : (r + 1) * 1024, :])
            if final:
                got = got * scale * gain_ref[pl.ds(start, size), :]
            return got.astype(BF16)

        def fill(ref, base, to, rows, block):
            def one(c, _):
                at = pl.multiple_of(c * block, block)
                ref[pl.ds(to + at, block), :] = value(pl.multiple_of(base + at, TILE), block)
                return 0

            lax.fori_loop(0, rows // block, one, 0)

        places = ((0, 0), (0, TILE + EXT), (1, 0), (2, 0)) if final else tuple((0, base) for base, _ in SPLITS)
        for (base, rows), (o, to) in zip(SPLITS, places):
            fill(outs[o], base, to, rows, min(rows, 256))
        if final:
            row0 = lax.broadcasted_iota(jnp.int32, (EXT, TOK), 0) == 0
            outs[0][TILE : TILE + EXT, :] = jnp.where(row0, kept_ref[...], 0.0).astype(BF16)

    vm = pl.BlockSpec(memory_space=pltpu.VMEM)
    operands = [origins, index, *arrays]
    if carry is not None:
        operands += list(carry)
    if final:
        operands += [gain, kept]
        outs = [jax.ShapeDtypeStruct(s, BF16) for s in ((TILE + EXT + 512, TOK), (512, TOK), (1024, TOK))]
    else:
        outs = [jax.ShapeDtypeStruct((PICKS, TOK), BF16), jax.ShapeDtypeStruct((8, TOK), F32)]
    return pl.pallas_call(
        body,
        out_shape=outs,
        in_specs=[pl.BlockSpec(memory_space=pltpu.SMEM)] + [vm] * (len(operands) - 1),
        out_specs=[vm] * len(outs),
        scratch_shapes=[pltpu.VMEM((1024 * n, TOK), BF16)],
        compiler_params=params(),
        cost_estimate=pl.CostEstimate(flops=2 * PICKS * 1024 * n * TOK, bytes_accessed=4 * MIB, transcendentals=0),
        name="pick",
    )(*operands)


def place(pieces, meta, slot, scratch):
    for r in range(8):
        row = pl.multiple_of(slot[r] * TILE, TILE)
        for j, off, size in meta[r]:
            for c in range(size):
                scratch[pl.ds(row, TILE), (off + c) * TOK : (off + c + 1) * TOK] = pieces[j][c]


def panel_gram(shards, slots):
    arrays, meta = flatten(shards)

    def body(slot, *refs):
        pieces, (pan_ref, gram_ref) = refs[: len(arrays)], refs[len(arrays) :]
        place(pieces, meta, slot, pan_ref)

        def one(c, _):
            rows = pl.ds(pl.multiple_of(c * 256, 256), 256)
            gram_ref[rows, :] = nt(pan_ref[rows, :], pan_ref[...])
            return 0

        lax.fori_loop(0, 4, one, 0)

    vm = pl.BlockSpec(memory_space=pltpu.VMEM)
    return pl.pallas_call(
        body,
        out_shape=[jax.ShapeDtypeStruct((PANEL, 2048), BF16), jax.ShapeDtypeStruct((PANEL, PANEL), F32)],
        in_specs=[pl.BlockSpec(memory_space=pltpu.SMEM)] + [vm] * len(arrays),
        out_specs=[vm] * 2,
        compiler_params=params(),
        cost_estimate=pl.CostEstimate(flops=1_000_000, bytes_accessed=1024, transcendentals=0),
        name="panel_gram",
    )(slots, *arrays)


def block_gram(row_shards, cols_all, pan, slots, chunks):
    row_arrays, row_meta = flatten(row_shards)
    steps = 4

    def body(slot, chunk, pan_ref, col_ref, *refs):
        rp, refs = refs[: len(row_arrays)], refs[len(row_arrays) :]
        hk_ref, hs_ref, pk_ref, ps_ref, pc_ref, rows, cols = refs
        i = pl.program_id(0)

        @pl.when(i == 0)
        def _():
            place(rp, row_meta, slot, rows)
            for c in range(8):
                cols[:, c * TOK : (c + 1) * TOK] = col_ref[chunk[c]]

        at = pl.ds(pl.multiple_of(i * TILE, TILE), TILE)
        to = pl.ds(pl.multiple_of(512 + i * TILE, TILE), TILE)
        both = jnp.concatenate([rows[at, :], rows[to, :]], axis=0)
        p = nt(both, pan_ref[...])
        pk_ref[...], ps_ref[...] = p[:TILE], p[TILE:]
        h = nt(both, cols[...])
        hk_ref[...], hs_ref[...] = h[:TILE], h[TILE:]
        pc_ref[...] = nt(cols[pl.ds(pl.multiple_of(i * 256, 256), 256), :], pan_ref[...])

    vm = pl.BlockSpec(memory_space=pltpu.VMEM)
    outs = [(512, 1024)] * 4 + [(1024, PANEL)]
    return pl.pallas_call(
        body,
        grid=(steps,),
        out_shape=[jax.ShapeDtypeStruct(s, F32) for s in outs],
        in_specs=[pl.BlockSpec(memory_space=pltpu.SMEM)] * 2 + [vm, vm] + [vm] * len(row_arrays),
        out_specs=[pl.BlockSpec((n // steps, 1024), lambda i: (i, 0)) for n, _ in outs],
        scratch_shapes=[pltpu.VMEM((1024, 2048), BF16)] * 2,
        compiler_params=params(),
        cost_estimate=pl.CostEstimate(flops=6 * 1024 * 1024 * 2048, bytes_accessed=24 * MIB, transcendentals=0),
        name="block_gram",
    )(slots, chunks, pan, cols_all, *row_arrays)


def factor_tile(a):
    groups, m = TILE // 8, 8
    lane = lax.broadcasted_iota(jnp.int32, (8, TILE), 1)
    sub = lax.broadcasted_iota(jnp.int32, (8, TILE), 0)
    A = [a[8 * g : 8 * g + 8, :] for g in range(groups)]
    E = [jnp.where(lane == sub + 8 * g, 1.0, 0.0).astype(F32) for g in range(groups)]

    def wide(v):
        return jnp.broadcast_to(v, (8, TILE))

    for g0 in range(groups):
        j = 8 * g0
        piv = {(i, l): wide(A[g0][i : i + 1, j + l : j + l + 1]) for i in range(m) for l in range(i, m)}
        R = [wide(A[g0][i : i + 1, :]) for i in range(m)]
        RE = [wide(E[g0][i : i + 1, :]) for i in range(m)]
        f, inv = {}, []
        for i in range(m):
            inv.append(1.0 / piv[i, i])
            for l in range(i + 1, m):
                f[i, l] = piv[i, l] * inv[i]
            for l in range(i + 1, m):
                for q in range(l, m):
                    piv[l, q] = piv[l, q] - f[i, l] * piv[i, q]
                R[l] = R[l] - f[i, l] * R[i]
                RE[l] = RE[l] - f[i, l] * RE[i]
        W, WE = [None] * m, [None] * m
        for i in reversed(range(m)):
            W[i], WE[i] = R[i] * inv[i], RE[i] * inv[i]
            for l in range(i + 1, m):
                W[i] = W[i] - f[i, l] * W[l]
                WE[i] = WE[i] - f[i, l] * WE[l]
        for g in range(g0 + 1, groups):
            ag, eg = A[g], E[g]
            for l in range(m):
                col = A[g][:, j + l : j + l + 1]
                ag = ag - col * W[l]
                eg = eg - col * WE[l]
            A[g], E[g] = ag, eg
        ag, eg = R[0], RE[0]
        for i in range(1, m):
            ag = jnp.where(sub == i, R[i], ag)
            eg = jnp.where(sub == i, RE[i], eg)
        A[g0], E[g0] = ag, eg
    U, V = [], []
    for g in range(groups):
        diag = jnp.sum(jnp.where(lane == sub + 8 * g, A[g], 0.0), axis=1, keepdims=True)
        rs = lax.rsqrt(diag)
        U.append(jnp.where(lane >= sub + 8 * g, A[g] * rs, 0.0))
        V.append(E[g] * rs)
    return jnp.concatenate(U, axis=0), jnp.concatenate(V, axis=0)


def cholesky(lo, hi, u, v=None, other=None, count=None):
    tiles = PANEL // TILE
    start = other is not None

    def body(*refs):
        if start:
            count_ref, g_ref, o_ref, u_ref, v_ref, ph, plo, lh, ll = refs
            inv = 1.0 / count_ref[0]
        else:
            g_ref, v_in, u_ref, v_ref, ph, plo, lh, ll = refs

        def load(c, _):
            rows = pl.ds(pl.multiple_of(c * 64, 64), 64)
            if start:
                u_ref[rows, :] = (g_ref[rows, :] + o_ref[rows, :]) * inv
            else:
                u_ref[rows, :] = g_ref[rows, :]
                v_ref[rows, :] = v_in[rows, :]
            return 0

        lax.fori_loop(0, PANEL // 64, load, 0)

        def step(k, _):
            at = pl.ds(pl.multiple_of(k * TILE, TILE), TILE)
            U, V = factor_tile(u_ref[at, at])
            v_ref[at, :] = V
            vs = split(V)
            panel = dot3(nn, vs, split(u_ref[at, :]))
            ph[...], plo[...] = split(panel)
            left = dot3(nt, split(u_ref[:, at]), vs)
            lh[...], ll[...] = split(left)
            u_ref[at, :] = panel
            u_ref[at, at] = U

            def update(j, _):
                rows = pl.ds(pl.multiple_of(j * TILE, TILE), TILE)
                u_ref[rows, :] -= dot3(nn, (lh[rows, :], ll[rows, :]), (ph[...], plo[...]))
                return 0

            lax.fori_loop(k + 1, tiles, update, 0)
            return 0

        lax.fori_loop(lo, hi, step, 0)

    vm = pl.BlockSpec(memory_space=pltpu.VMEM)
    sm = pl.BlockSpec(memory_space=pltpu.SMEM)
    return pl.pallas_call(
        body,
        out_shape=[jax.ShapeDtypeStruct((PANEL, PANEL), F32), jax.ShapeDtypeStruct((PANEL, TILE), F32)],
        in_specs=[sm, vm, vm] if start else [vm, vm],
        out_specs=[vm, vm],
        input_output_aliases={1: 0} if start else {0: 0, 1: 1},
        scratch_shapes=[pltpu.VMEM((TILE, PANEL), BF16)] * 2 + [pltpu.VMEM((PANEL, TILE), BF16)] * 2,
        compiler_params=params(),
        cost_estimate=pl.CostEstimate(flops=1_000_000, bytes_accessed=1024, transcendentals=0),
        name="cholesky",
    )(*((count, u, other) if start else (u, v)))


def finish(scalars, count, hk, hr, pk, pr, pc, pcr, u, v):
    two = 2 * TILE
    pairs = PANEL // two

    def body(sc, count_ref, hk_ref, hr_ref, pk_ref, pr_ref, pc_ref, pcr_ref, u_ref, v_ref, out_ref, uh, ul, vh, vl, xh, xl, b):
        inv = 1.0 / count_ref[0]

        def cut(c, _):
            rows = pl.ds(pl.multiple_of(c * 64, 64), 64)
            uh[rows, :], ul[rows, :] = split(u_ref[rows, :])
            return 0

        lax.fori_loop(0, PANEL // 64, cut, 0)

        for k in range(pairs):
            top, low = slice(k * two, k * two + TILE), slice(k * two + TILE, (k + 1) * two)
            v1, v2 = split(v_ref[top, :]), split(v_ref[low, :])
            cross = dot3(nn, split(u_ref[top, low].T), v1)
            cross = -dot3(nn, v2, split(cross))
            vh[top, :TILE], vl[top, :TILE] = v1
            vh[low, TILE:], vl[low, TILE:] = v2
            vh[top, TILE:] = jnp.zeros((TILE, TILE), BF16)
            vl[top, TILE:] = jnp.zeros((TILE, TILE), BF16)
            vh[low, :TILE], vl[low, :TILE] = split(cross)

        def gather_rows(c, _):
            rows = pl.ds(pl.multiple_of(c * 64, 64), 64)
            b[rows, :] = (pk_ref[rows, :] + pr_ref[rows, :]) * inv
            return 0

        def gather_cols(c, _):
            rows = pl.ds(pl.multiple_of(c * 64, 64), 64)
            b[pl.ds(pl.multiple_of(512 + c * 64, 64), 64), :] = (pc_ref[rows, :] + pcr_ref[rows, :]) * inv
            return 0

        lax.fori_loop(0, 8, gather_rows, 0)
        lax.fori_loop(0, 16, gather_cols, 0)

        for k in range(pairs):
            here, after = slice(k * two, (k + 1) * two), slice((k + 1) * two, PANEL)

            def solve(c, _, here=here, after=after, last=k + 1 == pairs):
                rows = pl.ds(pl.multiple_of(c * 512, 512), 512)
                x = dot3(nt, split(b[rows, here]), (vh[here, :], vl[here, :]))
                xs = split(x)
                b[rows, here] = x
                xh[rows, here], xl[rows, here] = xs
                if not last:
                    b[rows, after] -= dot3(nn, xs, (uh[here, after], ul[here, after]))
                return 0

            lax.fori_loop(0, 3, solve, 0)

        def trail(c, _):
            rows = pl.ds(pl.multiple_of(c * TILE, TILE), TILE)
            cols = slice(512 + TILE, 512 + 1024)
            up = dot3(nt, (xh[rows, :], xl[rows, :]), (xh[cols, :], xl[cols, :]))
            out_ref[rows, TILE:] = (hk_ref[rows, TILE:] + hr_ref[rows, TILE:]) * inv - up
            left = b[rows, pl.ds(pl.multiple_of(sc[1] * TILE, TILE), TILE)]
            row = (c * 16 + sc[0]) * TILE + lax.broadcasted_iota(jnp.int32, (TILE, TILE), 0)
            col = sc[1] * TILE + lax.broadcasted_iota(jnp.int32, (TILE, TILE), 1)
            out_ref[rows, :TILE] = jnp.where(row >= col, left, 0.0)
            return 0

        lax.fori_loop(0, 4, trail, 0)

    vm = pl.BlockSpec(memory_space=pltpu.VMEM)
    sm = pl.BlockSpec(memory_space=pltpu.SMEM)
    return pl.pallas_call(
        body,
        out_shape=jax.ShapeDtypeStruct((512, 1024), F32),
        in_specs=[sm, sm] + [vm] * 8,
        out_specs=vm,
        scratch_shapes=[pltpu.VMEM((PANEL, PANEL), BF16)] * 2
        + [pltpu.VMEM((PANEL, two), BF16)] * 2
        + [pltpu.VMEM((1536, PANEL), BF16)] * 2
        + [pltpu.VMEM((1536, PANEL), F32)],
        compiler_params=params(56),
        cost_estimate=pl.CostEstimate(flops=16_000_000_000, bytes_accessed=28 * MIB, transcendentals=0),
        name="finish",
    )(scalars, count, hk, hr, pk, pr, pc, pcr, u, v)


def shards_of(token_ids, column_order, residual, attn_out, out_proj, norm_gain):
    s = lax.axis_index("section").astype(jnp.int32)
    t = lax.axis_index("tensor").astype(jnp.int32)
    y, x = t // 4, t % 4
    z, yl, core = s // 4, (s // 2) % 2, s % 2

    def origin(dx, dy):
        return (y ^ dy) * 4 + (x - dx) % 4

    origins = jnp.stack([origin(*k) for k in KEYS])

    g_hi = lax.reduce_precision(norm_gain, 8, 7)
    g_mid = lax.reduce_precision(norm_gain - g_hi, 8, 7)
    g_lo = norm_gain - g_hi - g_mid
    parts = jnp.stack([g_hi, g_mid, g_lo]).astype(BF16)
    ext = jnp.concatenate([parts, jnp.zeros((EXT - 3, 1024), BF16)], axis=0)
    own = jnp.concatenate([attn_out, ext], axis=0)

    one = first(own, shift_t)
    two = second(*one, shift_t, 144)
    acc = project([[own], [one[0]]], out_proj, origins[:2])
    *two, acc = tie(*two, acc)
    three = third(two[0], two[1], shift_t, 144)
    acc = project([[one[1]], [two[0]], [one[2]], [two[1]]], out_proj, origins[2:6], acc)
    *three, acc = tie(*three, acc)
    a = listed(own, one, two, three)
    hidden = project(a[6:], out_proj, origins[6:], acc, residual)
    gains = [(pieces[-1], pieces[-1].shape[0] // EXT - 1) for pieces in a]

    tiles = [t]
    for dy in (1, 0):
        for dz in range(4):
            group = ((z + dz) % 4) * 2 + (yl ^ dy)
            tiles.append(16 * x + 2 * group + y)
    tiles += [j * 8 + t for j in range(8)]
    index = jnp.take(column_order.reshape(64, TILE), jnp.stack(tiles), axis=0).reshape(-1, 1)
    kept = (token_ids != 0).astype(F32).reshape(1, TOK)

    one = first(hidden, shift_t)
    rows_of = jnp.concatenate([index.reshape(-1, TILE), jnp.zeros((7, TILE), jnp.int32)], axis=0)
    gain = pick_gains(gains, origins, rows_of)
    *one, gain = tie(*one, gain)
    two = second(*one, shift_t, 512)
    carry = pick([[hidden], [one[0]]], origins[:2], index)
    *two, c0, c1 = tie(*two, *carry)
    three = third(two[0], two[1], shift_t, 512)
    carry = pick([[one[1]], [two[0]], [one[2]], [two[1]]], origins[2:6], index, (c0, c1))
    *three, c0, c1 = tie(*three, *carry)
    h = listed(hidden, one, two, three)
    message, rows0, cols = pick(h[6:], origins[6:], index, (c0, c1), gain, kept)

    same_core = [[c + 2 * g for g in range(8)] for c in range(2)]
    cols_all = lax.all_gather(cols, "section", axis=0, axis_index_groups=same_core)
    theirs = shift_s(message, 0, 1)
    head = TILE + EXT

    def part(msg, rows, dz):
        return jnp.concatenate([msg[:head], rows[dz * TILE : (dz + 1) * TILE]], axis=0)

    sent = [jnp.stack([part(message, rows0, dz), part(theirs, theirs[head:], dz)]) for dz in range(4)]
    got = [sent[0]] + [shift_s(sent[dz], dz, 0) for dz in (1, 2, 3)]
    pan8 = jnp.concatenate([g[:, :TILE] for g in got], axis=0)
    rows8 = jnp.concatenate([g[:, head:] for g in got], axis=0)
    kept_here = sum(jnp.sum(g[:, TILE : TILE + 1].astype(F32)) for g in got)
    count = (kept_here + shift_s(kept_here.reshape(1, 1), 0, 0, 1)[0, 0]).reshape(1)

    p1 = first(pan8, shift_t)
    p2 = second(*p1, shift_t, 4)
    p2, rows8 = tie(p2, rows8)
    p3 = third(p2[0], p2[1], shift_t, 4)
    r1 = first(rows8, shift_t)
    pan_all, gram = panel_gram(listed(pan8, p1, p2, p3), origins)

    gram, r1 = tie(gram, r1)
    gram_other = shift_s(gram, 0, 0, 1)
    r2 = second(*r1, shift_t, 4)
    u, v = cholesky(0, 3, gram, other=gram_other, count=count)
    u, r2 = tie(u, r2)
    r3 = third(r2[0], r2[1], shift_t, 4)
    u, v = cholesky(3, 5, u, v)
    u, r3, cols_all = tie(u, r3, cols_all)
    slots = jnp.stack([((o // 4) ^ core) * 4 + o % 4 for o in [origin(*k) for k in KEYS]])
    chunks = jnp.stack([((z - dz) % 4) * 2 + (yl ^ dy) for dz in range(4) for dy in range(2)])
    hk, hs, pk, ps, pc = block_gram(listed(rows8, r1, r2, r3), cols_all, pan_all, slots, chunks)
    u, hs, ps, pc = tie(u, hs, ps, pc)
    hr, pr, pcr = [shift_s(w, 0, 0, 1) for w in (hs, ps, pc)]
    u, v = cholesky(5, 8, u, v)
    return finish(jnp.stack([s, t]), count, hk, hr, pk, pr, pc, pcr, u, v)


def solution(mesh):
    placed = (
        P("section"),
        P(),
        P("section", "tensor"),
        P("section", "tensor"),
        P(None, "tensor"),
        P("tensor"),
    )
    return jax.shard_map(
        shards_of, mesh=mesh, in_specs=placed, out_specs=P("section", "tensor"), check_vma=False
    )
```

```python
import functools

import jax
import jax.numpy as jnp
from jax import lax
from jax.experimental import pallas as pl
from jax.experimental.pallas import tpu as pltpu
from jax.sharding import PartitionSpec as P

TILE = 128
PANEL = 1024
WIDTH = 8192
TOK = 256
EXT = 16
epsilon = 1e-06
F32 = jnp.float32
BF16 = jnp.bfloat16
KEYS = [(0, 0), (0, 1), (1, 0), (1, 1), (3, 0), (3, 1), (2, 0), (2, 1)]
CHUNK = {(d, f): d * 2 + f for d in range(4) for f in range(2)}
MIB = 1024 * 1024


def params(limit=48):
    return pltpu.CompilerParams(vmem_limit_bytes=limit * MIB)


def shift_t(value, dx, dy):
    pairs = [(t, ((t // 4) ^ dy) * 4 + (t % 4 + dx) % 4) for t in range(8)]
    return lax.ppermute(value, "tensor", pairs)


def shift_s(value, dz, dy, dc=0):
    pairs = [(s, ((s // 4 + dz) % 4) * 4 + ((s % 4) ^ (2 * dy + dc))) for s in range(16)]
    return lax.ppermute(value, "section", pairs)


def tie(*values):
    return lax.optimization_barrier(values)


def first(x, shift):
    return shift(x, 0, 1), shift(x, 1, 0), shift(x, 3, 0)


def second(b, ra, la, shift, half):
    return shift(b, 1, 0), shift(b, 3, 0), shift(ra[:half], 1, 0), shift(la[half:], 3, 0)


def third(rb, lb, shift, half):
    return shift(rb[:half], 1, 0), shift(lb[half:], 3, 0)


def listed(x, one, two, three):
    return [[x], [one[0]], [one[1]], [two[0]], [one[2]], [two[1]], [two[2], two[3]], list(three)]


def flatten(shards):
    arrays, meta = [], []
    for pieces in shards:
        off, entry = 0, []
        for piece in pieces:
            entry.append((len(arrays), off, piece.shape[0]))
            arrays.append(piece)
            off += piece.shape[0]
        meta.append(entry)
    return arrays, meta


def nt(a, b):
    return lax.dot_general(a, b, (((1,), (1,)), ((), ())), preferred_element_type=F32)


def nn(a, b):
    return lax.dot_general(a, b, (((1,), (0,)), ((), ())), preferred_element_type=F32)


def split(a):
    hi = a.astype(BF16)
    return hi, (a - hi.astype(F32)).astype(BF16)


def dot3(op, a, b):
    left = jnp.concatenate([a[0], a[0], a[1]], axis=1)
    right = jnp.concatenate([b[0], b[1], b[0]], axis=0 if op is nn else 1)
    return op(left, right)


def project(shards, out_proj, origins, acc=None, residual=None):
    arrays, meta = flatten(shards)
    n = len(shards)
    final = residual is not None
    cols = out_proj.shape[1]

    def body(*refs):
        _, w_ref, *rest = refs
        pieces, rest = rest[: len(arrays)], rest[len(arrays) :]
        if acc is not None:
            acc_ref, *rest = rest
        if final:
            res_ref, *rest = rest
        out_ref, acc_s = rest
        i = pl.program_id(0)

        @pl.when(i == 0)
        def _():
            acc_s[...] = acc_ref[...] if acc is not None else jnp.zeros_like(acc_s)

        for r in range(n):

            @pl.when(i == r)
            def _(r=r):
                for j, off, size in meta[r]:
                    size = min(size, TOK - off)
                    acc_s[off : off + size, :] += nn(pieces[j][:size, :], w_ref[...])

        @pl.when(i == n - 1)
        def _():
            if final:
                h = (res_ref[...].astype(F32) + acc_s[...]).astype(BF16).astype(F32)
                out_ref[...] = h.T.astype(BF16)
            else:
                out_ref[...] = acc_s[...]

    whole = lambda shape: pl.BlockSpec(shape, lambda i, o: (0,) * len(shape))
    operands = [out_proj, *arrays]
    specs = [pl.BlockSpec((1024, cols), lambda i, o: (o[i], 0))] + [whole(a.shape) for a in arrays]
    if acc is not None:
        operands.append(acc)
        specs.append(whole(acc.shape))
    if final:
        operands.append(residual)
        specs.append(whole(residual.shape))
    shape = (cols, TOK) if final else (TOK, cols)
    return pl.pallas_call(
        body,
        out_shape=jax.ShapeDtypeStruct(shape, BF16 if final else F32),
        grid_spec=pltpu.PrefetchScalarGridSpec(
            num_scalar_prefetch=1,
            grid=(n,),
            in_specs=specs,
            out_specs=whole(shape),
            scratch_shapes=[pltpu.VMEM((TOK, cols), F32)],
        ),
        compiler_params=params(),
        cost_estimate=pl.CostEstimate(flops=2 * TOK * 1024 * cols * n, bytes_accessed=n * 2 * MIB, transcendentals=0),
        name="project",
    )(origins, *operands)


PICKS = 2176
SPLITS = ((0, TILE), (TILE, 512), (TILE + 512, 512), (TILE + 1024, 1024))


def hot_rows(index_ref, start, size, base):
    lane = lax.broadcasted_iota(jnp.int32, (size, 1024), 1)
    return jnp.where(index_ref[pl.ds(start, size), :] - base == lane, 1.0, 0.0).astype(BF16)


def pick_gains(gains, origins, index_rows):
    def body(origin, index_ref, *refs):
        gain_refs, out_ref = refs[:8], refs[8]
        got = [jnp.zeros((8, TILE), F32) for _ in range(3)]
        for r in range(8):
            whole = jnp.sum(gain_refs[r][...].astype(F32), axis=0, keepdims=True)
            for q in range(8):
                row = jnp.broadcast_to(whole[:, q * TILE : (q + 1) * TILE], (8, TILE))
                for i in range(3):
                    idx = index_ref[8 * i : 8 * i + 8, :]
                    here = jnp.take_along_axis(row, idx % TILE, axis=1)
                    got[i] = jnp.where(idx // TILE == origin[r] * 8 + q, here, got[i])
        for c in range(PICKS // TILE):
            if c % 8 == 0:
                column = got[c // 8].T
            out_ref[c * TILE : (c + 1) * TILE, :] = column[:, c % 8 : c % 8 + 1]

    vm = pl.BlockSpec(memory_space=pltpu.VMEM)
    specs = [pl.BlockSpec((EXT, 1024), functools.partial(lambda b, i: (b, 0), b)) for _, b in gains]
    return pl.pallas_call(
        body,
        grid=(1,),
        out_shape=jax.ShapeDtypeStruct((PICKS, 1), F32),
        in_specs=[pl.BlockSpec(memory_space=pltpu.SMEM), vm] + specs,
        out_specs=vm,
        compiler_params=params(),
        cost_estimate=pl.CostEstimate(flops=2_000_000_000, bytes_accessed=1 * MIB, transcendentals=0),
        name="pick_gains",
    )(origins, index_rows, *[g for g, _ in gains])


def pick(shards, origins, index, carry=None, gain=None, kept=None):
    arrays, meta = flatten(shards)
    n = len(shards)
    final = gain is not None

    def body(*refs):
        origin, index_ref, *rest = refs
        pieces, rest = rest[: len(arrays)], rest[len(arrays) :]
        if carry is not None:
            (acc_ref, sq_ref), rest = rest[:2], rest[2:]
        if final:
            (gain_ref, kept_ref), rest = rest[:2], rest[2:]
        outs, table = rest[:-1], rest[-1]
        step = 128
        total = sq_ref[...] if carry is not None else jnp.zeros((8, TOK), F32)
        for r in range(n):
            for j, off, size in meta[r]:

                def add(c, total, j=j, at=r * 1024 + off):
                    from_rows = pl.ds(pl.multiple_of(c * step, step), step)
                    v = pieces[j][from_rows, :]
                    table[pl.ds(pl.multiple_of(at + c * step, step), step), :] = v
                    v = v.astype(F32)
                    return total + jnp.sum((v * v).reshape(step // 8, 8, TOK), axis=0)

                total = lax.fori_loop(0, size // step, add, total)
        if final:
            scale = lax.rsqrt(jnp.sum(total, axis=0, keepdims=True) / WIDTH + epsilon) * kept_ref[...]
        else:
            outs[1][...] = total

        def value(start, size):
            got = jnp.zeros((size, TOK), F32)
            if carry is not None:
                got = acc_ref[pl.ds(start, size), :].astype(F32)
            for r in range(n):
                got += nn(hot_rows(index_ref, start, size, origin[r] * 1024), table[r * 1024 : (r + 1) * 1024, :])
            if final:
                got = got * scale * gain_ref[pl.ds(start, size), :]
            return got.astype(BF16)

        def fill(ref, base, to, rows, block):
            def one(c, _):
                at = pl.multiple_of(c * block, block)
                ref[pl.ds(to + at, block), :] = value(pl.multiple_of(base + at, TILE), block)
                return 0

            lax.fori_loop(0, rows // block, one, 0)

        places = ((0, 0), (0, TILE + EXT), (1, 0), (2, 0)) if final else tuple((0, base) for base, _ in SPLITS)
        for (base, rows), (o, to) in zip(SPLITS, places):
            fill(outs[o], base, to, rows, min(rows, 256))
        if final:
            row0 = lax.broadcasted_iota(jnp.int32, (EXT, TOK), 0) == 0
            outs[0][TILE : TILE + EXT, :] = jnp.where(row0, kept_ref[...], 0.0).astype(BF16)

    vm = pl.BlockSpec(memory_space=pltpu.VMEM)
    operands = [origins, index, *arrays]
    if carry is not None:
        operands += list(carry)
    if final:
        operands += [gain, kept]
        outs = [jax.ShapeDtypeStruct(s, BF16) for s in ((TILE + EXT + 512, TOK), (512, TOK), (1024, TOK))]
    else:
        outs = [jax.ShapeDtypeStruct((PICKS, TOK), BF16), jax.ShapeDtypeStruct((8, TOK), F32)]
    return pl.pallas_call(
        body,
        out_shape=outs,
        in_specs=[pl.BlockSpec(memory_space=pltpu.SMEM)] + [vm] * (len(operands) - 1),
        out_specs=[vm] * len(outs),
        scratch_shapes=[pltpu.VMEM((1024 * n, TOK), BF16)],
        compiler_params=params(),
        cost_estimate=pl.CostEstimate(flops=2 * PICKS * 1024 * n * TOK, bytes_accessed=4 * MIB, transcendentals=0),
        name="pick",
    )(*operands)


def place(pieces, meta, slot, scratch):
    for r in range(8):
        row = pl.multiple_of(slot[r] * TILE, TILE)
        for j, off, size in meta[r]:
            for c in range(size):
                scratch[pl.ds(row, TILE), (off + c) * TOK : (off + c + 1) * TOK] = pieces[j][c]


def panel_gram(shards, slots):
    arrays, meta = flatten(shards)

    def body(slot, *refs):
        pieces, (pan_ref, gram_ref) = refs[: len(arrays)], refs[len(arrays) :]
        place(pieces, meta, slot, pan_ref)

        def one(c, _):
            rows = pl.ds(pl.multiple_of(c * 256, 256), 256)
            gram_ref[rows, :] = nt(pan_ref[rows, :], pan_ref[...])
            return 0

        lax.fori_loop(0, 4, one, 0)

    vm = pl.BlockSpec(memory_space=pltpu.VMEM)
    return pl.pallas_call(
        body,
        out_shape=[jax.ShapeDtypeStruct((PANEL, 2048), BF16), jax.ShapeDtypeStruct((PANEL, PANEL), F32)],
        in_specs=[pl.BlockSpec(memory_space=pltpu.SMEM)] + [vm] * len(arrays),
        out_specs=[vm] * 2,
        compiler_params=params(),
        cost_estimate=pl.CostEstimate(flops=1_000_000, bytes_accessed=1024, transcendentals=0),
        name="panel_gram",
    )(slots, *arrays)


def block_gram(row_shards, cols_all, pan, slots, chunks):
    row_arrays, row_meta = flatten(row_shards)
    steps = 4

    def body(slot, chunk, pan_ref, col_ref, *refs):
        rp, refs = refs[: len(row_arrays)], refs[len(row_arrays) :]
        hk_ref, hs_ref, pk_ref, ps_ref, pc_ref, rows, cols = refs
        i = pl.program_id(0)

        @pl.when(i == 0)
        def _():
            place(rp, row_meta, slot, rows)
            for c in range(8):
                cols[:, c * TOK : (c + 1) * TOK] = col_ref[chunk[c]]

        at = pl.ds(pl.multiple_of(i * TILE, TILE), TILE)
        to = pl.ds(pl.multiple_of(512 + i * TILE, TILE), TILE)
        both = jnp.concatenate([rows[at, :], rows[to, :]], axis=0)
        p = nt(both, pan_ref[...])
        pk_ref[...], ps_ref[...] = p[:TILE], p[TILE:]
        h = nt(both, cols[...])
        hk_ref[...], hs_ref[...] = h[:TILE], h[TILE:]
        pc_ref[...] = nt(cols[pl.ds(pl.multiple_of(i * 256, 256), 256), :], pan_ref[...])

    vm = pl.BlockSpec(memory_space=pltpu.VMEM)
    outs = [(512, 1024)] * 4 + [(1024, PANEL)]
    return pl.pallas_call(
        body,
        grid=(steps,),
        out_shape=[jax.ShapeDtypeStruct(s, F32) for s in outs],
        in_specs=[pl.BlockSpec(memory_space=pltpu.SMEM)] * 2 + [vm, vm] + [vm] * len(row_arrays),
        out_specs=[pl.BlockSpec((n // steps, 1024), lambda i: (i, 0)) for n, _ in outs],
        scratch_shapes=[pltpu.VMEM((1024, 2048), BF16)] * 2,
        compiler_params=params(),
        cost_estimate=pl.CostEstimate(flops=6 * 1024 * 1024 * 2048, bytes_accessed=24 * MIB, transcendentals=0),
        name="block_gram",
    )(slots, chunks, pan, cols_all, *row_arrays)


def factor_tile(a):
    groups, m = TILE // 8, 8
    lane = lax.broadcasted_iota(jnp.int32, (8, TILE), 1)
    sub = lax.broadcasted_iota(jnp.int32, (8, TILE), 0)
    A = [a[8 * g : 8 * g + 8, :] for g in range(groups)]
    E = [jnp.where(lane == sub + 8 * g, 1.0, 0.0).astype(F32) for g in range(groups)]

    def wide(v):
        return jnp.broadcast_to(v, (8, TILE))

    for g0 in range(groups):
        j = 8 * g0
        piv = {(i, l): wide(A[g0][i : i + 1, j + l : j + l + 1]) for i in range(m) for l in range(i, m)}
        R = [wide(A[g0][i : i + 1, :]) for i in range(m)]
        RE = [wide(E[g0][i : i + 1, :]) for i in range(m)]
        f, inv = {}, []
        for i in range(m):
            inv.append(1.0 / piv[i, i])
            for l in range(i + 1, m):
                f[i, l] = piv[i, l] * inv[i]
            for l in range(i + 1, m):
                for q in range(l, m):
                    piv[l, q] = piv[l, q] - (piv[i, l] * piv[i, q]) * inv[i]
                R[l] = R[l] - f[i, l] * R[i]
                RE[l] = RE[l] - f[i, l] * RE[i]
        W, WE = [None] * m, [None] * m
        for i in reversed(range(m)):
            W[i], WE[i] = R[i] * inv[i], RE[i] * inv[i]
            for l in range(i + 1, m):
                W[i] = W[i] - f[i, l] * W[l]
                WE[i] = WE[i] - f[i, l] * WE[l]
        for g in range(g0 + 1, groups):
            ag, eg = A[g], E[g]
            for l in reversed(range(m)):
                col = A[g][:, j + l : j + l + 1]
                ag = ag - col * W[l]
                eg = eg - col * WE[l]
            A[g], E[g] = ag, eg
        ag, eg = R[0], RE[0]
        for i in range(1, m):
            ag = jnp.where(sub == i, R[i], ag)
            eg = jnp.where(sub == i, RE[i], eg)
        A[g0], E[g0] = ag, eg
    U, V = [], []
    for g in range(groups):
        diag = jnp.sum(jnp.where(lane == sub + 8 * g, A[g], 0.0), axis=1, keepdims=True)
        rs = lax.rsqrt(diag)
        U.append(jnp.where(lane >= sub + 8 * g, A[g] * rs, 0.0))
        V.append(E[g] * rs)
    return jnp.concatenate(U, axis=0), jnp.concatenate(V, axis=0)


def cholesky(lo, hi, u, v=None, other=None, count=None):
    tiles = PANEL // TILE
    start = other is not None

    def body(*refs):
        if start:
            count_ref, g_ref, o_ref, u_ref, v_ref, ph, plo, lh, ll = refs
            inv = 1.0 / count_ref[0]
        else:
            g_ref, v_in, u_ref, v_ref, ph, plo, lh, ll = refs

        def load(c, _):
            rows = pl.ds(pl.multiple_of(c * 64, 64), 64)
            if start:
                u_ref[rows, :] = (g_ref[rows, :] + o_ref[rows, :]) * inv
            else:
                u_ref[rows, :] = g_ref[rows, :]
                v_ref[rows, :] = v_in[rows, :]
            return 0

        lax.fori_loop(0, PANEL // 64, load, 0)

        def step(k, _):
            at = pl.ds(pl.multiple_of(k * TILE, TILE), TILE)
            U, V = factor_tile(u_ref[at, at])
            v_ref[at, :] = V
            vs = split(V)
            panel = dot3(nn, vs, split(u_ref[at, :]))
            ph[...], plo[...] = split(panel)
            left = dot3(nt, split(u_ref[:, at]), vs)
            lh[...], ll[...] = split(left)
            u_ref[at, :] = panel
            u_ref[at, at] = U

            def update(j, _):
                rows = pl.ds(pl.multiple_of(j * TILE, TILE), TILE)
                u_ref[rows, :] -= dot3(nn, (lh[rows, :], ll[rows, :]), (ph[...], plo[...]))
                return 0

            lax.fori_loop(k + 1, tiles, update, 0)
            return 0

        lax.fori_loop(lo, hi, step, 0)

    vm = pl.BlockSpec(memory_space=pltpu.VMEM)
    sm = pl.BlockSpec(memory_space=pltpu.SMEM)
    return pl.pallas_call(
        body,
        out_shape=[jax.ShapeDtypeStruct((PANEL, PANEL), F32), jax.ShapeDtypeStruct((PANEL, TILE), F32)],
        in_specs=[sm, vm, vm] if start else [vm, vm],
        out_specs=[vm, vm],
        scratch_shapes=[pltpu.VMEM((TILE, PANEL), BF16)] * 2 + [pltpu.VMEM((PANEL, TILE), BF16)] * 2,
        compiler_params=params(20),
        cost_estimate=pl.CostEstimate(flops=1_000_000, bytes_accessed=1024, transcendentals=0),
        name="cholesky",
    )(*((count, u, other) if start else (u, v)))


def finish(scalars, count, hk, hr, pk, pr, pc, pcr, u, v):
    two, half = 2 * TILE, 512
    pairs = PANEL // two

    def body(sc, count_ref, hk_ref, hr_ref, pk_ref, pr_ref, pc_ref, pcr_ref, u_ref, v_ref, out_ref, uh, ul, vh, vl, xh, xl, b):
        i = pl.program_id(0)
        inv = 1.0 / count_ref[0]

        @pl.when(i == 0)
        def _():
            def cut(c, _):
                rows = pl.ds(pl.multiple_of(c * TILE, TILE), TILE)
                uh[rows, :], ul[rows, :] = split(u_ref[rows, :])
                return 0

            lax.fori_loop(0, PANEL // TILE, cut, 0)

            for k in range(pairs):
                top, low = slice(k * two, k * two + TILE), slice(k * two + TILE, (k + 1) * two)
                v1, v2 = split(v_ref[top, :]), split(v_ref[low, :])
                cross = dot3(nn, split(u_ref[top, low].T), v1)
                cross = -dot3(nn, v2, split(cross))
                vh[top, :TILE], vl[top, :TILE] = v1
                vh[low, TILE:], vl[low, TILE:] = v2
                vh[top, TILE:] = jnp.zeros((TILE, TILE), BF16)
                vl[top, TILE:] = jnp.zeros((TILE, TILE), BF16)
                vh[low, :TILE], vl[low, :TILE] = split(cross)

            def load(c, _):
                rows = pl.ds(pl.multiple_of(c * TILE, TILE), TILE)
                b[rows, :] = (pk_ref[rows, :] + pr_ref[rows, :]) * inv
                return 0

            lax.fori_loop(0, half // TILE, load, 0)

        @pl.when(i > 0)
        def _():
            def load(c, _):
                rows = pl.ds(pl.multiple_of(c * TILE, TILE), TILE)
                b[rows, :] = (pc_ref[rows, :] + pcr_ref[rows, :]) * inv
                return 0

            lax.fori_loop(0, half // TILE, load, 0)

        to = pl.ds(pl.multiple_of(jnp.minimum(i, 1) * half, half), half)
        for k in range(pairs):
            here, after = slice(k * two, (k + 1) * two), slice((k + 1) * two, PANEL)
            x = dot3(nt, split(b[:, here]), (vh[here, :], vl[here, :]))
            xs = split(x)
            b[:, here] = x
            xh[to, here], xl[to, here] = xs
            if k + 1 < pairs:
                b[:, after] -= dot3(nn, xs, (uh[here, after], ul[here, after]))

        @pl.when(i == 0)
        def _():
            def left(c, _):
                rows = pl.ds(pl.multiple_of(c * TILE, TILE), TILE)
                own = b[rows, pl.ds(pl.multiple_of(sc[1] * TILE, TILE), TILE)]
                row = (c * 16 + sc[0]) * TILE + lax.broadcasted_iota(jnp.int32, (TILE, TILE), 0)
                col = sc[1] * TILE + lax.broadcasted_iota(jnp.int32, (TILE, TILE), 1)
                out_ref[rows, :TILE] = jnp.where(row >= col, own, 0.0)
                return 0

            lax.fori_loop(0, half // TILE, left, 0)

        def trail(c, first):
            rows = pl.ds(pl.multiple_of(c * two, two), two)
            cols = slice(half + first, 2 * half)
            up = dot3(nt, (xh[rows, :], xl[rows, :]), (xh[cols, :], xl[cols, :]))
            out_ref[rows, first:] = (hk_ref[rows, first:] + hr_ref[rows, first:]) * inv - up

        @pl.when(i == 1)
        def _():
            lax.fori_loop(0, half // two, lambda c, _: (trail(c, TILE), 0)[1], 0)

        @pl.when(i == 2)
        def _():
            lax.fori_loop(0, half // two, lambda c, _: (trail(c, 0), 0)[1], 0)

    sm = pl.BlockSpec(memory_space=pltpu.SMEM)
    later = lambda i: jnp.maximum(i - 1, 0)
    wide = pl.BlockSpec((half, half), lambda i: (0, later(i)))
    tall = pl.BlockSpec((half, PANEL), lambda i: (later(i), 0))
    whole = lambda n, m: pl.BlockSpec((n, m), lambda i: (0, 0))
    return pl.pallas_call(
        body,
        grid=(3,),
        out_shape=jax.ShapeDtypeStruct((half, 1024), F32),
        in_specs=[sm, sm, wide, wide, whole(half, PANEL), whole(half, PANEL), tall, tall, whole(PANEL, PANEL), whole(PANEL, TILE)],
        out_specs=wide,
        scratch_shapes=[pltpu.VMEM((PANEL, PANEL), BF16)] * 2
        + [pltpu.VMEM((PANEL, two), BF16)] * 2
        + [pltpu.VMEM((2 * half, PANEL), BF16)] * 2
        + [pltpu.VMEM((half, PANEL), F32)],
        compiler_params=params(62),
        cost_estimate=pl.CostEstimate(flops=16_000_000_000, bytes_accessed=28 * MIB, transcendentals=0),
        name="finish",
    )(scalars, count, hk, hr, pk, pr, pc, pcr, u, v)


def shards_of(token_ids, column_order, residual, attn_out, out_proj, norm_gain):
    s = lax.axis_index("section").astype(jnp.int32)
    t = lax.axis_index("tensor").astype(jnp.int32)
    y, x = t // 4, t % 4
    z, yl, core = s // 4, (s // 2) % 2, s % 2

    def origin(dx, dy):
        return (y ^ dy) * 4 + (x - dx) % 4

    origins = jnp.stack([origin(*k) for k in KEYS])

    g_hi = lax.reduce_precision(norm_gain, 8, 7)
    g_mid = lax.reduce_precision(norm_gain - g_hi, 8, 7)
    g_lo = norm_gain - g_hi - g_mid
    parts = jnp.stack([g_hi, g_mid, g_lo]).astype(BF16)
    ext = jnp.concatenate([parts, jnp.zeros((EXT - 3, 1024), BF16)], axis=0)
    own = jnp.concatenate([attn_out, ext], axis=0)

    one = first(own, shift_t)
    two = second(*one, shift_t, 144)
    acc = project([[own], [one[0]]], out_proj, origins[:2])
    *two, acc = tie(*two, acc)
    three = third(two[0], two[1], shift_t, 144)
    acc = project([[one[1]], [two[0]], [one[2]], [two[1]]], out_proj, origins[2:6], acc)
    *three, acc = tie(*three, acc)
    a = listed(own, one, two, three)
    hidden = project(a[6:], out_proj, origins[6:], acc, residual)
    gains = [(pieces[-1], pieces[-1].shape[0] // EXT - 1) for pieces in a]

    tiles = [t]
    for dy in (1, 0):
        for dz in range(4):
            group = ((z + dz) % 4) * 2 + (yl ^ dy)
            tiles.append(16 * x + 2 * group + y)
    tiles += [j * 8 + t for j in range(8)]
    index = jnp.take(column_order.reshape(64, TILE), jnp.stack(tiles), axis=0).reshape(-1, 1)
    kept = (token_ids != 0).astype(F32).reshape(1, TOK)

    one = first(hidden, shift_t)
    rows_of = jnp.concatenate([index.reshape(-1, TILE), jnp.zeros((7, TILE), jnp.int32)], axis=0)
    gain = pick_gains(gains, origins, rows_of)
    *one, gain = tie(*one, gain)
    two = second(*one, shift_t, 512)
    carry = pick([[hidden], [one[0]]], origins[:2], index)
    *two, c0, c1 = tie(*two, *carry)
    three = third(two[0], two[1], shift_t, 512)
    carry = pick([[one[1]], [two[0]], [one[2]], [two[1]]], origins[2:6], index, (c0, c1))
    *three, c0, c1 = tie(*three, *carry)
    h = listed(hidden, one, two, three)
    message, rows0, cols = pick(h[6:], origins[6:], index, (c0, c1), gain, kept)

    same_core = [[c + 2 * g for g in range(8)] for c in range(2)]
    theirs = shift_s(message, 0, 1)
    head = TILE + EXT

    def part(msg, rows, dz):
        return jnp.concatenate([msg[:head], rows[dz * TILE : (dz + 1) * TILE]], axis=0)

    sent = [jnp.stack([part(message, rows0, dz), part(theirs, theirs[head:], dz)]) for dz in range(4)]
    got = [sent[0]] + [shift_s(sent[dz], dz, 0) for dz in (1, 2, 3)]
    pan8 = jnp.concatenate([g[:, :TILE] for g in got], axis=0)
    rows8 = jnp.concatenate([g[:, head:] for g in got], axis=0)
    kept_here = sum(jnp.sum(g[:, TILE : TILE + 1].astype(F32)) for g in got)
    count = (kept_here + shift_s(kept_here.reshape(1, 1), 0, 0, 1)[0, 0]).reshape(1)

    p1 = first(pan8, shift_t)
    p2 = second(*p1, shift_t, 4)
    p2, rows8, cols, count = tie(p2, rows8, cols, count)
    cols_all = lax.all_gather(cols, "section", axis=0, axis_index_groups=same_core)
    p3 = third(p2[0], p2[1], shift_t, 4)
    p3, rows8 = tie(p3, rows8)
    r1 = first(rows8, shift_t)
    pan_all, gram = panel_gram(listed(pan8, p1, p2, p3), origins)

    gram_other = shift_s(gram, 0, 0, 1)
    u, v = cholesky(0, 2, gram, other=gram_other, count=count)
    u, r1 = tie(u, r1)
    r2 = second(*r1, shift_t, 4)
    u, v = cholesky(2, 4, u, v)
    u, r2 = tie(u, r2)
    r3 = third(r2[0], r2[1], shift_t, 4)
    u, v = cholesky(4, 6, u, v)
    u, r3, cols_all = tie(u, r3, cols_all)
    slots = jnp.stack([((o // 4) ^ core) * 4 + o % 4 for o in [origin(*k) for k in KEYS]])
    chunks = jnp.stack([((z - dz) % 4) * 2 + (yl ^ dy) for dz in range(4) for dy in range(2)])
    hk, hs, pk, ps, pc = block_gram(listed(rows8, r1, r2, r3), cols_all, pan_all, slots, chunks)
    u, hs, ps, pc = tie(u, hs, ps, pc)
    hr, pr, pcr = [shift_s(w, 0, 0, 1) for w in (hs, ps, pc)]
    u, v = cholesky(6, 8, u, v)
    return finish(jnp.stack([s, t]), count, hk, hr, pk, pr, pc, pcr, u, v)


def solution(mesh):
    placed = (
        P("section"),
        P(),
        P("section", "tensor"),
        P("section", "tensor"),
        P(None, "tensor"),
        P("tensor"),
    )
    return jax.shard_map(
        shards_of, mesh=mesh, in_specs=placed, out_specs=P("section", "tensor"), check_vma=False
    )
```

```python
import functools

import jax
import jax.numpy as jnp
from jax import lax
from jax.experimental import pallas as pl
from jax.experimental.pallas import tpu as pltpu
from jax.sharding import PartitionSpec as P

TILE = 128
PANEL = 1024
WIDTH = 8192
TOK = 256
EXT = 16
epsilon = 1e-06
F32 = jnp.float32
BF16 = jnp.bfloat16
KEYS = [(0, 0), (0, 1), (1, 0), (1, 1), (3, 0), (3, 1), (2, 0), (2, 1)]
CHUNK = {(d, f): d * 2 + f for d in range(4) for f in range(2)}
MIB = 1024 * 1024


def params(limit=48):
    return pltpu.CompilerParams(vmem_limit_bytes=limit * MIB)


def shift_t(value, dx, dy):
    pairs = [(t, ((t // 4) ^ dy) * 4 + (t % 4 + dx) % 4) for t in range(8)]
    return lax.ppermute(value, "tensor", pairs)


def shift_s(value, dz, dy, dc=0):
    pairs = [(s, ((s // 4 + dz) % 4) * 4 + ((s % 4) ^ (2 * dy + dc))) for s in range(16)]
    return lax.ppermute(value, "section", pairs)


def tie(*values):
    return lax.optimization_barrier(values)


def first(x, shift):
    return shift(x, 0, 1), shift(x, 1, 0), shift(x, 3, 0)


def second(b, ra, la, shift, half):
    return shift(b, 1, 0), shift(b, 3, 0), shift(ra[:half], 1, 0), shift(la[half:], 3, 0)


def third(rb, lb, shift, half):
    return shift(rb[:half], 1, 0), shift(lb[half:], 3, 0)


def listed(x, one, two, three):
    return [[x], [one[0]], [one[1]], [two[0]], [one[2]], [two[1]], [two[2], two[3]], list(three)]


def flatten(shards):
    arrays, meta = [], []
    for pieces in shards:
        off, entry = 0, []
        for piece in pieces:
            entry.append((len(arrays), off, piece.shape[0]))
            arrays.append(piece)
            off += piece.shape[0]
        meta.append(entry)
    return arrays, meta


def nt(a, b):
    return lax.dot_general(a, b, (((1,), (1,)), ((), ())), preferred_element_type=F32)


def nn(a, b):
    return lax.dot_general(a, b, (((1,), (0,)), ((), ())), preferred_element_type=F32)


def split(a):
    hi = a.astype(BF16)
    return hi, (a - hi.astype(F32)).astype(BF16)


def dot3(op, a, b):
    left = jnp.concatenate([a[0], a[0], a[1]], axis=1)
    right = jnp.concatenate([b[0], b[1], b[0]], axis=0 if op is nn else 1)
    return op(left, right)


def project(shards, out_proj, origins, acc=None, residual=None):
    arrays, meta = flatten(shards)
    n = len(shards)
    final = residual is not None
    cols = out_proj.shape[1]

    def body(*refs):
        _, w_ref, *rest = refs
        pieces, rest = rest[: len(arrays)], rest[len(arrays) :]
        if acc is not None:
            acc_ref, *rest = rest
        if final:
            res_ref, *rest = rest
        out_ref, acc_s = rest
        i = pl.program_id(0)

        @pl.when(i == 0)
        def _():
            acc_s[...] = acc_ref[...] if acc is not None else jnp.zeros_like(acc_s)

        for r in range(n):

            @pl.when(i == r)
            def _(r=r):
                for j, off, size in meta[r]:
                    size = min(size, TOK - off)
                    acc_s[off : off + size, :] += nn(pieces[j][:size, :], w_ref[...])

        @pl.when(i == n - 1)
        def _():
            if final:
                h = (res_ref[...].astype(F32) + acc_s[...]).astype(BF16).astype(F32)
                out_ref[...] = h.T.astype(BF16)
            else:
                out_ref[...] = acc_s[...]

    whole = lambda shape: pl.BlockSpec(shape, lambda i, o: (0,) * len(shape))
    operands = [out_proj, *arrays]
    specs = [pl.BlockSpec((1024, cols), lambda i, o: (o[i], 0))] + [whole(a.shape) for a in arrays]
    if acc is not None:
        operands.append(acc)
        specs.append(whole(acc.shape))
    if final:
        operands.append(residual)
        specs.append(whole(residual.shape))
    shape = (cols, TOK) if final else (TOK, cols)
    return pl.pallas_call(
        body,
        out_shape=jax.ShapeDtypeStruct(shape, BF16 if final else F32),
        grid_spec=pltpu.PrefetchScalarGridSpec(
            num_scalar_prefetch=1,
            grid=(n,),
            in_specs=specs,
            out_specs=whole(shape),
            scratch_shapes=[pltpu.VMEM((TOK, cols), F32)],
        ),
        compiler_params=params(),
        cost_estimate=pl.CostEstimate(flops=2 * TOK * 1024 * cols * n, bytes_accessed=n * 2 * MIB, transcendentals=0),
        name="project",
    )(origins, *operands)


PICKS = 2176
SPLITS = ((0, TILE), (TILE, 512), (TILE + 512, 512), (TILE + 1024, 1024))


def hot_rows(index_ref, start, size, base):
    lane = lax.broadcasted_iota(jnp.int32, (size, 1024), 1)
    return jnp.where(index_ref[pl.ds(start, size), :] - base == lane, 1.0, 0.0).astype(BF16)


def pick_gains(gains, origins, index_rows):
    def body(origin, index_ref, *refs):
        gain_refs, out_ref = refs[:8], refs[8]
        got = [jnp.zeros((8, TILE), F32) for _ in range(3)]
        for r in range(8):
            whole = jnp.sum(gain_refs[r][...].astype(F32), axis=0, keepdims=True)
            for q in range(8):
                row = jnp.broadcast_to(whole[:, q * TILE : (q + 1) * TILE], (8, TILE))
                for i in range(3):
                    idx = index_ref[8 * i : 8 * i + 8, :]
                    here = jnp.take_along_axis(row, idx % TILE, axis=1)
                    got[i] = jnp.where(idx // TILE == origin[r] * 8 + q, here, got[i])
        for c in range(PICKS // TILE):
            if c % 8 == 0:
                column = got[c // 8].T
            out_ref[c * TILE : (c + 1) * TILE, :] = column[:, c % 8 : c % 8 + 1]

    vm = pl.BlockSpec(memory_space=pltpu.VMEM)
    specs = [pl.BlockSpec((EXT, 1024), functools.partial(lambda b, i: (b, 0), b)) for _, b in gains]
    return pl.pallas_call(
        body,
        grid=(1,),
        out_shape=jax.ShapeDtypeStruct((PICKS, 1), F32),
        in_specs=[pl.BlockSpec(memory_space=pltpu.SMEM), vm] + specs,
        out_specs=vm,
        compiler_params=params(),
        cost_estimate=pl.CostEstimate(flops=2_000_000_000, bytes_accessed=1 * MIB, transcendentals=0),
        name="pick_gains",
    )(origins, index_rows, *[g for g, _ in gains])


def pick(shards, origins, index, carry=None, gain=None, kept=None):
    arrays, meta = flatten(shards)
    n = len(shards)
    final = gain is not None

    def body(*refs):
        origin, index_ref, *rest = refs
        pieces, rest = rest[: len(arrays)], rest[len(arrays) :]
        if carry is not None:
            (acc_ref, sq_ref), rest = rest[:2], rest[2:]
        if final:
            (gain_ref, kept_ref), rest = rest[:2], rest[2:]
        outs, table = rest[:-1], rest[-1]
        step = 128
        total = sq_ref[...] if carry is not None else jnp.zeros((8, TOK), F32)
        for r in range(n):
            for j, off, size in meta[r]:

                def add(c, total, j=j, at=r * 1024 + off):
                    from_rows = pl.ds(pl.multiple_of(c * step, step), step)
                    v = pieces[j][from_rows, :]
                    table[pl.ds(pl.multiple_of(at + c * step, step), step), :] = v
                    v = v.astype(F32)
                    return total + jnp.sum((v * v).reshape(step // 8, 8, TOK), axis=0)

                total = lax.fori_loop(0, size // step, add, total)
        if final:
            scale = lax.rsqrt(jnp.sum(total, axis=0, keepdims=True) / WIDTH + epsilon) * kept_ref[...]
        else:
            outs[1][...] = total

        def value(start, size):
            got = jnp.zeros((size, TOK), F32)
            if carry is not None:
                got = acc_ref[pl.ds(start, size), :].astype(F32)
            for r in range(n):
                got += nn(hot_rows(index_ref, start, size, origin[r] * 1024), table[r * 1024 : (r + 1) * 1024, :])
            if final:
                got = got * scale * gain_ref[pl.ds(start, size), :]
            return got.astype(BF16)

        def fill(ref, base, to, rows, block):
            def one(c, _):
                at = pl.multiple_of(c * block, block)
                ref[pl.ds(to + at, block), :] = value(pl.multiple_of(base + at, TILE), block)
                return 0

            lax.fori_loop(0, rows // block, one, 0)

        places = ((0, 0), (0, TILE + EXT), (1, 0), (2, 0)) if final else tuple((0, base) for base, _ in SPLITS)
        for (base, rows), (o, to) in zip(SPLITS, places):
            fill(outs[o], base, to, rows, min(rows, 256))
        if final:
            row0 = lax.broadcasted_iota(jnp.int32, (EXT, TOK), 0) == 0
            outs[0][TILE : TILE + EXT, :] = jnp.where(row0, kept_ref[...], 0.0).astype(BF16)

    vm = pl.BlockSpec(memory_space=pltpu.VMEM)
    operands = [origins, index, *arrays]
    if carry is not None:
        operands += list(carry)
    if final:
        operands += [gain, kept]
        outs = [jax.ShapeDtypeStruct(s, BF16) for s in ((TILE + EXT + 512, TOK), (512, TOK), (1024, TOK))]
    else:
        outs = [jax.ShapeDtypeStruct((PICKS, TOK), BF16), jax.ShapeDtypeStruct((8, TOK), F32)]
    return pl.pallas_call(
        body,
        out_shape=outs,
        in_specs=[pl.BlockSpec(memory_space=pltpu.SMEM)] + [vm] * (len(operands) - 1),
        out_specs=[vm] * len(outs),
        scratch_shapes=[pltpu.VMEM((1024 * n, TOK), BF16)],
        compiler_params=params(),
        cost_estimate=pl.CostEstimate(flops=2 * PICKS * 1024 * n * TOK, bytes_accessed=4 * MIB, transcendentals=0),
        name="pick",
    )(*operands)


def place(pieces, meta, slot, scratch):
    for r in range(8):
        row = pl.multiple_of(slot[r] * TILE, TILE)
        for j, off, size in meta[r]:
            for c in range(size):
                scratch[pl.ds(row, TILE), (off + c) * TOK : (off + c + 1) * TOK] = pieces[j][c]


def panel_gram(shards, slots):
    arrays, meta = flatten(shards)

    def body(slot, *refs):
        pieces, (pan_ref, gram_ref) = refs[: len(arrays)], refs[len(arrays) :]
        place(pieces, meta, slot, pan_ref)

        def one(c, _):
            rows = pl.ds(pl.multiple_of(c * 256, 256), 256)
            gram_ref[rows, :] = nt(pan_ref[rows, :], pan_ref[...])
            return 0

        lax.fori_loop(0, 4, one, 0)

    vm = pl.BlockSpec(memory_space=pltpu.VMEM)
    return pl.pallas_call(
        body,
        out_shape=[jax.ShapeDtypeStruct((PANEL, 2048), BF16), jax.ShapeDtypeStruct((PANEL, PANEL), F32)],
        in_specs=[pl.BlockSpec(memory_space=pltpu.SMEM)] + [vm] * len(arrays),
        out_specs=[vm] * 2,
        compiler_params=params(),
        cost_estimate=pl.CostEstimate(flops=1_000_000, bytes_accessed=1024, transcendentals=0),
        name="panel_gram",
    )(slots, *arrays)


def block_gram(row_shards, cols_all, pan, slots, chunks):
    row_arrays, row_meta = flatten(row_shards)
    steps = 4

    def body(slot, chunk, pan_ref, col_ref, *refs):
        rp, refs = refs[: len(row_arrays)], refs[len(row_arrays) :]
        hk_ref, hs_ref, pk_ref, ps_ref, pc_ref, rows, cols = refs
        i = pl.program_id(0)

        @pl.when(i == 0)
        def _():
            place(rp, row_meta, slot, rows)
            for c in range(8):
                cols[:, c * TOK : (c + 1) * TOK] = col_ref[chunk[c]]

        at = pl.ds(pl.multiple_of(i * TILE, TILE), TILE)
        to = pl.ds(pl.multiple_of(512 + i * TILE, TILE), TILE)
        both = jnp.concatenate([rows[at, :], rows[to, :]], axis=0)
        p = nt(both, pan_ref[...])
        pk_ref[...], ps_ref[...] = p[:TILE], p[TILE:]
        h = nt(both, cols[...])
        hk_ref[...], hs_ref[...] = h[:TILE], h[TILE:]
        pc_ref[...] = nt(cols[pl.ds(pl.multiple_of(i * 256, 256), 256), :], pan_ref[...])

    vm = pl.BlockSpec(memory_space=pltpu.VMEM)
    outs = [(512, 1024)] * 4 + [(1024, PANEL)]
    return pl.pallas_call(
        body,
        grid=(steps,),
        out_shape=[jax.ShapeDtypeStruct(s, F32) for s in outs],
        in_specs=[pl.BlockSpec(memory_space=pltpu.SMEM)] * 2 + [vm, vm] + [vm] * len(row_arrays),
        out_specs=[pl.BlockSpec((n // steps, 1024), lambda i: (i, 0)) for n, _ in outs],
        scratch_shapes=[pltpu.VMEM((1024, 2048), BF16)] * 2,
        compiler_params=params(),
        cost_estimate=pl.CostEstimate(flops=6 * 1024 * 1024 * 2048, bytes_accessed=24 * MIB, transcendentals=0),
        name="block_gram",
    )(slots, chunks, pan, cols_all, *row_arrays)


def factor_tile(a):
    groups, m = TILE // 8, 8
    lane = lax.broadcasted_iota(jnp.int32, (8, TILE), 1)
    sub = lax.broadcasted_iota(jnp.int32, (8, TILE), 0)
    A = [a[8 * g : 8 * g + 8, :] for g in range(groups)]
    E = [jnp.where(lane == sub + 8 * g, 1.0, 0.0).astype(F32) for g in range(groups)]

    def wide(v):
        return jnp.broadcast_to(v, (8, TILE))

    for g0 in range(groups):
        j = 8 * g0
        piv = {(i, l): wide(A[g0][i : i + 1, j + l : j + l + 1]) for i in range(m) for l in range(i, m)}
        R = [wide(A[g0][i : i + 1, :]) for i in range(m)]
        RE = [wide(E[g0][i : i + 1, :]) for i in range(m)]
        f, inv = {}, []
        for i in range(m):
            inv.append(1.0 / piv[i, i])
            for l in range(i + 1, m):
                f[i, l] = piv[i, l] * inv[i]
            for l in range(i + 1, m):
                for q in range(l, m):
                    piv[l, q] = piv[l, q] - (piv[i, l] * piv[i, q]) * inv[i]
                R[l] = R[l] - f[i, l] * R[i]
                RE[l] = RE[l] - f[i, l] * RE[i]
        W, WE = [None] * m, [None] * m
        for i in reversed(range(m)):
            W[i], WE[i] = R[i] * inv[i], RE[i] * inv[i]
            for l in range(i + 1, m):
                W[i] = W[i] - f[i, l] * W[l]
                WE[i] = WE[i] - f[i, l] * WE[l]
        for g in range(g0 + 1, groups):
            ag, eg = A[g], E[g]
            for l in reversed(range(m)):
                col = A[g][:, j + l : j + l + 1]
                ag = ag - col * W[l]
                eg = eg - col * WE[l]
            A[g], E[g] = ag, eg
        ag, eg = R[0], RE[0]
        for i in range(1, m):
            ag = jnp.where(sub == i, R[i], ag)
            eg = jnp.where(sub == i, RE[i], eg)
        A[g0], E[g0] = ag, eg
    U, V = [], []
    for g in range(groups):
        diag = jnp.sum(jnp.where(lane == sub + 8 * g, A[g], 0.0), axis=1, keepdims=True)
        rs = lax.rsqrt(diag)
        U.append(jnp.where(lane >= sub + 8 * g, A[g] * rs, 0.0))
        V.append(E[g] * rs)
    return jnp.concatenate(U, axis=0), jnp.concatenate(V, axis=0)


def cholesky(a, other=None, count=None):
    n = a.shape[0]
    tiles = n // TILE
    start = other is not None
    band = 2 * TILE
    more = n > band

    def body(*refs):
        if start:
            count_ref, g_ref, o_ref, *refs = refs
            inv = 1.0 / count_ref[0]
        else:
            g_ref, *refs = refs
        band_ref, v_ref, *refs = refs
        if more:
            rest_ref, *refs = refs
        w, ph, plo, lh, ll = refs

        def load(c, _):
            rows = pl.ds(pl.multiple_of(c * TILE, TILE), TILE)
            w[rows, :] = (g_ref[rows, :] + o_ref[rows, :]) * inv if start else g_ref[rows, :]
            return 0

        lax.fori_loop(0, tiles, load, 0)

        def step(k, _):
            at = pl.ds(pl.multiple_of(k * TILE, TILE), TILE)
            U, V = factor_tile(w[at, at])
            v_ref[at, :] = V
            vs = split(V)
            panel = dot3(nn, vs, split(w[at, :]))
            ph[...], plo[...] = split(panel)
            left = dot3(nt, split(w[:, at]), vs)
            lh[...], ll[...] = split(left)
            band_ref[at, :] = panel
            band_ref[at, at] = U

            def update(j, _):
                rows = pl.ds(pl.multiple_of(j * TILE, TILE), TILE)
                w[rows, :] -= dot3(nn, (lh[rows, :], ll[rows, :]), (ph[...], plo[...]))
                return 0

            lax.fori_loop(k + 1, tiles, update, 0)
            return 0

        lax.fori_loop(0, 2, step, 0)
        if more:

            def keep(c, _):
                rows = pl.ds(pl.multiple_of(c * TILE, TILE), TILE)
                rest_ref[rows, :] = w[pl.ds(pl.multiple_of(band + c * TILE, TILE), TILE), band:]
                return 0

            lax.fori_loop(0, tiles - 2, keep, 0)

    vm = pl.BlockSpec(memory_space=pltpu.VMEM)
    sm = pl.BlockSpec(memory_space=pltpu.SMEM)
    outs = [(band, n), (band, TILE)] + ([(n - band, n - band)] if more else [])
    return pl.pallas_call(
        body,
        out_shape=[jax.ShapeDtypeStruct(o, F32) for o in outs],
        in_specs=[sm, vm, vm] if start else [vm],
        out_specs=[vm] * len(outs),
        scratch_shapes=[pltpu.VMEM((n, n), F32)] + [pltpu.VMEM((TILE, n), BF16)] * 2 + [pltpu.VMEM((n, TILE), BF16)] * 2,
        compiler_params=params(24),
        cost_estimate=pl.CostEstimate(flops=1_000_000, bytes_accessed=1024, transcendentals=0),
        name="cholesky",
    )(*((count, a, other) if start else (a,)))


def finish(scalars, count, hk, hr, pk, pr, pc, pcr, bands, inverses):
    two, half = 2 * TILE, 512
    pairs = PANEL // two

    def body(sc, count_ref, hk_ref, hr_ref, pk_ref, pr_ref, pc_ref, pcr_ref, *refs):
        u_refs, v_refs, refs = refs[:pairs], refs[pairs : 2 * pairs], refs[2 * pairs :]
        out_ref, uh, ul, vh, vl, xh, xl, b = refs
        i = pl.program_id(0)
        inv = 1.0 / count_ref[0]

        @pl.when(i == 0)
        def _():
            for k in range(pairs):
                for c in (0, TILE):
                    rows, cols = slice(k * two + c, k * two + c + TILE), slice(k * two, PANEL)
                    uh[rows, cols], ul[rows, cols] = split(u_refs[k][c : c + TILE, :])

            for k in range(pairs):
                top, low = slice(k * two, k * two + TILE), slice(k * two + TILE, (k + 1) * two)
                v1, v2 = split(v_refs[k][:TILE, :]), split(v_refs[k][TILE:, :])
                cross = dot3(nn, split(u_refs[k][:TILE, TILE:two].T), v1)
                cross = -dot3(nn, v2, split(cross))
                vh[top, :TILE], vl[top, :TILE] = v1
                vh[low, TILE:], vl[low, TILE:] = v2
                vh[top, TILE:] = jnp.zeros((TILE, TILE), BF16)
                vl[top, TILE:] = jnp.zeros((TILE, TILE), BF16)
                vh[low, :TILE], vl[low, :TILE] = split(cross)

            def load(c, _):
                rows = pl.ds(pl.multiple_of(c * TILE, TILE), TILE)
                b[rows, :] = (pk_ref[rows, :] + pr_ref[rows, :]) * inv
                return 0

            lax.fori_loop(0, half // TILE, load, 0)

        @pl.when(i > 0)
        def _():
            def load(c, _):
                rows = pl.ds(pl.multiple_of(c * TILE, TILE), TILE)
                b[rows, :] = (pc_ref[rows, :] + pcr_ref[rows, :]) * inv
                return 0

            lax.fori_loop(0, half // TILE, load, 0)

        to = pl.ds(pl.multiple_of(jnp.minimum(i, 1) * half, half), half)
        for k in range(pairs):
            here, after = slice(k * two, (k + 1) * two), slice((k + 1) * two, PANEL)
            x = dot3(nt, split(b[:, here]), (vh[here, :], vl[here, :]))
            xs = split(x)
            b[:, here] = x
            xh[to, here], xl[to, here] = xs
            if k + 1 < pairs:
                b[:, after] -= dot3(nn, xs, (uh[here, after], ul[here, after]))

        @pl.when(i == 0)
        def _():
            def left(c, _):
                rows = pl.ds(pl.multiple_of(c * TILE, TILE), TILE)
                own = b[rows, pl.ds(pl.multiple_of(sc[1] * TILE, TILE), TILE)]
                row = (c * 16 + sc[0]) * TILE + lax.broadcasted_iota(jnp.int32, (TILE, TILE), 0)
                col = sc[1] * TILE + lax.broadcasted_iota(jnp.int32, (TILE, TILE), 1)
                out_ref[rows, :TILE] = jnp.where(row >= col, own, 0.0)
                return 0

            lax.fori_loop(0, half // TILE, left, 0)

        def trail(c, first):
            rows = pl.ds(pl.multiple_of(c * two, two), two)
            cols = slice(half + first, 2 * half)
            up = dot3(nt, (xh[rows, :], xl[rows, :]), (xh[cols, :], xl[cols, :]))
            out_ref[rows, first:] = (hk_ref[rows, first:] + hr_ref[rows, first:]) * inv - up

        @pl.when(i == 1)
        def _():
            lax.fori_loop(0, half // two, lambda c, _: (trail(c, TILE), 0)[1], 0)

        @pl.when(i == 2)
        def _():
            lax.fori_loop(0, half // two, lambda c, _: (trail(c, 0), 0)[1], 0)

    sm = pl.BlockSpec(memory_space=pltpu.SMEM)
    later = lambda i: jnp.maximum(i - 1, 0)
    wide = pl.BlockSpec((half, half), lambda i: (0, later(i)))
    tall = pl.BlockSpec((half, PANEL), lambda i: (later(i), 0))
    whole = lambda n, m: pl.BlockSpec((n, m), lambda i: (0, 0))
    return pl.pallas_call(
        body,
        grid=(3,),
        out_shape=jax.ShapeDtypeStruct((half, 1024), F32),
        in_specs=[sm, sm, wide, wide, whole(half, PANEL), whole(half, PANEL), tall, tall]
        + [whole(two, PANEL - k * two) for k in range(pairs)]
        + [whole(two, TILE)] * pairs,
        out_specs=wide,
        scratch_shapes=[pltpu.VMEM((PANEL, PANEL), BF16)] * 2
        + [pltpu.VMEM((PANEL, two), BF16)] * 2
        + [pltpu.VMEM((2 * half, PANEL), BF16)] * 2
        + [pltpu.VMEM((half, PANEL), F32)],
        compiler_params=params(62),
        cost_estimate=pl.CostEstimate(flops=16_000_000_000, bytes_accessed=28 * MIB, transcendentals=0),
        name="finish",
    )(scalars, count, hk, hr, pk, pr, pc, pcr, *bands, *inverses)


def shards_of(token_ids, column_order, residual, attn_out, out_proj, norm_gain):
    s = lax.axis_index("section").astype(jnp.int32)
    t = lax.axis_index("tensor").astype(jnp.int32)
    y, x = t // 4, t % 4
    z, yl, core = s // 4, (s // 2) % 2, s % 2

    def origin(dx, dy):
        return (y ^ dy) * 4 + (x - dx) % 4

    origins = jnp.stack([origin(*k) for k in KEYS])

    g_hi = lax.reduce_precision(norm_gain, 8, 7)
    g_mid = lax.reduce_precision(norm_gain - g_hi, 8, 7)
    g_lo = norm_gain - g_hi - g_mid
    parts = jnp.stack([g_hi, g_mid, g_lo]).astype(BF16)
    ext = jnp.concatenate([parts, jnp.zeros((EXT - 3, 1024), BF16)], axis=0)
    own = jnp.concatenate([attn_out, ext], axis=0)

    one = first(own, shift_t)
    two = second(*one, shift_t, 144)
    acc = project([[own], [one[0]]], out_proj, origins[:2])
    *two, acc = tie(*two, acc)
    three = third(two[0], two[1], shift_t, 144)
    acc = project([[one[1]], [two[0]], [one[2]], [two[1]]], out_proj, origins[2:6], acc)
    *three, acc = tie(*three, acc)
    a = listed(own, one, two, three)
    hidden = project(a[6:], out_proj, origins[6:], acc, residual)
    gains = [(pieces[-1], pieces[-1].shape[0] // EXT - 1) for pieces in a]

    tiles = [t]
    for dy in (1, 0):
        for dz in range(4):
            group = ((z + dz) % 4) * 2 + (yl ^ dy)
            tiles.append(16 * x + 2 * group + y)
    tiles += [j * 8 + t for j in range(8)]
    index = jnp.take(column_order.reshape(64, TILE), jnp.stack(tiles), axis=0).reshape(-1, 1)
    kept = (token_ids != 0).astype(F32).reshape(1, TOK)

    one = first(hidden, shift_t)
    rows_of = jnp.concatenate([index.reshape(-1, TILE), jnp.zeros((7, TILE), jnp.int32)], axis=0)
    gain = pick_gains(gains, origins, rows_of)
    *one, gain = tie(*one, gain)
    two = second(*one, shift_t, 512)
    carry = pick([[hidden], [one[0]]], origins[:2], index)
    *two, c0, c1 = tie(*two, *carry)
    three = third(two[0], two[1], shift_t, 512)
    carry = pick([[one[1]], [two[0]], [one[2]], [two[1]]], origins[2:6], index, (c0, c1))
    *three, c0, c1 = tie(*three, *carry)
    h = listed(hidden, one, two, three)
    message, rows0, cols = pick(h[6:], origins[6:], index, (c0, c1), gain, kept)

    same_core = [[c + 2 * g for g in range(8)] for c in range(2)]
    theirs = shift_s(message, 0, 1)
    head = TILE + EXT

    def part(msg, rows, dz):
        return jnp.concatenate([msg[:head], rows[dz * TILE : (dz + 1) * TILE]], axis=0)

    sent = [jnp.stack([part(message, rows0, dz), part(theirs, theirs[head:], dz)]) for dz in range(4)]
    got = [sent[0]] + [shift_s(sent[dz], dz, 0) for dz in (1, 2, 3)]
    pan8 = jnp.concatenate([g[:, :TILE] for g in got], axis=0)
    rows8 = jnp.concatenate([g[:, head:] for g in got], axis=0)
    kept_here = sum(jnp.sum(g[:, TILE : TILE + 1].astype(F32)) for g in got)
    count = (kept_here + shift_s(kept_here.reshape(1, 1), 0, 0, 1)[0, 0]).reshape(1)

    p1 = first(pan8, shift_t)
    p2 = second(*p1, shift_t, 4)
    p2, rows8, cols, count = tie(p2, rows8, cols, count)
    cols_all = lax.all_gather(cols, "section", axis=0, axis_index_groups=same_core)
    p3 = third(p2[0], p2[1], shift_t, 4)
    p3, rows8 = tie(p3, rows8)
    r1 = first(rows8, shift_t)
    pan_all, gram = panel_gram(listed(pan8, p1, p2, p3), origins)

    gram_other = shift_s(gram, 0, 0, 1)
    u0, v0, u = cholesky(gram, gram_other, count)
    u, r1 = tie(u, r1)
    r2 = second(*r1, shift_t, 4)
    u1, v1, u = cholesky(u)
    u, r2 = tie(u, r2)
    r3 = third(r2[0], r2[1], shift_t, 4)
    u2, v2, u = cholesky(u)
    u, r3, cols_all = tie(u, r3, cols_all)
    slots = jnp.stack([((o // 4) ^ core) * 4 + o % 4 for o in [origin(*k) for k in KEYS]])
    chunks = jnp.stack([((z - dz) % 4) * 2 + (yl ^ dy) for dz in range(4) for dy in range(2)])
    hk, hs, pk, ps, pc = block_gram(listed(rows8, r1, r2, r3), cols_all, pan_all, slots, chunks)
    u, hs, ps, pc = tie(u, hs, ps, pc)
    hr, pr, pcr = [shift_s(w, 0, 0, 1) for w in (hs, ps, pc)]
    u3, v3 = cholesky(u)
    scalars = jnp.stack([s, t])
    return finish(scalars, count, hk, hr, pk, pr, pc, pcr, (u0, u1, u2, u3), (v0, v1, v2, v3))


def solution(mesh):
    placed = (
        P("section"),
        P(),
        P("section", "tensor"),
        P("section", "tensor"),
        P(None, "tensor"),
        P("tensor"),
    )
    return jax.shard_map(
        shards_of, mesh=mesh, in_specs=placed, out_specs=P("section", "tensor"), check_vma=False
    )
```

```python
import functools

import jax
import jax.numpy as jnp
from jax import lax
from jax.experimental import pallas as pl
from jax.experimental.pallas import tpu as pltpu
from jax.sharding import PartitionSpec as P

TILE = 128
PANEL = 1024
WIDTH = 8192
TOK = 256
EXT = 16
epsilon = 1e-06
F32 = jnp.float32
BF16 = jnp.bfloat16
KEYS = [(0, 0), (0, 1), (1, 0), (1, 1), (3, 0), (3, 1), (2, 0), (2, 1)]
CHUNK = {(d, f): d * 2 + f for d in range(4) for f in range(2)}
MIB = 1024 * 1024


def params(limit=48):
    return pltpu.CompilerParams(vmem_limit_bytes=limit * MIB)


def shift_t(value, dx, dy):
    pairs = [(t, ((t // 4) ^ dy) * 4 + (t % 4 + dx) % 4) for t in range(8)]
    return lax.ppermute(value, "tensor", pairs)


def shift_s(value, dz, dy, dc=0):
    pairs = [(s, ((s // 4 + dz) % 4) * 4 + ((s % 4) ^ (2 * dy + dc))) for s in range(16)]
    return lax.ppermute(value, "section", pairs)


def tie(*values):
    return lax.optimization_barrier(values)


def first(x, shift):
    return shift(x, 0, 1), shift(x, 1, 0), shift(x, 3, 0)


def second(b, ra, la, shift, half):
    return shift(b, 1, 0), shift(b, 3, 0), shift(ra[:half], 1, 0), shift(la[half:], 3, 0)


def third(rb, lb, shift, half):
    return shift(rb[:half], 1, 0), shift(lb[half:], 3, 0)


def listed(x, one, two, three):
    return [[x], [one[0]], [one[1]], [two[0]], [one[2]], [two[1]], [two[2], two[3]], list(three)]


def flatten(shards):
    arrays, meta = [], []
    for pieces in shards:
        off, entry = 0, []
        for piece in pieces:
            entry.append((len(arrays), off, piece.shape[0]))
            arrays.append(piece)
            off += piece.shape[0]
        meta.append(entry)
    return arrays, meta


def nt(a, b):
    return lax.dot_general(a, b, (((1,), (1,)), ((), ())), preferred_element_type=F32)


def nn(a, b):
    return lax.dot_general(a, b, (((1,), (0,)), ((), ())), preferred_element_type=F32)


def split(a):
    hi = a.astype(BF16)
    return hi, (a - hi.astype(F32)).astype(BF16)


def dot3(op, a, b):
    left = jnp.concatenate([a[0], a[0], a[1]], axis=1)
    right = jnp.concatenate([b[0], b[1], b[0]], axis=0 if op is nn else 1)
    return op(left, right)


def project(shards, out_proj, origins, acc=None, residual=None):
    arrays, meta = flatten(shards)
    n = len(shards)
    final = residual is not None
    cols = out_proj.shape[1]

    def body(*refs):
        _, w_ref, *rest = refs
        pieces, rest = rest[: len(arrays)], rest[len(arrays) :]
        if acc is not None:
            acc_ref, *rest = rest
        if final:
            res_ref, *rest = rest
        out_ref, acc_s = rest
        i = pl.program_id(0)

        @pl.when(i == 0)
        def _():
            acc_s[...] = acc_ref[...] if acc is not None else jnp.zeros_like(acc_s)

        for r in range(n):

            @pl.when(i == r)
            def _(r=r):
                for j, off, size in meta[r]:
                    size = min(size, TOK - off)
                    acc_s[off : off + size, :] += nn(pieces[j][:size, :], w_ref[...])

        @pl.when(i == n - 1)
        def _():
            if final:
                h = (res_ref[...].astype(F32) + acc_s[...]).astype(BF16).astype(F32)
                out_ref[...] = h.T.astype(BF16)
            else:
                out_ref[...] = acc_s[...]

    whole = lambda shape: pl.BlockSpec(shape, lambda i, o: (0,) * len(shape))
    operands = [out_proj, *arrays]
    specs = [pl.BlockSpec((1024, cols), lambda i, o: (o[i], 0))] + [whole(a.shape) for a in arrays]
    if acc is not None:
        operands.append(acc)
        specs.append(whole(acc.shape))
    if final:
        operands.append(residual)
        specs.append(whole(residual.shape))
    shape = (cols, TOK) if final else (TOK, cols)
    return pl.pallas_call(
        body,
        out_shape=jax.ShapeDtypeStruct(shape, BF16 if final else F32),
        grid_spec=pltpu.PrefetchScalarGridSpec(
            num_scalar_prefetch=1,
            grid=(n,),
            in_specs=specs,
            out_specs=whole(shape),
            scratch_shapes=[pltpu.VMEM((TOK, cols), F32)],
        ),
        compiler_params=params(),
        cost_estimate=pl.CostEstimate(flops=2 * TOK * 1024 * cols * n, bytes_accessed=n * 2 * MIB, transcendentals=0),
        name="project",
    )(origins, *operands)


PICKS = 2176
SPLITS = ((0, TILE), (TILE, 512), (TILE + 512, 512), (TILE + 1024, 1024))


def hot_rows(index_ref, start, size, base):
    lane = lax.broadcasted_iota(jnp.int32, (size, 1024), 1)
    return jnp.where(index_ref[pl.ds(start, size), :] - base == lane, 1.0, 0.0).astype(BF16)


def pick_gains(gains, origins, index_rows):
    def body(origin, index_ref, *refs):
        gain_refs, out_ref = refs[:8], refs[8]
        got = [jnp.zeros((8, TILE), F32) for _ in range(3)]
        for r in range(8):
            whole = jnp.sum(gain_refs[r][...].astype(F32), axis=0, keepdims=True)
            for q in range(8):
                row = jnp.broadcast_to(whole[:, q * TILE : (q + 1) * TILE], (8, TILE))
                for i in range(3):
                    idx = index_ref[8 * i : 8 * i + 8, :]
                    here = jnp.take_along_axis(row, idx % TILE, axis=1)
                    got[i] = jnp.where(idx // TILE == origin[r] * 8 + q, here, got[i])
        for c in range(PICKS // TILE):
            if c % 8 == 0:
                column = got[c // 8].T
            out_ref[c * TILE : (c + 1) * TILE, :] = column[:, c % 8 : c % 8 + 1]

    vm = pl.BlockSpec(memory_space=pltpu.VMEM)
    specs = [pl.BlockSpec((EXT, 1024), functools.partial(lambda b, i: (b, 0), b)) for _, b in gains]
    return pl.pallas_call(
        body,
        grid=(1,),
        out_shape=jax.ShapeDtypeStruct((PICKS, 1), F32),
        in_specs=[pl.BlockSpec(memory_space=pltpu.SMEM), vm] + specs,
        out_specs=vm,
        compiler_params=params(),
        cost_estimate=pl.CostEstimate(flops=2_000_000_000, bytes_accessed=1 * MIB, transcendentals=0),
        name="pick_gains",
    )(origins, index_rows, *[g for g, _ in gains])


def pick(shards, origins, index, carry=None, gain=None, kept=None):
    arrays, meta = flatten(shards)
    n = len(shards)
    final = gain is not None

    def body(*refs):
        origin, index_ref, *rest = refs
        pieces, rest = rest[: len(arrays)], rest[len(arrays) :]
        if carry is not None:
            (acc_ref, sq_ref), rest = rest[:2], rest[2:]
        if final:
            (gain_ref, kept_ref), rest = rest[:2], rest[2:]
        outs, table = rest[:-1], rest[-1]
        step = 128
        total = sq_ref[...] if carry is not None else jnp.zeros((8, TOK), F32)
        for r in range(n):
            for j, off, size in meta[r]:

                def add(c, total, j=j, at=r * 1024 + off):
                    from_rows = pl.ds(pl.multiple_of(c * step, step), step)
                    v = pieces[j][from_rows, :]
                    table[pl.ds(pl.multiple_of(at + c * step, step), step), :] = v
                    v = v.astype(F32)
                    return total + jnp.sum((v * v).reshape(step // 8, 8, TOK), axis=0)

                total = lax.fori_loop(0, size // step, add, total)
        if final:
            scale = lax.rsqrt(jnp.sum(total, axis=0, keepdims=True) / WIDTH + epsilon) * kept_ref[...]
        else:
            outs[1][...] = total

        def value(start, size):
            got = jnp.zeros((size, TOK), F32)
            if carry is not None:
                got = acc_ref[pl.ds(start, size), :].astype(F32)
            for r in range(n):
                got += nn(hot_rows(index_ref, start, size, origin[r] * 1024), table[r * 1024 : (r + 1) * 1024, :])
            if final:
                got = got * scale * gain_ref[pl.ds(start, size), :]
            return got.astype(BF16)

        def fill(ref, base, to, rows, block):
            def one(c, _):
                at = pl.multiple_of(c * block, block)
                ref[pl.ds(to + at, block), :] = value(pl.multiple_of(base + at, TILE), block)
                return 0

            lax.fori_loop(0, rows // block, one, 0)

        places = ((0, 0), (0, TILE + EXT), (1, 0), (2, 0)) if final else tuple((0, base) for base, _ in SPLITS)
        for (base, rows), (o, to) in zip(SPLITS, places):
            fill(outs[o], base, to, rows, min(rows, 256))
        if final:
            row0 = lax.broadcasted_iota(jnp.int32, (EXT, TOK), 0) == 0
            outs[0][TILE : TILE + EXT, :] = jnp.where(row0, kept_ref[...], 0.0).astype(BF16)

    vm = pl.BlockSpec(memory_space=pltpu.VMEM)
    operands = [origins, index, *arrays]
    if carry is not None:
        operands += list(carry)
    if final:
        operands += [gain, kept]
        outs = [jax.ShapeDtypeStruct(s, BF16) for s in ((TILE + EXT + 512, TOK), (512, TOK), (1024, TOK))]
    else:
        outs = [jax.ShapeDtypeStruct((PICKS, TOK), BF16), jax.ShapeDtypeStruct((8, TOK), F32)]
    return pl.pallas_call(
        body,
        out_shape=outs,
        in_specs=[pl.BlockSpec(memory_space=pltpu.SMEM)] + [vm] * (len(operands) - 1),
        out_specs=[vm] * len(outs),
        scratch_shapes=[pltpu.VMEM((1024 * n, TOK), BF16)],
        compiler_params=params(),
        cost_estimate=pl.CostEstimate(flops=2 * PICKS * 1024 * n * TOK, bytes_accessed=4 * MIB, transcendentals=0),
        name="pick",
    )(*operands)


def place(pieces, meta, slot, scratch):
    for r in range(8):
        row = pl.multiple_of(slot[r] * TILE, TILE)
        for j, off, size in meta[r]:
            for c in range(size):
                scratch[pl.ds(row, TILE), (off + c) * TOK : (off + c + 1) * TOK] = pieces[j][c]


def panel_gram(shards, slots):
    arrays, meta = flatten(shards)

    def body(slot, *refs):
        pieces, (pan_ref, gram_ref) = refs[: len(arrays)], refs[len(arrays) :]
        place(pieces, meta, slot, pan_ref)

        def one(c, _):
            rows = pl.ds(pl.multiple_of(c * 256, 256), 256)
            gram_ref[rows, :] = nt(pan_ref[rows, :], pan_ref[...])
            return 0

        lax.fori_loop(0, 4, one, 0)

    vm = pl.BlockSpec(memory_space=pltpu.VMEM)
    return pl.pallas_call(
        body,
        out_shape=[jax.ShapeDtypeStruct((PANEL, 2048), BF16), jax.ShapeDtypeStruct((PANEL, PANEL), F32)],
        in_specs=[pl.BlockSpec(memory_space=pltpu.SMEM)] + [vm] * len(arrays),
        out_specs=[vm] * 2,
        compiler_params=params(),
        cost_estimate=pl.CostEstimate(flops=1_000_000, bytes_accessed=1024, transcendentals=0),
        name="panel_gram",
    )(slots, *arrays)


def block_gram(row_shards, cols_all, pan, slots, chunks):
    row_arrays, row_meta = flatten(row_shards)
    steps = 4

    def body(slot, chunk, pan_ref, col_ref, *refs):
        rp, refs = refs[: len(row_arrays)], refs[len(row_arrays) :]
        hk_ref, hs_ref, pk_ref, ps_ref, pc_ref, rows, cols = refs
        i = pl.program_id(0)

        @pl.when(i == 0)
        def _():
            place(rp, row_meta, slot, rows)
            for c in range(8):
                cols[:, c * TOK : (c + 1) * TOK] = col_ref[chunk[c]]

        at = pl.ds(pl.multiple_of(i * TILE, TILE), TILE)
        to = pl.ds(pl.multiple_of(512 + i * TILE, TILE), TILE)
        both = jnp.concatenate([rows[at, :], rows[to, :]], axis=0)
        p = nt(both, pan_ref[...])
        pk_ref[...], ps_ref[...] = p[:TILE], p[TILE:]
        h = nt(both, cols[...])
        hk_ref[...], hs_ref[...] = h[:TILE], h[TILE:]
        pc_ref[...] = nt(cols[pl.ds(pl.multiple_of(i * 256, 256), 256), :], pan_ref[...])

    vm = pl.BlockSpec(memory_space=pltpu.VMEM)
    outs = [(512, 1024)] * 4 + [(1024, PANEL)]
    return pl.pallas_call(
        body,
        grid=(steps,),
        out_shape=[jax.ShapeDtypeStruct(s, F32) for s in outs],
        in_specs=[pl.BlockSpec(memory_space=pltpu.SMEM)] * 2 + [vm, vm] + [vm] * len(row_arrays),
        out_specs=[pl.BlockSpec((n // steps, 1024), lambda i: (i, 0)) for n, _ in outs],
        scratch_shapes=[pltpu.VMEM((1024, 2048), BF16)] * 2,
        compiler_params=params(62),
        cost_estimate=pl.CostEstimate(flops=6 * 1024 * 1024 * 2048, bytes_accessed=24 * MIB, transcendentals=0),
        name="block_gram",
    )(slots, chunks, pan, cols_all, *row_arrays)


def factor_tile(a):
    groups, m = TILE // 8, 8
    lane = lax.broadcasted_iota(jnp.int32, (8, TILE), 1)
    sub = lax.broadcasted_iota(jnp.int32, (8, TILE), 0)
    A = [a[8 * g : 8 * g + 8, :] for g in range(groups)]
    E = [jnp.where(lane == sub + 8 * g, 1.0, 0.0).astype(F32) for g in range(groups)]

    def wide(v):
        return jnp.broadcast_to(v, (8, TILE))

    for g0 in range(groups):
        j = 8 * g0
        piv = {(i, l): wide(A[g0][i : i + 1, j + l : j + l + 1]) for i in range(m) for l in range(i, m)}
        R = [wide(A[g0][i : i + 1, :]) for i in range(m)]
        RE = [wide(E[g0][i : i + 1, :]) for i in range(m)]
        f, inv = {}, []
        for i in range(m):
            inv.append(1.0 / piv[i, i])
            for l in range(i + 1, m):
                f[i, l] = piv[i, l] * inv[i]
            for l in range(i + 1, m):
                for q in range(l, m):
                    piv[l, q] = piv[l, q] - (piv[i, l] * piv[i, q]) * inv[i]
                R[l] = R[l] - f[i, l] * R[i]
                RE[l] = RE[l] - f[i, l] * RE[i]
        W, WE = [None] * m, [None] * m
        for i in reversed(range(m)):
            W[i], WE[i] = R[i] * inv[i], RE[i] * inv[i]
            for l in range(i + 1, m):
                W[i] = W[i] - f[i, l] * W[l]
                WE[i] = WE[i] - f[i, l] * WE[l]
        for g in range(g0 + 1, groups):
            ag, eg = A[g], E[g]
            for l in reversed(range(m)):
                col = A[g][:, j + l : j + l + 1]
                ag = ag - col * W[l]
                eg = eg - col * WE[l]
            A[g], E[g] = ag, eg
        ag, eg = R[0], RE[0]
        for i in range(1, m):
            ag = jnp.where(sub == i, R[i], ag)
            eg = jnp.where(sub == i, RE[i], eg)
        A[g0], E[g0] = ag, eg
    U, V = [], []
    for g in range(groups):
        diag = jnp.sum(jnp.where(lane == sub + 8 * g, A[g], 0.0), axis=1, keepdims=True)
        rs = lax.rsqrt(diag)
        U.append(jnp.where(lane >= sub + 8 * g, A[g] * rs, 0.0))
        V.append(E[g] * rs)
    return jnp.concatenate(U, axis=0), jnp.concatenate(V, axis=0)


def cholesky(a, other=None, count=None):
    n = a.shape[0]
    tiles = n // TILE
    start = other is not None
    band = 2 * TILE
    more = n > band

    def body(*refs):
        if start:
            count_ref, g_ref, o_ref, *refs = refs
            inv = 1.0 / count_ref[0]
        else:
            g_ref, *refs = refs
        band_ref, v_ref, *refs = refs
        if more:
            rest_ref, *refs = refs
        w, ph, plo, lh, ll = refs

        def load(c, _):
            rows = pl.ds(pl.multiple_of(c * TILE, TILE), TILE)
            w[rows, :] = (g_ref[rows, :] + o_ref[rows, :]) * inv if start else g_ref[rows, :]
            return 0

        lax.fori_loop(0, tiles, load, 0)

        def step(k, _):
            at = pl.ds(pl.multiple_of(k * TILE, TILE), TILE)
            U, V = factor_tile(w[at, at])
            v_ref[at, :] = V
            vs = split(V)
            panel = dot3(nn, vs, split(w[at, :]))
            ph[...], plo[...] = split(panel)
            left = dot3(nt, split(w[:, at]), vs)
            lh[...], ll[...] = split(left)
            band_ref[at, :] = panel
            band_ref[at, at] = U

            def update(j, _):
                rows = pl.ds(pl.multiple_of(j * TILE, TILE), TILE)
                w[rows, :] -= dot3(nn, (lh[rows, :], ll[rows, :]), (ph[...], plo[...]))
                return 0

            lax.fori_loop(k + 1, tiles, update, 0)
            return 0

        lax.fori_loop(0, 2, step, 0)
        if more:

            def keep(c, _):
                rows = pl.ds(pl.multiple_of(c * TILE, TILE), TILE)
                rest_ref[rows, :] = w[pl.ds(pl.multiple_of(band + c * TILE, TILE), TILE), band:]
                return 0

            lax.fori_loop(0, tiles - 2, keep, 0)

    vm = pl.BlockSpec(memory_space=pltpu.VMEM)
    sm = pl.BlockSpec(memory_space=pltpu.SMEM)
    outs = [(band, n), (band, TILE)] + ([(n - band, n - band)] if more else [])
    return pl.pallas_call(
        body,
        out_shape=[jax.ShapeDtypeStruct(o, F32) for o in outs],
        in_specs=[sm, vm, vm] if start else [vm],
        out_specs=[vm] * len(outs),
        scratch_shapes=[pltpu.VMEM((n, n), F32)] + [pltpu.VMEM((TILE, n), BF16)] * 2 + [pltpu.VMEM((n, TILE), BF16)] * 2,
        compiler_params=params(24),
        cost_estimate=pl.CostEstimate(flops=1_000_000, bytes_accessed=1024, transcendentals=0),
        name="cholesky",
    )(*((count, a, other) if start else (a,)))


def finish(scalars, count, hk, hr, pk, pr, pc, pcr, bands, inverses):
    two, half = 2 * TILE, 512
    pairs = PANEL // two

    def body(sc, count_ref, hk_ref, hr_ref, pk_ref, pr_ref, pc_ref, pcr_ref, *refs):
        u_refs, v_refs, refs = refs[:pairs], refs[pairs : 2 * pairs], refs[2 * pairs :]
        out_ref, uh, ul, vh, vl, xh, xl, b = refs
        i = pl.program_id(0)
        inv = 1.0 / count_ref[0]

        @pl.when(i == 0)
        def _():
            for k in range(pairs):
                for c in (0, TILE):
                    rows, cols = slice(k * two + c, k * two + c + TILE), slice(k * two, PANEL)
                    uh[rows, cols], ul[rows, cols] = split(u_refs[k][c : c + TILE, :])

            for k in range(pairs):
                top, low = slice(k * two, k * two + TILE), slice(k * two + TILE, (k + 1) * two)
                v1, v2 = split(v_refs[k][:TILE, :]), split(v_refs[k][TILE:, :])
                cross = dot3(nn, split(u_refs[k][:TILE, TILE:two].T), v1)
                cross = -dot3(nn, v2, split(cross))
                vh[top, :TILE], vl[top, :TILE] = v1
                vh[low, TILE:], vl[low, TILE:] = v2
                vh[top, TILE:] = jnp.zeros((TILE, TILE), BF16)
                vl[top, TILE:] = jnp.zeros((TILE, TILE), BF16)
                vh[low, :TILE], vl[low, :TILE] = split(cross)

            def load(c, _):
                rows = pl.ds(pl.multiple_of(c * TILE, TILE), TILE)
                b[rows, :] = (pk_ref[rows, :] + pr_ref[rows, :]) * inv
                return 0

            lax.fori_loop(0, half // TILE, load, 0)

        @pl.when(i > 0)
        def _():
            def load(c, _):
                rows = pl.ds(pl.multiple_of(c * TILE, TILE), TILE)
                b[rows, :] = (pc_ref[rows, :] + pcr_ref[rows, :]) * inv
                return 0

            lax.fori_loop(0, half // TILE, load, 0)

        to = pl.ds(pl.multiple_of(jnp.minimum(i, 1) * half, half), half)
        for k in range(pairs):
            here, after = slice(k * two, (k + 1) * two), slice((k + 1) * two, PANEL)
            x = dot3(nt, split(b[:, here]), (vh[here, :], vl[here, :]))
            xs = split(x)
            b[:, here] = x
            xh[to, here], xl[to, here] = xs
            if k + 1 < pairs:
                b[:, after] -= dot3(nn, xs, (uh[here, after], ul[here, after]))

        @pl.when(i == 0)
        def _():
            def left(c, _):
                rows = pl.ds(pl.multiple_of(c * TILE, TILE), TILE)
                own = b[rows, pl.ds(pl.multiple_of(sc[1] * TILE, TILE), TILE)]
                row = (c * 16 + sc[0]) * TILE + lax.broadcasted_iota(jnp.int32, (TILE, TILE), 0)
                col = sc[1] * TILE + lax.broadcasted_iota(jnp.int32, (TILE, TILE), 1)
                out_ref[rows, :TILE] = jnp.where(row >= col, own, 0.0)
                return 0

            lax.fori_loop(0, half // TILE, left, 0)

        def trail(c, first):
            rows = pl.ds(pl.multiple_of(c * two, two), two)
            cols = slice(half + first, 2 * half)
            up = dot3(nt, (xh[rows, :], xl[rows, :]), (xh[cols, :], xl[cols, :]))
            out_ref[rows, first:] = (hk_ref[rows, first:] + hr_ref[rows, first:]) * inv - up

        @pl.when(i == 1)
        def _():
            lax.fori_loop(0, half // two, lambda c, _: (trail(c, TILE), 0)[1], 0)

        @pl.when(i == 2)
        def _():
            lax.fori_loop(0, half // two, lambda c, _: (trail(c, 0), 0)[1], 0)

    sm = pl.BlockSpec(memory_space=pltpu.SMEM)
    later = lambda i: jnp.maximum(i - 1, 0)
    wide = pl.BlockSpec((half, half), lambda i: (0, later(i)))
    tall = pl.BlockSpec((half, PANEL), lambda i: (later(i), 0))
    whole = lambda n, m: pl.BlockSpec((n, m), lambda i: (0, 0))
    return pl.pallas_call(
        body,
        grid=(3,),
        out_shape=jax.ShapeDtypeStruct((half, 1024), F32),
        in_specs=[sm, sm, wide, wide, whole(half, PANEL), whole(half, PANEL), tall, tall]
        + [whole(two, PANEL - k * two) for k in range(pairs)]
        + [whole(two, TILE)] * pairs,
        out_specs=wide,
        scratch_shapes=[pltpu.VMEM((PANEL, PANEL), BF16)] * 2
        + [pltpu.VMEM((PANEL, two), BF16)] * 2
        + [pltpu.VMEM((2 * half, PANEL), BF16)] * 2
        + [pltpu.VMEM((half, PANEL), F32)],
        compiler_params=params(62),
        cost_estimate=pl.CostEstimate(flops=16_000_000_000, bytes_accessed=28 * MIB, transcendentals=0),
        name="finish",
    )(scalars, count, hk, hr, pk, pr, pc, pcr, *bands, *inverses)


def shards_of(token_ids, column_order, residual, attn_out, out_proj, norm_gain):
    s = lax.axis_index("section").astype(jnp.int32)
    t = lax.axis_index("tensor").astype(jnp.int32)
    y, x = t // 4, t % 4
    z, yl, core = s // 4, (s // 2) % 2, s % 2

    def origin(dx, dy):
        return (y ^ dy) * 4 + (x - dx) % 4

    origins = jnp.stack([origin(*k) for k in KEYS])
    early = jnp.stack([origin(*KEYS[i]) for i in (0, 1, 2, 4)])
    middle = jnp.stack([origin(*KEYS[i]) for i in (3, 5)])
    late = jnp.stack([origin(*KEYS[i]) for i in (6, 7)])

    g_hi = lax.reduce_precision(norm_gain, 8, 7)
    g_mid = lax.reduce_precision(norm_gain - g_hi, 8, 7)
    g_lo = norm_gain - g_hi - g_mid
    parts = jnp.stack([g_hi, g_mid, g_lo]).astype(BF16)
    ext = jnp.concatenate([parts, jnp.zeros((EXT - 3, 1024), BF16)], axis=0)
    own = jnp.concatenate([attn_out, ext], axis=0)

    one = first(own, shift_t)
    two = second(*one, shift_t, 144)
    acc = project([[own], [one[0]], [one[1]], [one[2]]], out_proj, early)
    *two, acc = tie(*two, acc)
    three = third(two[0], two[1], shift_t, 144)
    acc = project([[two[0]], [two[1]]], out_proj, middle, acc)
    *three, acc = tie(*three, acc)
    a = listed(own, one, two, three)
    hidden = project(a[6:], out_proj, late, acc, residual)
    gains = [(pieces[-1], pieces[-1].shape[0] // EXT - 1) for pieces in a]

    tiles = [t]
    for dy in (1, 0):
        for dz in range(4):
            group = ((z + dz) % 4) * 2 + (yl ^ dy)
            tiles.append(16 * x + 2 * group + y)
    tiles += [j * 8 + t for j in range(8)]
    index = jnp.take(column_order.reshape(64, TILE), jnp.stack(tiles), axis=0).reshape(-1, 1)
    kept = (token_ids != 0).astype(F32).reshape(1, TOK)

    one = first(hidden, shift_t)
    rows_of = jnp.concatenate([index.reshape(-1, TILE), jnp.zeros((7, TILE), jnp.int32)], axis=0)
    gain = pick_gains(gains, origins, rows_of)
    *one, gain = tie(*one, gain)
    two = second(*one, shift_t, 512)
    carry = pick([[hidden], [one[0]], [one[1]], [one[2]]], early, index)
    *two, c0, c1 = tie(*two, *carry)
    three = third(two[0], two[1], shift_t, 512)
    carry = pick([[two[0]], [two[1]]], middle, index, (c0, c1))
    *three, c0, c1 = tie(*three, *carry)
    h = listed(hidden, one, two, three)
    message, rows0, cols = pick(h[6:], late, index, (c0, c1), gain, kept)

    same_core = [[c + 2 * g for g in range(8)] for c in range(2)]
    theirs = shift_s(message, 0, 1)
    head = TILE + EXT

    def part(msg, rows, dz):
        return jnp.concatenate([msg[:head], rows[dz * TILE : (dz + 1) * TILE]], axis=0)

    sent = [jnp.stack([part(message, rows0, dz), part(theirs, theirs[head:], dz)]) for dz in range(4)]
    got = [sent[0]] + [shift_s(sent[dz], dz, 0) for dz in (1, 2, 3)]
    pan8 = jnp.concatenate([g[:, :TILE] for g in got], axis=0)
    rows8 = jnp.concatenate([g[:, head:] for g in got], axis=0)
    kept_here = sum(jnp.sum(g[:, TILE : TILE + 1].astype(F32)) for g in got)
    count = (kept_here + shift_s(kept_here.reshape(1, 1), 0, 0, 1)[0, 0]).reshape(1)

    p1 = first(pan8, shift_t)
    p2 = second(*p1, shift_t, 4)
    p2, rows8, cols, count = tie(p2, rows8, cols, count)
    cols_all = lax.all_gather(cols, "section", axis=0, axis_index_groups=same_core)
    p3 = third(p2[0], p2[1], shift_t, 4)
    p3, rows8 = tie(p3, rows8)
    r1 = first(rows8, shift_t)
    pan_all, gram = panel_gram(listed(pan8, p1, p2, p3), origins)

    gram_other = shift_s(gram, 0, 0, 1)
    u0, v0, u = cholesky(gram, gram_other, count)
    u, r1 = tie(u, r1)
    r2 = second(*r1, shift_t, 4)
    u1, v1, u = cholesky(u)
    u, r2 = tie(u, r2)
    r3 = third(r2[0], r2[1], shift_t, 4)
    u2, v2, u = cholesky(u)
    u, r3, cols_all = tie(u, r3, cols_all)
    slots = jnp.stack([((o // 4) ^ core) * 4 + o % 4 for o in [origin(*k) for k in KEYS]])
    chunks = jnp.stack([((z - dz) % 4) * 2 + (yl ^ dy) for dz in range(4) for dy in range(2)])
    hk, hs, pk, ps, pc = block_gram(listed(rows8, r1, r2, r3), cols_all, pan_all, slots, chunks)
    u, hs, ps, pc = tie(u, hs, ps, pc)
    hr, pr, pcr = [shift_s(w, 0, 0, 1) for w in (hs, ps, pc)]
    u3, v3 = cholesky(u)
    scalars = jnp.stack([s, t])
    return finish(scalars, count, hk, hr, pk, pr, pc, pcr, (u0, u1, u2, u3), (v0, v1, v2, v3))


def solution(mesh):
    placed = (
        P("section"),
        P(),
        P("section", "tensor"),
        P("section", "tensor"),
        P(None, "tensor"),
        P("tensor"),
    )
    return jax.shard_map(
        shards_of, mesh=mesh, in_specs=placed, out_specs=P("section", "tensor"), check_vma=False
    )
```

```python
import functools

import jax
import jax.numpy as jnp
from jax import lax
from jax.experimental import pallas as pl
from jax.experimental.pallas import tpu as pltpu
from jax.sharding import PartitionSpec as P

TILE = 128
PANEL = 1024
WIDTH = 8192
TOK = 256
EXT = 16
epsilon = 1e-06
F32 = jnp.float32
BF16 = jnp.bfloat16
KEYS = [(0, 0), (0, 1), (1, 0), (1, 1), (3, 0), (3, 1), (2, 0), (2, 1)]
CHUNK = {(d, f): d * 2 + f for d in range(4) for f in range(2)}
MIB = 1024 * 1024


def params(limit=48):
    return pltpu.CompilerParams(vmem_limit_bytes=limit * MIB)


def shift_t(value, dx, dy):
    pairs = [(t, ((t // 4) ^ dy) * 4 + (t % 4 + dx) % 4) for t in range(8)]
    return lax.ppermute(value, "tensor", pairs)


def shift_s(value, dz, dy, dc=0):
    pairs = [(s, ((s // 4 + dz) % 4) * 4 + ((s % 4) ^ (2 * dy + dc))) for s in range(16)]
    return lax.ppermute(value, "section", pairs)


def tie(*values):
    return lax.optimization_barrier(values)


def first(x, shift):
    return shift(x, 0, 1), shift(x, 1, 0), shift(x, 3, 0)


def second(b, ra, la, shift, half):
    return shift(b, 1, 0), shift(b, 3, 0), shift(ra[:half], 1, 0), shift(la[half:], 3, 0)


def third(rb, lb, shift, half):
    return shift(rb[:half], 1, 0), shift(lb[half:], 3, 0)


def listed(x, one, two, three):
    return [[x], [one[0]], [one[1]], [two[0]], [one[2]], [two[1]], [two[2], two[3]], list(three)]


def flatten(shards):
    arrays, meta = [], []
    for pieces in shards:
        off, entry = 0, []
        for piece in pieces:
            entry.append((len(arrays), off, piece.shape[0]))
            arrays.append(piece)
            off += piece.shape[0]
        meta.append(entry)
    return arrays, meta


def nt(a, b):
    return lax.dot_general(a, b, (((1,), (1,)), ((), ())), preferred_element_type=F32)


def nn(a, b):
    return lax.dot_general(a, b, (((1,), (0,)), ((), ())), preferred_element_type=F32)


def split(a):
    hi = a.astype(BF16)
    return hi, (a - hi.astype(F32)).astype(BF16)


def dot3(op, a, b):
    left = jnp.concatenate([a[0], a[0], a[1]], axis=1)
    right = jnp.concatenate([b[0], b[1], b[0]], axis=0 if op is nn else 1)
    return op(left, right)


def project(shards, out_proj, origins, acc=None, residual=None):
    arrays, meta = flatten(shards)
    n = len(shards)
    final = residual is not None
    cols = out_proj.shape[1]

    def body(*refs):
        _, w_ref, *rest = refs
        pieces, rest = rest[: len(arrays)], rest[len(arrays) :]
        if acc is not None:
            acc_ref, *rest = rest
        if final:
            res_ref, *rest = rest
        out_ref, acc_s = rest
        i = pl.program_id(0)

        @pl.when(i == 0)
        def _():
            acc_s[...] = acc_ref[...] if acc is not None else jnp.zeros_like(acc_s)

        for r in range(n):

            @pl.when(i == r)
            def _(r=r):
                for j, off, size in meta[r]:
                    size = min(size, TOK - off)
                    acc_s[off : off + size, :] += nn(pieces[j][:size, :], w_ref[...])

        @pl.when(i == n - 1)
        def _():
            if final:
                h = (res_ref[...].astype(F32) + acc_s[...]).astype(BF16).astype(F32)
                out_ref[...] = h.T.astype(BF16)
            else:
                out_ref[...] = acc_s[...]

    whole = lambda shape: pl.BlockSpec(shape, lambda i, o: (0,) * len(shape))
    operands = [out_proj, *arrays]
    specs = [pl.BlockSpec((1024, cols), lambda i, o: (o[i], 0))] + [whole(a.shape) for a in arrays]
    if acc is not None:
        operands.append(acc)
        specs.append(whole(acc.shape))
    if final:
        operands.append(residual)
        specs.append(whole(residual.shape))
    shape = (cols, TOK) if final else (TOK, cols)
    return pl.pallas_call(
        body,
        out_shape=jax.ShapeDtypeStruct(shape, BF16 if final else F32),
        grid_spec=pltpu.PrefetchScalarGridSpec(
            num_scalar_prefetch=1,
            grid=(n,),
            in_specs=specs,
            out_specs=whole(shape),
            scratch_shapes=[pltpu.VMEM((TOK, cols), F32)],
        ),
        compiler_params=params(),
        cost_estimate=pl.CostEstimate(flops=2 * TOK * 1024 * cols * n, bytes_accessed=n * 2 * MIB, transcendentals=0),
        name="project",
    )(origins, *operands)


PICKS = 2176
SPLITS = ((0, TILE), (TILE, 512), (TILE + 512, 512), (TILE + 1024, 1024))


def hot_rows(index_ref, start, size, base):
    lane = lax.broadcasted_iota(jnp.int32, (size, 1024), 1)
    return jnp.where(index_ref[pl.ds(start, size), :] - base == lane, 1.0, 0.0).astype(BF16)


def pick_gains(gains, origins, index_rows):
    def body(origin, index_ref, *refs):
        gain_refs, out_ref = refs[:8], refs[8]
        got = [jnp.zeros((8, TILE), F32) for _ in range(3)]
        for r in range(8):
            whole = jnp.sum(gain_refs[r][...].astype(F32), axis=0, keepdims=True)
            for q in range(8):
                row = jnp.broadcast_to(whole[:, q * TILE : (q + 1) * TILE], (8, TILE))
                for i in range(3):
                    idx = index_ref[8 * i : 8 * i + 8, :]
                    here = jnp.take_along_axis(row, idx % TILE, axis=1)
                    got[i] = jnp.where(idx // TILE == origin[r] * 8 + q, here, got[i])
        for c in range(PICKS // TILE):
            if c % 8 == 0:
                column = got[c // 8].T
            out_ref[c * TILE : (c + 1) * TILE, :] = column[:, c % 8 : c % 8 + 1]

    vm = pl.BlockSpec(memory_space=pltpu.VMEM)
    specs = [pl.BlockSpec((EXT, 1024), functools.partial(lambda b, i: (b, 0), b)) for _, b in gains]
    return pl.pallas_call(
        body,
        grid=(1,),
        out_shape=jax.ShapeDtypeStruct((PICKS, 1), F32),
        in_specs=[pl.BlockSpec(memory_space=pltpu.SMEM), vm] + specs,
        out_specs=vm,
        compiler_params=params(),
        cost_estimate=pl.CostEstimate(flops=2_000_000_000, bytes_accessed=1 * MIB, transcendentals=0),
        name="pick_gains",
    )(origins, index_rows, *[g for g, _ in gains])


def pick(shards, origins, index, carry=None, gain=None, kept=None):
    arrays, meta = flatten(shards)
    n = len(shards)
    final = gain is not None

    def body(*refs):
        origin, index_ref, *rest = refs
        pieces, rest = rest[: len(arrays)], rest[len(arrays) :]
        if carry is not None:
            (acc_ref, sq_ref), rest = rest[:2], rest[2:]
        if final:
            (gain_ref, kept_ref), rest = rest[:2], rest[2:]
        outs, table = rest[:-1], rest[-1]
        step = 128
        total = sq_ref[...] if carry is not None else jnp.zeros((8, TOK), F32)
        for r in range(n):
            for j, off, size in meta[r]:

                def add(c, total, j=j, at=r * 1024 + off):
                    from_rows = pl.ds(pl.multiple_of(c * step, step), step)
                    v = pieces[j][from_rows, :]
                    table[pl.ds(pl.multiple_of(at + c * step, step), step), :] = v
                    v = v.astype(F32)
                    return total + jnp.sum((v * v).reshape(step // 8, 8, TOK), axis=0)

                total = lax.fori_loop(0, size // step, add, total)
        if final:
            scale = lax.rsqrt(jnp.sum(total, axis=0, keepdims=True) / WIDTH + epsilon) * kept_ref[...]
        else:
            outs[1][...] = total

        def value(start, size):
            got = jnp.zeros((size, TOK), F32)
            if carry is not None:
                got = acc_ref[pl.ds(start, size), :].astype(F32)
            for r in range(n):
                got += nn(hot_rows(index_ref, start, size, origin[r] * 1024), table[r * 1024 : (r + 1) * 1024, :])
            if final:
                got = got * scale * gain_ref[pl.ds(start, size), :]
            return got.astype(BF16)

        def fill(ref, base, to, rows, block):
            def one(c, _):
                at = pl.multiple_of(c * block, block)
                ref[pl.ds(to + at, block), :] = value(pl.multiple_of(base + at, TILE), block)
                return 0

            lax.fori_loop(0, rows // block, one, 0)

        places = ((0, 0), (0, TILE + EXT), (1, 0), (2, 0)) if final else tuple((0, base) for base, _ in SPLITS)
        for (base, rows), (o, to) in zip(SPLITS, places):
            fill(outs[o], base, to, rows, min(rows, 256))
        if final:
            row0 = lax.broadcasted_iota(jnp.int32, (EXT, TOK), 0) == 0
            outs[0][TILE : TILE + EXT, :] = jnp.where(row0, kept_ref[...], 0.0).astype(BF16)

    vm = pl.BlockSpec(memory_space=pltpu.VMEM)
    operands = [origins, index, *arrays]
    if carry is not None:
        operands += list(carry)
    if final:
        operands += [gain, kept]
        outs = [jax.ShapeDtypeStruct(s, BF16) for s in ((TILE + EXT + 512, TOK), (512, TOK), (1024, TOK))]
    else:
        outs = [jax.ShapeDtypeStruct((PICKS, TOK), BF16), jax.ShapeDtypeStruct((8, TOK), F32)]
    return pl.pallas_call(
        body,
        out_shape=outs,
        in_specs=[pl.BlockSpec(memory_space=pltpu.SMEM)] + [vm] * (len(operands) - 1),
        out_specs=[vm] * len(outs),
        scratch_shapes=[pltpu.VMEM((1024 * n, TOK), BF16)],
        compiler_params=params(),
        cost_estimate=pl.CostEstimate(flops=2 * PICKS * 1024 * n * TOK, bytes_accessed=4 * MIB, transcendentals=0),
        name="pick",
    )(*operands)


def place(pieces, meta, slot, scratch):
    for r in range(8):
        row = pl.multiple_of(slot[r] * TILE, TILE)
        for j, off, size in meta[r]:
            for c in range(size):
                scratch[pl.ds(row, TILE), (off + c) * TOK : (off + c + 1) * TOK] = pieces[j][c]


def panel_gram(shards, slots):
    arrays, meta = flatten(shards)

    def body(slot, *refs):
        pieces, (pan_ref, gram_ref) = refs[: len(arrays)], refs[len(arrays) :]
        place(pieces, meta, slot, pan_ref)

        def one(c, _):
            rows = pl.ds(pl.multiple_of(c * 256, 256), 256)
            gram_ref[rows, :] = nt(pan_ref[rows, :], pan_ref[...])
            return 0

        lax.fori_loop(0, 4, one, 0)

    vm = pl.BlockSpec(memory_space=pltpu.VMEM)
    return pl.pallas_call(
        body,
        out_shape=[jax.ShapeDtypeStruct((PANEL, 2048), BF16), jax.ShapeDtypeStruct((PANEL, PANEL), F32)],
        in_specs=[pl.BlockSpec(memory_space=pltpu.SMEM)] + [vm] * len(arrays),
        out_specs=[vm] * 2,
        compiler_params=params(),
        cost_estimate=pl.CostEstimate(flops=1_000_000, bytes_accessed=1024, transcendentals=0),
        name="panel_gram",
    )(slots, *arrays)


def block_gram(row_shards, cols_all, pan, slots, chunks):
    row_arrays, row_meta = flatten(row_shards)
    steps = 4

    def body(slot, chunk, pan_ref, col_ref, *refs):
        rp, refs = refs[: len(row_arrays)], refs[len(row_arrays) :]
        hk_ref, hs_ref, pk_ref, ps_ref, pc_ref, rows, cols = refs
        i = pl.program_id(0)

        @pl.when(i == 0)
        def _():
            place(rp, row_meta, slot, rows)
            for c in range(8):
                cols[:, c * TOK : (c + 1) * TOK] = col_ref[chunk[c]]

        at = pl.ds(pl.multiple_of(i * TILE, TILE), TILE)
        to = pl.ds(pl.multiple_of(512 + i * TILE, TILE), TILE)
        both = jnp.concatenate([rows[at, :], rows[to, :]], axis=0)
        p = nt(both, pan_ref[...])
        pk_ref[...], ps_ref[...] = p[:TILE], p[TILE:]
        h = nt(both, cols[...])
        hk_ref[...], hs_ref[...] = h[:TILE], h[TILE:]
        pc_ref[...] = nt(cols[pl.ds(pl.multiple_of(i * 256, 256), 256), :], pan_ref[...])

    vm = pl.BlockSpec(memory_space=pltpu.VMEM)
    outs = [(512, 1024)] * 4 + [(1024, PANEL)]
    return pl.pallas_call(
        body,
        grid=(steps,),
        out_shape=[jax.ShapeDtypeStruct(s, F32) for s in outs],
        in_specs=[pl.BlockSpec(memory_space=pltpu.SMEM)] * 2 + [vm, vm] + [vm] * len(row_arrays),
        out_specs=[pl.BlockSpec((n // steps, 1024), lambda i: (i, 0)) for n, _ in outs],
        scratch_shapes=[pltpu.VMEM((1024, 2048), BF16)] * 2,
        compiler_params=params(62),
        cost_estimate=pl.CostEstimate(flops=6 * 1024 * 1024 * 2048, bytes_accessed=24 * MIB, transcendentals=0),
        name="block_gram",
    )(slots, chunks, pan, cols_all, *row_arrays)


def factor_tile(a):
    groups, m = TILE // 8, 8
    lane = lax.broadcasted_iota(jnp.int32, (8, TILE), 1)
    sub = lax.broadcasted_iota(jnp.int32, (8, TILE), 0)
    A = [a[8 * g : 8 * g + 8, :] for g in range(groups)]
    E = [jnp.where(lane == sub + 8 * g, 1.0, 0.0).astype(F32) for g in range(groups)]

    def wide(v):
        return jnp.broadcast_to(v, (8, TILE))

    for g0 in range(groups):
        j = 8 * g0
        piv = {(i, l): wide(A[g0][i : i + 1, j + l : j + l + 1]) for i in range(m) for l in range(i, m)}
        R = [wide(A[g0][i : i + 1, :]) for i in range(m)]
        RE = [wide(E[g0][i : i + 1, :]) for i in range(m)]
        f, inv = {}, []
        for i in range(m):
            inv.append(1.0 / piv[i, i])
            for l in range(i + 1, m):
                f[i, l] = piv[i, l] * inv[i]
            for l in range(i + 1, m):
                for q in range(l, m):
                    piv[l, q] = piv[l, q] - (piv[i, l] * piv[i, q]) * inv[i]
                R[l] = R[l] - f[i, l] * R[i]
                RE[l] = RE[l] - f[i, l] * RE[i]
        W, WE = [None] * m, [None] * m
        for i in reversed(range(m)):
            W[i], WE[i] = R[i] * inv[i], RE[i] * inv[i]
            for l in range(i + 1, m):
                W[i] = W[i] - f[i, l] * W[l]
                WE[i] = WE[i] - f[i, l] * WE[l]
        for g in range(g0 + 1, groups):
            ag, eg = A[g], E[g]
            for l in reversed(range(m)):
                col = A[g][:, j + l : j + l + 1]
                ag = ag - col * W[l]
                eg = eg - col * WE[l]
            A[g], E[g] = ag, eg
        ag, eg = R[0], RE[0]
        for i in range(1, m):
            ag = jnp.where(sub == i, R[i], ag)
            eg = jnp.where(sub == i, RE[i], eg)
        A[g0], E[g0] = ag, eg
    U, V = [], []
    for g in range(groups):
        diag = jnp.sum(jnp.where(lane == sub + 8 * g, A[g], 0.0), axis=1, keepdims=True)
        rs = lax.rsqrt(diag)
        U.append(jnp.where(lane >= sub + 8 * g, A[g] * rs, 0.0))
        V.append(E[g] * rs)
    return jnp.concatenate(U, axis=0), jnp.concatenate(V, axis=0)


def cholesky(a, other=None, count=None):
    n = a.shape[0]
    tiles = n // TILE
    start = other is not None
    band = 2 * TILE
    more = n > band

    def body(*refs):
        if start:
            count_ref, g_ref, o_ref, *refs = refs
            inv = 1.0 / count_ref[0]
        else:
            g_ref, *refs = refs
        band_ref, v_ref, *refs = refs
        if more:
            rest_ref, *refs = refs
        w, ph, plo, lh, ll = refs

        def load(c, _):
            rows = pl.ds(pl.multiple_of(c * TILE, TILE), TILE)
            w[rows, :] = (g_ref[rows, :] + o_ref[rows, :]) * inv if start else g_ref[rows, :]
            return 0

        lax.fori_loop(0, tiles, load, 0)

        def step(k, _):
            at = pl.ds(pl.multiple_of(k * TILE, TILE), TILE)
            U, V = factor_tile(w[at, at])
            v_ref[at, :] = V
            vs = split(V)
            panel = dot3(nn, vs, split(w[at, :]))
            ph[...], plo[...] = split(panel)
            left = dot3(nt, split(w[:, at]), vs)
            lh[...], ll[...] = split(left)
            band_ref[at, :] = panel
            band_ref[at, at] = U

            def update(j, _):
                rows = pl.ds(pl.multiple_of(j * TILE, TILE), TILE)
                w[rows, :] -= dot3(nn, (lh[rows, :], ll[rows, :]), (ph[...], plo[...]))
                return 0

            lax.fori_loop(k + 1, tiles, update, 0)
            return 0

        lax.fori_loop(0, 2, step, 0)
        if more:

            def keep(c, _):
                rows = pl.ds(pl.multiple_of(c * TILE, TILE), TILE)
                rest_ref[rows, :] = w[pl.ds(pl.multiple_of(band + c * TILE, TILE), TILE), band:]
                return 0

            lax.fori_loop(0, tiles - 2, keep, 0)

    vm = pl.BlockSpec(memory_space=pltpu.VMEM)
    sm = pl.BlockSpec(memory_space=pltpu.SMEM)
    outs = [(band, n), (band, TILE)] + ([(n - band, n - band)] if more else [])
    return pl.pallas_call(
        body,
        out_shape=[jax.ShapeDtypeStruct(o, F32) for o in outs],
        in_specs=[sm, vm, vm] if start else [vm],
        out_specs=[vm] * len(outs),
        scratch_shapes=[pltpu.VMEM((n, n), F32)] + [pltpu.VMEM((TILE, n), BF16)] * 2 + [pltpu.VMEM((n, TILE), BF16)] * 2,
        compiler_params=params(24),
        cost_estimate=pl.CostEstimate(flops=1_000_000, bytes_accessed=1024, transcendentals=0),
        name="cholesky",
    )(*((count, a, other) if start else (a,)))


def finish(scalars, count, hk, hr, pk, pr, pc, pcr, bands, inverses):
    two, half = 2 * TILE, 512
    pairs = PANEL // two

    def body(sc, count_ref, hk_ref, hr_ref, pk_ref, pr_ref, pc_ref, pcr_ref, *refs):
        u_refs, v_refs, refs = refs[:pairs], refs[pairs : 2 * pairs], refs[2 * pairs :]
        out_ref, uh, ul, vh, vl, xh, xl, b = refs
        i = pl.program_id(0)
        inv = 1.0 / count_ref[0]

        @pl.when(i == 0)
        def _():
            for k in range(pairs):
                for c in (0, TILE):
                    rows, cols = slice(k * two + c, k * two + c + TILE), slice(k * two, PANEL)
                    uh[rows, cols], ul[rows, cols] = split(u_refs[k][c : c + TILE, :])

            for k in range(pairs):
                top, low = slice(k * two, k * two + TILE), slice(k * two + TILE, (k + 1) * two)
                v1, v2 = split(v_refs[k][:TILE, :]), split(v_refs[k][TILE:, :])
                cross = dot3(nn, split(u_refs[k][:TILE, TILE:two].T), v1)
                cross = -dot3(nn, v2, split(cross))
                vh[top, :TILE], vl[top, :TILE] = v1
                vh[low, TILE:], vl[low, TILE:] = v2
                vh[top, TILE:] = jnp.zeros((TILE, TILE), BF16)
                vl[top, TILE:] = jnp.zeros((TILE, TILE), BF16)
                vh[low, :TILE], vl[low, :TILE] = split(cross)

            def load(c, _):
                rows = pl.ds(pl.multiple_of(c * TILE, TILE), TILE)
                b[rows, :] = (pk_ref[rows, :] + pr_ref[rows, :]) * inv
                return 0

            lax.fori_loop(0, half // TILE, load, 0)

        @pl.when(i > 0)
        def _():
            def load(c, _):
                rows = pl.ds(pl.multiple_of(c * TILE, TILE), TILE)
                b[rows, :] = (pc_ref[rows, :] + pcr_ref[rows, :]) * inv
                return 0

            lax.fori_loop(0, half // TILE, load, 0)

        to = pl.ds(pl.multiple_of(jnp.minimum(i, 1) * half, half), half)
        for k in range(pairs):
            here, after = slice(k * two, (k + 1) * two), slice((k + 1) * two, PANEL)
            x = dot3(nt, split(b[:, here]), (vh[here, :], vl[here, :]))
            xs = split(x)
            b[:, here] = x
            xh[to, here], xl[to, here] = xs
            if k + 1 < pairs:
                b[:, after] -= dot3(nn, xs, (uh[here, after], ul[here, after]))

        @pl.when(i == 0)
        def _():
            def left(c, _):
                rows = pl.ds(pl.multiple_of(c * TILE, TILE), TILE)
                own = b[rows, pl.ds(pl.multiple_of(sc[1] * TILE, TILE), TILE)]
                row = (c * 16 + sc[0]) * TILE + lax.broadcasted_iota(jnp.int32, (TILE, TILE), 0)
                col = sc[1] * TILE + lax.broadcasted_iota(jnp.int32, (TILE, TILE), 1)
                out_ref[rows, :TILE] = jnp.where(row >= col, own, 0.0)
                return 0

            lax.fori_loop(0, half // TILE, left, 0)

        def trail(c, first):
            rows = pl.ds(pl.multiple_of(c * two, two), two)
            cols = slice(half + first, 2 * half)
            up = dot3(nt, (xh[rows, :], xl[rows, :]), (xh[cols, :], xl[cols, :]))
            out_ref[rows, first:] = (hk_ref[rows, first:] + hr_ref[rows, first:]) * inv - up

        @pl.when(i == 1)
        def _():
            lax.fori_loop(0, half // two, lambda c, _: (trail(c, TILE), 0)[1], 0)

        @pl.when(i == 2)
        def _():
            lax.fori_loop(0, half // two, lambda c, _: (trail(c, 0), 0)[1], 0)

    sm = pl.BlockSpec(memory_space=pltpu.SMEM)
    later = lambda i: jnp.maximum(i - 1, 0)
    wide = pl.BlockSpec((half, half), lambda i: (0, later(i)))
    tall = pl.BlockSpec((half, PANEL), lambda i: (later(i), 0))
    whole = lambda n, m: pl.BlockSpec((n, m), lambda i: (0, 0))
    return pl.pallas_call(
        body,
        grid=(3,),
        out_shape=jax.ShapeDtypeStruct((half, 1024), F32),
        in_specs=[sm, sm, wide, wide, whole(half, PANEL), whole(half, PANEL), tall, tall]
        + [whole(two, PANEL - k * two) for k in range(pairs)]
        + [whole(two, TILE)] * pairs,
        out_specs=wide,
        scratch_shapes=[pltpu.VMEM((PANEL, PANEL), BF16)] * 2
        + [pltpu.VMEM((PANEL, two), BF16)] * 2
        + [pltpu.VMEM((2 * half, PANEL), BF16)] * 2
        + [pltpu.VMEM((half, PANEL), F32)],
        compiler_params=params(62),
        cost_estimate=pl.CostEstimate(flops=16_000_000_000, bytes_accessed=28 * MIB, transcendentals=0),
        name="finish",
    )(scalars, count, hk, hr, pk, pr, pc, pcr, *bands, *inverses)


def shards_of(token_ids, column_order, residual, attn_out, out_proj, norm_gain):
    s = lax.axis_index("section").astype(jnp.int32)
    t = lax.axis_index("tensor").astype(jnp.int32)
    y, x = t // 4, t % 4
    z, yl, core = s // 4, (s // 2) % 2, s % 2

    def origin(dx, dy):
        return (y ^ dy) * 4 + (x - dx) % 4

    origins = jnp.stack([origin(*k) for k in KEYS])
    early = jnp.stack([origin(*KEYS[i]) for i in (0, 1, 2, 4)])
    middle = jnp.stack([origin(*KEYS[i]) for i in (3, 5)])
    late = jnp.stack([origin(*KEYS[i]) for i in (6, 7)])

    g_hi = lax.reduce_precision(norm_gain, 8, 7)
    g_mid = lax.reduce_precision(norm_gain - g_hi, 8, 7)
    g_lo = norm_gain - g_hi - g_mid
    parts = jnp.stack([g_hi, g_mid, g_lo]).astype(BF16)
    ext = jnp.concatenate([parts, jnp.zeros((EXT - 3, 1024), BF16)], axis=0)
    own = jnp.concatenate([attn_out, ext], axis=0)

    one = first(own, shift_t)
    two = second(*one, shift_t, 144)
    acc = project([[own], [one[0]], [one[1]], [one[2]]], out_proj, early)
    *two, acc = tie(*two, acc)
    three = third(two[0], two[1], shift_t, 144)
    acc = project([[two[0]], [two[1]]], out_proj, middle, acc)
    *three, acc = tie(*three, acc)
    a = listed(own, one, two, three)
    hidden = project(a[6:], out_proj, late, acc, residual)
    gains = [(pieces[-1], pieces[-1].shape[0] // EXT - 1) for pieces in a]

    tiles = [t]
    for dy in (1, 0):
        for dz in range(4):
            group = ((z + dz) % 4) * 2 + (yl ^ dy)
            tiles.append(16 * x + 2 * group + y)
    tiles += [j * 8 + t for j in range(8)]
    index = jnp.take(column_order.reshape(64, TILE), jnp.stack(tiles), axis=0).reshape(-1, 1)
    kept = (token_ids != 0).astype(F32).reshape(1, TOK)

    one = first(hidden, shift_t)
    rows_of = jnp.concatenate([index.reshape(-1, TILE), jnp.zeros((7, TILE), jnp.int32)], axis=0)
    gain = pick_gains(gains, origins, rows_of)
    *one, gain = tie(*one, gain)
    two = second(*one, shift_t, 512)
    carry = pick([[hidden], [one[0]], [one[1]], [one[2]]], early, index)
    *two, c0, c1 = tie(*two, *carry)
    three = third(two[0], two[1], shift_t, 512)
    carry = pick([[two[0]], [two[1]]], middle, index, (c0, c1))
    *three, c0, c1 = tie(*three, *carry)
    h = listed(hidden, one, two, three)
    message, rows0, cols = pick(h[6:], late, index, (c0, c1), gain, kept)

    same_core = [[c + 2 * g for g in range(8)] for c in range(2)]
    theirs = shift_s(message, 0, 1)
    head = TILE + EXT

    def part(msg, rows, dz):
        return jnp.concatenate([msg[:head], rows[dz * TILE : (dz + 1) * TILE]], axis=0)

    sent = [jnp.stack([part(message, rows0, dz), part(theirs, theirs[head:], dz)]) for dz in range(4)]
    got = [sent[0]] + [shift_s(sent[dz], dz, 0) for dz in (1, 2, 3)]
    pan8 = jnp.concatenate([g[:, :TILE] for g in got], axis=0)
    rows8 = jnp.concatenate([g[:, head:] for g in got], axis=0)
    kept_here = sum(jnp.sum(g[:, TILE : TILE + 1].astype(F32)) for g in got)
    count = (kept_here + shift_s(kept_here.reshape(1, 1), 0, 0, 1)[0, 0]).reshape(1)

    p1 = first(pan8, shift_t)
    p2 = second(*p1, shift_t, 4)
    p2, cols = tie(p2, cols)
    cols_all = lax.all_gather(cols, "section", axis=0, axis_index_groups=same_core)
    p3 = third(p2[0], p2[1], shift_t, 4)
    p3, rows8, count = tie(p3, rows8, count)
    r1 = first(rows8, shift_t)
    pan_all, gram = panel_gram(listed(pan8, p1, p2, p3), origins)

    gram_other = shift_s(gram, 0, 0, 1)
    u0, v0, u = cholesky(gram, gram_other, count)
    u, r1 = tie(u, r1)
    r2 = second(*r1, shift_t, 4)
    u1, v1, u = cholesky(u)
    u, r2 = tie(u, r2)
    r3 = third(r2[0], r2[1], shift_t, 4)
    u2, v2, u = cholesky(u)
    u, r3, cols_all = tie(u, r3, cols_all)
    slots = jnp.stack([((o // 4) ^ core) * 4 + o % 4 for o in [origin(*k) for k in KEYS]])
    chunks = jnp.stack([((z - dz) % 4) * 2 + (yl ^ dy) for dz in range(4) for dy in range(2)])
    hk, hs, pk, ps, pc = block_gram(listed(rows8, r1, r2, r3), cols_all, pan_all, slots, chunks)
    u, hs, ps, pc = tie(u, hs, ps, pc)
    hr, pr, pcr = [shift_s(w, 0, 0, 1) for w in (hs, ps, pc)]
    u3, v3 = cholesky(u)
    scalars = jnp.stack([s, t])
    return finish(scalars, count, hk, hr, pk, pr, pc, pcr, (u0, u1, u2, u3), (v0, v1, v2, v3))


def solution(mesh):
    placed = (
        P("section"),
        P(),
        P("section", "tensor"),
        P("section", "tensor"),
        P(None, "tensor"),
        P("tensor"),
    )
    return jax.shard_map(
        shards_of, mesh=mesh, in_specs=placed, out_specs=P("section", "tensor"), check_vma=False
    )
```

```python
import functools

import jax
import jax.numpy as jnp
from jax import lax
from jax.experimental import pallas as pl
from jax.experimental.pallas import tpu as pltpu
from jax.sharding import PartitionSpec as P

TILE = 128
PANEL = 1024
WIDTH = 8192
TOK = 256
EXT = 16
epsilon = 1e-06
F32 = jnp.float32
BF16 = jnp.bfloat16
KEYS = [(0, 0), (0, 1), (1, 0), (1, 1), (3, 0), (3, 1), (2, 0), (2, 1)]
CHUNK = {(d, f): d * 2 + f for d in range(4) for f in range(2)}
MIB = 1024 * 1024


def params(limit=48):
    return pltpu.CompilerParams(vmem_limit_bytes=limit * MIB)


def shift_t(value, dx, dy):
    pairs = [(t, ((t // 4) ^ dy) * 4 + (t % 4 + dx) % 4) for t in range(8)]
    return lax.ppermute(value, "tensor", pairs)


def shift_s(value, dz, dy, dc=0):
    pairs = [(s, ((s // 4 + dz) % 4) * 4 + ((s % 4) ^ (2 * dy + dc))) for s in range(16)]
    return lax.ppermute(value, "section", pairs)


def tie(*values):
    return lax.optimization_barrier(values)


def first(x, shift):
    return shift(x, 0, 1), shift(x, 1, 0), shift(x, 3, 0)


def second(b, ra, la, shift, half):
    return shift(b, 1, 0), shift(b, 3, 0), shift(ra[:half], 1, 0), shift(la[half:], 3, 0)


def third(rb, lb, shift, half):
    return shift(rb[:half], 1, 0), shift(lb[half:], 3, 0)


def listed(x, one, two, three):
    return [[x], [one[0]], [one[1]], [two[0]], [one[2]], [two[1]], [two[2], two[3]], list(three)]


def flatten(shards):
    arrays, meta = [], []
    for pieces in shards:
        off, entry = 0, []
        for piece in pieces:
            entry.append((len(arrays), off, piece.shape[0]))
            arrays.append(piece)
            off += piece.shape[0]
        meta.append(entry)
    return arrays, meta


def nt(a, b):
    return lax.dot_general(a, b, (((1,), (1,)), ((), ())), preferred_element_type=F32)


def nn(a, b):
    return lax.dot_general(a, b, (((1,), (0,)), ((), ())), preferred_element_type=F32)


def split(a):
    hi = a.astype(BF16)
    return hi, (a - hi.astype(F32)).astype(BF16)


def dot3(op, a, b):
    left = jnp.concatenate([a[0], a[0], a[1]], axis=1)
    right = jnp.concatenate([b[0], b[1], b[0]], axis=0 if op is nn else 1)
    return op(left, right)


def project(shards, out_proj, origins, acc=None, residual=None):
    arrays, meta = flatten(shards)
    n = len(shards)
    final = residual is not None
    cols = out_proj.shape[1]

    def body(*refs):
        _, w_ref, *rest = refs
        pieces, rest = rest[: len(arrays)], rest[len(arrays) :]
        if acc is not None:
            acc_ref, *rest = rest
        if final:
            res_ref, *rest = rest
        out_ref, acc_s = rest
        i = pl.program_id(0)

        @pl.when(i == 0)
        def _():
            acc_s[...] = acc_ref[...] if acc is not None else jnp.zeros_like(acc_s)

        for r in range(n):

            @pl.when(i == r)
            def _(r=r):
                for j, off, size in meta[r]:
                    size = min(size, TOK - off)
                    acc_s[off : off + size, :] += nn(pieces[j][:size, :], w_ref[...])

        @pl.when(i == n - 1)
        def _():
            if final:
                h = (res_ref[...].astype(F32) + acc_s[...]).astype(BF16).astype(F32)
                out_ref[...] = h.T.astype(BF16)
            else:
                out_ref[...] = acc_s[...]

    whole = lambda shape: pl.BlockSpec(shape, lambda i, o: (0,) * len(shape))
    operands = [out_proj, *arrays]
    specs = [pl.BlockSpec((1024, cols), lambda i, o: (o[i], 0))] + [whole(a.shape) for a in arrays]
    if acc is not None:
        operands.append(acc)
        specs.append(whole(acc.shape))
    if final:
        operands.append(residual)
        specs.append(whole(residual.shape))
    shape = (cols, TOK) if final else (TOK, cols)
    return pl.pallas_call(
        body,
        out_shape=jax.ShapeDtypeStruct(shape, BF16 if final else F32),
        grid_spec=pltpu.PrefetchScalarGridSpec(
            num_scalar_prefetch=1,
            grid=(n,),
            in_specs=specs,
            out_specs=whole(shape),
            scratch_shapes=[pltpu.VMEM((TOK, cols), F32)],
        ),
        compiler_params=params(),
        cost_estimate=pl.CostEstimate(flops=2 * TOK * 1024 * cols * n, bytes_accessed=n * 2 * MIB, transcendentals=0),
        name="project",
    )(origins, *operands)


PICKS = 2176
SPLITS = ((0, TILE), (TILE, 512), (TILE + 512, 512), (TILE + 1024, 1024))


def hot_rows(index_ref, start, size, base):
    lane = lax.broadcasted_iota(jnp.int32, (size, 1024), 1)
    return jnp.where(index_ref[pl.ds(start, size), :] - base == lane, 1.0, 0.0).astype(BF16)


def pick_gains(gains, origins, index_rows):
    def body(origin, index_ref, *refs):
        gain_refs, out_ref = refs[:8], refs[8]
        got = [jnp.zeros((8, TILE), F32) for _ in range(3)]
        for r in range(8):
            whole = jnp.sum(gain_refs[r][...].astype(F32), axis=0, keepdims=True)
            for q in range(8):
                row = jnp.broadcast_to(whole[:, q * TILE : (q + 1) * TILE], (8, TILE))
                for i in range(3):
                    idx = index_ref[8 * i : 8 * i + 8, :]
                    here = jnp.take_along_axis(row, idx % TILE, axis=1)
                    got[i] = jnp.where(idx // TILE == origin[r] * 8 + q, here, got[i])
        for c in range(PICKS // TILE):
            if c % 8 == 0:
                column = got[c // 8].T
            out_ref[c * TILE : (c + 1) * TILE, :] = column[:, c % 8 : c % 8 + 1]

    vm = pl.BlockSpec(memory_space=pltpu.VMEM)
    specs = [pl.BlockSpec((EXT, 1024), functools.partial(lambda b, i: (b, 0), b)) for _, b in gains]
    return pl.pallas_call(
        body,
        grid=(1,),
        out_shape=jax.ShapeDtypeStruct((PICKS, 1), F32),
        in_specs=[pl.BlockSpec(memory_space=pltpu.SMEM), vm] + specs,
        out_specs=vm,
        compiler_params=params(),
        cost_estimate=pl.CostEstimate(flops=2_000_000_000, bytes_accessed=1 * MIB, transcendentals=0),
        name="pick_gains",
    )(origins, index_rows, *[g for g, _ in gains])


def pick(shards, origins, index, carry=None, gain=None, kept=None):
    arrays, meta = flatten(shards)
    n = len(shards)
    final = gain is not None

    def body(*refs):
        origin, index_ref, *rest = refs
        pieces, rest = rest[: len(arrays)], rest[len(arrays) :]
        if carry is not None:
            (acc_ref, sq_ref), rest = rest[:2], rest[2:]
        if final:
            (gain_ref, kept_ref), rest = rest[:2], rest[2:]
        outs, table = rest[:-1], rest[-1]
        step = 128
        total = sq_ref[...] if carry is not None else jnp.zeros((8, TOK), F32)
        for r in range(n):
            for j, off, size in meta[r]:

                def add(c, total, j=j, at=r * 1024 + off):
                    from_rows = pl.ds(pl.multiple_of(c * step, step), step)
                    v = pieces[j][from_rows, :]
                    table[pl.ds(pl.multiple_of(at + c * step, step), step), :] = v
                    v = v.astype(F32)
                    return total + jnp.sum((v * v).reshape(step // 8, 8, TOK), axis=0)

                total = lax.fori_loop(0, size // step, add, total)
        if final:
            scale = lax.rsqrt(jnp.sum(total, axis=0, keepdims=True) / WIDTH + epsilon) * kept_ref[...]
        else:
            outs[1][...] = total

        def value(start, size):
            got = jnp.zeros((size, TOK), F32)
            if carry is not None:
                got = acc_ref[pl.ds(start, size), :].astype(F32)
            for r in range(n):
                got += nn(hot_rows(index_ref, start, size, origin[r] * 1024), table[r * 1024 : (r + 1) * 1024, :])
            if final:
                got = got * scale * gain_ref[pl.ds(start, size), :]
            return got.astype(BF16)

        def fill(ref, base, to, rows, block):
            def one(c, _):
                at = pl.multiple_of(c * block, block)
                ref[pl.ds(to + at, block), :] = value(pl.multiple_of(base + at, TILE), block)
                return 0

            lax.fori_loop(0, rows // block, one, 0)

        places = ((0, 0), (0, TILE + EXT), (1, 0), (2, 0)) if final else tuple((0, base) for base, _ in SPLITS)
        for (base, rows), (o, to) in zip(SPLITS, places):
            fill(outs[o], base, to, rows, min(rows, 512))
        if final:
            row0 = lax.broadcasted_iota(jnp.int32, (EXT, TOK), 0) == 0
            outs[0][TILE : TILE + EXT, :] = jnp.where(row0, kept_ref[...], 0.0).astype(BF16)

    vm = pl.BlockSpec(memory_space=pltpu.VMEM)
    operands = [origins, index, *arrays]
    if carry is not None:
        operands += list(carry)
    if final:
        operands += [gain, kept]
        outs = [jax.ShapeDtypeStruct(s, BF16) for s in ((TILE + EXT + 512, TOK), (512, TOK), (1024, TOK))]
    else:
        outs = [jax.ShapeDtypeStruct((PICKS, TOK), BF16), jax.ShapeDtypeStruct((8, TOK), F32)]
    return pl.pallas_call(
        body,
        out_shape=outs,
        in_specs=[pl.BlockSpec(memory_space=pltpu.SMEM)] + [vm] * (len(operands) - 1),
        out_specs=[vm] * len(outs),
        scratch_shapes=[pltpu.VMEM((1024 * n, TOK), BF16)],
        compiler_params=params(),
        cost_estimate=pl.CostEstimate(flops=2 * PICKS * 1024 * n * TOK, bytes_accessed=4 * MIB, transcendentals=0),
        name="pick",
    )(*operands)


def place(pieces, meta, slot, scratch):
    for r in range(8):
        row = pl.multiple_of(slot[r] * TILE, TILE)
        for j, off, size in meta[r]:
            for c in range(size):
                scratch[pl.ds(row, TILE), (off + c) * TOK : (off + c + 1) * TOK] = pieces[j][c]


def panel_gram(shards, slots):
    arrays, meta = flatten(shards)

    def body(slot, *refs):
        pieces, (pan_ref, gram_ref) = refs[: len(arrays)], refs[len(arrays) :]
        place(pieces, meta, slot, pan_ref)

        def one(c, _):
            rows = pl.ds(pl.multiple_of(c * 256, 256), 256)
            gram_ref[rows, :] = nt(pan_ref[rows, :], pan_ref[...])
            return 0

        lax.fori_loop(0, 4, one, 0)

    vm = pl.BlockSpec(memory_space=pltpu.VMEM)
    return pl.pallas_call(
        body,
        out_shape=[jax.ShapeDtypeStruct((PANEL, 2048), BF16), jax.ShapeDtypeStruct((PANEL, PANEL), F32)],
        in_specs=[pl.BlockSpec(memory_space=pltpu.SMEM)] + [vm] * len(arrays),
        out_specs=[vm] * 2,
        compiler_params=params(),
        cost_estimate=pl.CostEstimate(flops=1_000_000, bytes_accessed=1024, transcendentals=0),
        name="panel_gram",
    )(slots, *arrays)


def block_gram(row_shards, cols_all, pan, slots, chunks):
    row_arrays, row_meta = flatten(row_shards)
    steps = 4

    def body(slot, chunk, pan_ref, col_ref, *refs):
        rp, refs = refs[: len(row_arrays)], refs[len(row_arrays) :]
        hk_ref, hs_ref, pk_ref, ps_ref, pc_ref, rows, cols = refs
        i = pl.program_id(0)

        @pl.when(i == 0)
        def _():
            place(rp, row_meta, slot, rows)
            for c in range(8):
                cols[:, c * TOK : (c + 1) * TOK] = col_ref[chunk[c]]

        at = pl.ds(pl.multiple_of(i * TILE, TILE), TILE)
        to = pl.ds(pl.multiple_of(512 + i * TILE, TILE), TILE)
        both = jnp.concatenate([rows[at, :], rows[to, :]], axis=0)
        p = nt(both, pan_ref[...])
        pk_ref[...], ps_ref[...] = p[:TILE], p[TILE:]
        h = nt(both, cols[...])
        hk_ref[...], hs_ref[...] = h[:TILE], h[TILE:]
        pc_ref[...] = nt(cols[pl.ds(pl.multiple_of(i * 256, 256), 256), :], pan_ref[...])

    vm = pl.BlockSpec(memory_space=pltpu.VMEM)
    outs = [(512, 1024)] * 4 + [(1024, PANEL)]
    return pl.pallas_call(
        body,
        grid=(steps,),
        out_shape=[jax.ShapeDtypeStruct(s, F32) for s in outs],
        in_specs=[pl.BlockSpec(memory_space=pltpu.SMEM)] * 2 + [vm, vm] + [vm] * len(row_arrays),
        out_specs=[pl.BlockSpec((n // steps, 1024), lambda i: (i, 0)) for n, _ in outs],
        scratch_shapes=[pltpu.VMEM((1024, 2048), BF16)] * 2,
        compiler_params=params(62),
        cost_estimate=pl.CostEstimate(flops=6 * 1024 * 1024 * 2048, bytes_accessed=24 * MIB, transcendentals=0),
        name="block_gram",
    )(slots, chunks, pan, cols_all, *row_arrays)


def factor_tile(a):
    groups, m = TILE // 8, 8
    lane = lax.broadcasted_iota(jnp.int32, (8, TILE), 1)
    sub = lax.broadcasted_iota(jnp.int32, (8, TILE), 0)
    A = [a[8 * g : 8 * g + 8, :] for g in range(groups)]
    E = [jnp.where(lane == sub + 8 * g, 1.0, 0.0).astype(F32) for g in range(groups)]

    def wide(v):
        return jnp.broadcast_to(v, (8, TILE))

    for g0 in range(groups):
        j = 8 * g0
        piv = {(i, l): wide(A[g0][i : i + 1, j + l : j + l + 1]) for i in range(m) for l in range(i, m)}
        R = [wide(A[g0][i : i + 1, :]) for i in range(m)]
        RE = [wide(E[g0][i : i + 1, :]) for i in range(m)]
        f, inv = {}, []
        for i in range(m):
            inv.append(1.0 / piv[i, i])
            for l in range(i + 1, m):
                f[i, l] = piv[i, l] * inv[i]
            for l in range(i + 1, m):
                for q in range(l, m):
                    piv[l, q] = piv[l, q] - (piv[i, l] * piv[i, q]) * inv[i]
                R[l] = R[l] - f[i, l] * R[i]
                RE[l] = RE[l] - f[i, l] * RE[i]
        W, WE = [None] * m, [None] * m
        for i in reversed(range(m)):
            W[i], WE[i] = R[i] * inv[i], RE[i] * inv[i]
            for l in range(i + 1, m):
                W[i] = W[i] - f[i, l] * W[l]
                WE[i] = WE[i] - f[i, l] * WE[l]
        for g in range(g0 + 1, groups):
            ag, eg = A[g], E[g]
            for l in reversed(range(m)):
                col = A[g][:, j + l : j + l + 1]
                ag = ag - col * W[l]
                eg = eg - col * WE[l]
            A[g], E[g] = ag, eg
        ag, eg = R[0], RE[0]
        for i in range(1, m):
            ag = jnp.where(sub == i, R[i], ag)
            eg = jnp.where(sub == i, RE[i], eg)
        A[g0], E[g0] = ag, eg
    U, V = [], []
    for g in range(groups):
        diag = jnp.sum(jnp.where(lane == sub + 8 * g, A[g], 0.0), axis=1, keepdims=True)
        rs = lax.rsqrt(diag)
        U.append(jnp.where(lane >= sub + 8 * g, A[g] * rs, 0.0))
        V.append(E[g] * rs)
    return jnp.concatenate(U, axis=0), jnp.concatenate(V, axis=0)


def cholesky(a, other=None, count=None):
    n = a.shape[0]
    tiles = n // TILE
    start = other is not None
    band = 2 * TILE
    more = n > band

    def body(*refs):
        if start:
            count_ref, g_ref, o_ref, *refs = refs
            inv = 1.0 / count_ref[0]
        else:
            g_ref, *refs = refs
        band_ref, v_ref, *refs = refs
        if more:
            rest_ref, *refs = refs
        w, ph, plo, lh, ll = refs

        def load(c, _):
            rows = pl.ds(pl.multiple_of(c * TILE, TILE), TILE)
            w[rows, :] = (g_ref[rows, :] + o_ref[rows, :]) * inv if start else g_ref[rows, :]
            return 0

        lax.fori_loop(0, tiles, load, 0)

        def step(k, _):
            at = pl.ds(pl.multiple_of(k * TILE, TILE), TILE)
            U, V = factor_tile(w[at, at])
            v_ref[at, :] = V
            vs = split(V)
            panel = dot3(nn, vs, split(w[at, :]))
            ph[...], plo[...] = split(panel)
            left = dot3(nt, split(w[:, at]), vs)
            lh[...], ll[...] = split(left)
            band_ref[at, :] = panel
            band_ref[at, at] = U

            def update(j, _):
                rows = pl.ds(pl.multiple_of(j * TILE, TILE), TILE)
                w[rows, :] -= dot3(nn, (lh[rows, :], ll[rows, :]), (ph[...], plo[...]))
                return 0

            lax.fori_loop(k + 1, tiles, update, 0)
            return 0

        lax.fori_loop(0, 2, step, 0)
        if more:

            def keep(c, _):
                rows = pl.ds(pl.multiple_of(c * TILE, TILE), TILE)
                rest_ref[rows, :] = w[pl.ds(pl.multiple_of(band + c * TILE, TILE), TILE), band:]
                return 0

            lax.fori_loop(0, tiles - 2, keep, 0)

    vm = pl.BlockSpec(memory_space=pltpu.VMEM)
    sm = pl.BlockSpec(memory_space=pltpu.SMEM)
    outs = [(band, n), (band, TILE)] + ([(n - band, n - band)] if more else [])
    return pl.pallas_call(
        body,
        out_shape=[jax.ShapeDtypeStruct(o, F32) for o in outs],
        in_specs=[sm, vm, vm] if start else [vm],
        out_specs=[vm] * len(outs),
        scratch_shapes=[pltpu.VMEM((n, n), F32)] + [pltpu.VMEM((TILE, n), BF16)] * 2 + [pltpu.VMEM((n, TILE), BF16)] * 2,
        compiler_params=params(24),
        cost_estimate=pl.CostEstimate(flops=1_000_000, bytes_accessed=1024, transcendentals=0),
        name="cholesky",
    )(*((count, a, other) if start else (a,)))


def finish(scalars, count, hk, hr, pk, pr, pc, pcr, bands, inverses):
    two, half = 2 * TILE, 512
    pairs = PANEL // two

    def body(sc, count_ref, hk_ref, hr_ref, pk_ref, pr_ref, pc_ref, pcr_ref, *refs):
        u_refs, v_refs, refs = refs[:pairs], refs[pairs : 2 * pairs], refs[2 * pairs :]
        out_ref, uh, ul, vh, vl, xh, xl, b = refs
        i = pl.program_id(0)
        inv = 1.0 / count_ref[0]

        @pl.when(i == 0)
        def _():
            for k in range(pairs):
                for c in (0, TILE):
                    rows, cols = slice(k * two + c, k * two + c + TILE), slice(k * two, PANEL)
                    uh[rows, cols], ul[rows, cols] = split(u_refs[k][c : c + TILE, :])

            for k in range(pairs):
                top, low = slice(k * two, k * two + TILE), slice(k * two + TILE, (k + 1) * two)
                v1, v2 = split(v_refs[k][:TILE, :]), split(v_refs[k][TILE:, :])
                cross = dot3(nn, split(u_refs[k][:TILE, TILE:two].T), v1)
                cross = -dot3(nn, v2, split(cross))
                vh[top, :TILE], vl[top, :TILE] = v1
                vh[low, TILE:], vl[low, TILE:] = v2
                vh[top, TILE:] = jnp.zeros((TILE, TILE), BF16)
                vl[top, TILE:] = jnp.zeros((TILE, TILE), BF16)
                vh[low, :TILE], vl[low, :TILE] = split(cross)

            def load(c, _):
                rows = pl.ds(pl.multiple_of(c * TILE, TILE), TILE)
                b[rows, :] = (pk_ref[rows, :] + pr_ref[rows, :]) * inv
                return 0

            lax.fori_loop(0, half // TILE, load, 0)

        @pl.when(i > 0)
        def _():
            def load(c, _):
                rows = pl.ds(pl.multiple_of(c * TILE, TILE), TILE)
                b[rows, :] = (pc_ref[rows, :] + pcr_ref[rows, :]) * inv
                return 0

            lax.fori_loop(0, half // TILE, load, 0)

        to = pl.ds(pl.multiple_of(jnp.minimum(i, 1) * half, half), half)
        for k in range(pairs):
            here, after = slice(k * two, (k + 1) * two), slice((k + 1) * two, PANEL)
            x = dot3(nt, split(b[:, here]), (vh[here, :], vl[here, :]))
            xs = split(x)
            b[:, here] = x
            xh[to, here], xl[to, here] = xs
            if k + 1 < pairs:
                b[:, after] -= dot3(nn, xs, (uh[here, after], ul[here, after]))

        @pl.when(i == 0)
        def _():
            def left(c, _):
                rows = pl.ds(pl.multiple_of(c * TILE, TILE), TILE)
                own = b[rows, pl.ds(pl.multiple_of(sc[1] * TILE, TILE), TILE)]
                row = (c * 16 + sc[0]) * TILE + lax.broadcasted_iota(jnp.int32, (TILE, TILE), 0)
                col = sc[1] * TILE + lax.broadcasted_iota(jnp.int32, (TILE, TILE), 1)
                out_ref[rows, :TILE] = jnp.where(row >= col, own, 0.0)
                return 0

            lax.fori_loop(0, half // TILE, left, 0)

        def trail(c, first):
            rows = pl.ds(pl.multiple_of(c * two, two), two)
            cols = slice(half + first, 2 * half)
            up = dot3(nt, (xh[rows, :], xl[rows, :]), (xh[cols, :], xl[cols, :]))
            out_ref[rows, first:] = (hk_ref[rows, first:] + hr_ref[rows, first:]) * inv - up

        @pl.when(i == 1)
        def _():
            lax.fori_loop(0, half // two, lambda c, _: (trail(c, TILE), 0)[1], 0)

        @pl.when(i == 2)
        def _():
            lax.fori_loop(0, half // two, lambda c, _: (trail(c, 0), 0)[1], 0)

    sm = pl.BlockSpec(memory_space=pltpu.SMEM)
    later = lambda i: jnp.maximum(i - 1, 0)
    wide = pl.BlockSpec((half, half), lambda i: (0, later(i)))
    tall = pl.BlockSpec((half, PANEL), lambda i: (later(i), 0))
    whole = lambda n, m: pl.BlockSpec((n, m), lambda i: (0, 0))
    return pl.pallas_call(
        body,
        grid=(3,),
        out_shape=jax.ShapeDtypeStruct((half, 1024), F32),
        in_specs=[sm, sm, wide, wide, whole(half, PANEL), whole(half, PANEL), tall, tall]
        + [whole(two, PANEL - k * two) for k in range(pairs)]
        + [whole(two, TILE)] * pairs,
        out_specs=wide,
        scratch_shapes=[pltpu.VMEM((PANEL, PANEL), BF16)] * 2
        + [pltpu.VMEM((PANEL, two), BF16)] * 2
        + [pltpu.VMEM((2 * half, PANEL), BF16)] * 2
        + [pltpu.VMEM((half, PANEL), F32)],
        compiler_params=params(62),
        cost_estimate=pl.CostEstimate(flops=16_000_000_000, bytes_accessed=28 * MIB, transcendentals=0),
        name="finish",
    )(scalars, count, hk, hr, pk, pr, pc, pcr, *bands, *inverses)


def shards_of(token_ids, column_order, residual, attn_out, out_proj, norm_gain):
    s = lax.axis_index("section").astype(jnp.int32)
    t = lax.axis_index("tensor").astype(jnp.int32)
    y, x = t // 4, t % 4
    z, yl, core = s // 4, (s // 2) % 2, s % 2

    def origin(dx, dy):
        return (y ^ dy) * 4 + (x - dx) % 4

    origins = jnp.stack([origin(*k) for k in KEYS])
    early = jnp.stack([origin(*KEYS[i]) for i in (0, 1, 2, 4)])
    middle = jnp.stack([origin(*KEYS[i]) for i in (3, 5)])
    late = jnp.stack([origin(*KEYS[i]) for i in (6, 7)])

    g_hi = lax.reduce_precision(norm_gain, 8, 7)
    g_mid = lax.reduce_precision(norm_gain - g_hi, 8, 7)
    g_lo = norm_gain - g_hi - g_mid
    parts = jnp.stack([g_hi, g_mid, g_lo]).astype(BF16)
    ext = jnp.concatenate([parts, jnp.zeros((EXT - 3, 1024), BF16)], axis=0)
    own = jnp.concatenate([attn_out, ext], axis=0)

    one = first(own, shift_t)
    two = second(*one, shift_t, 144)
    acc = project([[own], [one[0]], [one[1]], [one[2]]], out_proj, early)
    *two, acc = tie(*two, acc)
    three = third(two[0], two[1], shift_t, 144)
    acc = project([[two[0]], [two[1]]], out_proj, middle, acc)
    *three, acc = tie(*three, acc)
    a = listed(own, one, two, three)
    hidden = project(a[6:], out_proj, late, acc, residual)
    gains = [(pieces[-1], pieces[-1].shape[0] // EXT - 1) for pieces in a]

    tiles = [t]
    for dy in (1, 0):
        for dz in range(4):
            group = ((z + dz) % 4) * 2 + (yl ^ dy)
            tiles.append(16 * x + 2 * group + y)
    tiles += [j * 8 + t for j in range(8)]
    index = jnp.take(column_order.reshape(64, TILE), jnp.stack(tiles), axis=0).reshape(-1, 1)
    kept = (token_ids != 0).astype(F32).reshape(1, TOK)

    one = first(hidden, shift_t)
    rows_of = jnp.concatenate([index.reshape(-1, TILE), jnp.zeros((7, TILE), jnp.int32)], axis=0)
    gain = pick_gains(gains, origins, rows_of)
    *one, gain = tie(*one, gain)
    two = second(*one, shift_t, 512)
    carry = pick([[hidden], [one[0]], [one[1]], [one[2]]], early, index)
    *two, c0, c1 = tie(*two, *carry)
    three = third(two[0], two[1], shift_t, 512)
    carry = pick([[two[0]], [two[1]]], middle, index, (c0, c1))
    *three, c0, c1 = tie(*three, *carry)
    h = listed(hidden, one, two, three)
    message, rows0, cols = pick(h[6:], late, index, (c0, c1), gain, kept)

    same_core = [[c + 2 * g for g in range(8)] for c in range(2)]
    theirs = shift_s(message, 0, 1)
    head = TILE + EXT

    def part(msg, rows, dz):
        return jnp.concatenate([msg[:head], rows[dz * TILE : (dz + 1) * TILE]], axis=0)

    sent = [jnp.stack([part(message, rows0, dz), part(theirs, theirs[head:], dz)]) for dz in range(4)]
    got = [sent[0]] + [shift_s(sent[dz], dz, 0) for dz in (1, 2, 3)]
    pan8 = jnp.concatenate([g[:, :TILE] for g in got], axis=0)
    rows8 = jnp.concatenate([g[:, head:] for g in got], axis=0)
    kept_here = sum(jnp.sum(g[:, TILE : TILE + 1].astype(F32)) for g in got)
    count = (kept_here + shift_s(kept_here.reshape(1, 1), 0, 0, 1)[0, 0]).reshape(1)

    p1 = first(pan8, shift_t)
    p2 = second(*p1, shift_t, 4)
    p2, rows8, cols, count = tie(p2, rows8, cols, count)
    cols_all = lax.all_gather(cols, "section", axis=0, axis_index_groups=same_core)
    p3 = third(p2[0], p2[1], shift_t, 4)
    p3, rows8 = tie(p3, rows8)
    r1 = first(rows8, shift_t)
    pan_all, gram = panel_gram(listed(pan8, p1, p2, p3), origins)

    gram_other = shift_s(gram, 0, 0, 1)
    u0, v0, u = cholesky(gram, gram_other, count)
    u, r1 = tie(u, r1)
    r2 = second(*r1, shift_t, 4)
    u1, v1, u = cholesky(u)
    u, r2 = tie(u, r2)
    r3 = third(r2[0], r2[1], shift_t, 4)
    u2, v2, u = cholesky(u)
    u, r3, cols_all = tie(u, r3, cols_all)
    slots = jnp.stack([((o // 4) ^ core) * 4 + o % 4 for o in [origin(*k) for k in KEYS]])
    chunks = jnp.stack([((z - dz) % 4) * 2 + (yl ^ dy) for dz in range(4) for dy in range(2)])
    hk, hs, pk, ps, pc = block_gram(listed(rows8, r1, r2, r3), cols_all, pan_all, slots, chunks)
    u, hs, ps, pc = tie(u, hs, ps, pc)
    hr, pr, pcr = [shift_s(w, 0, 0, 1) for w in (hs, ps, pc)]
    u3, v3 = cholesky(u)
    scalars = jnp.stack([s, t])
    return finish(scalars, count, hk, hr, pk, pr, pc, pcr, (u0, u1, u2, u3), (v0, v1, v2, v3))


def solution(mesh):
    placed = (
        P("section"),
        P(),
        P("section", "tensor"),
        P("section", "tensor"),
        P(None, "tensor"),
        P("tensor"),
    )
    return jax.shard_map(
        shards_of, mesh=mesh, in_specs=placed, out_specs=P("section", "tensor"), check_vma=False
    )
```
